32 devices in a mesh: dp: 4 (over y, x), fsdp: 8 (over z, core).
Axes of the slice: x: 2, y: 2, z: 4, core: 2. Of those that a mesh axis runs over, the one named last changes fastest.
Arguments:
- tokens: bfloat16 [64, 197, 768], P(('dp', 'fsdp')), may hold values from -6 to 6
- counts: int32 [64], P(('dp', 'fsdp')), may hold values from 65 to 197, as said below
- params_first: bfloat16 [7098368], P(('dp', 'fsdp')), may hold values from -3 to 3
- params_second: bfloat16 [7098368], P(('dp', 'fsdp')), may hold values from -3 to 3
- cotangent: bfloat16 [64, 197, 768], P(('dp', 'fsdp')), may hold values from -6 to 6
Outputs:
- output: bfloat16 [64, 197, 768], P(('dp', 'fsdp'))
- grad_tokens: bfloat16 [64, 197, 768], P(('dp', 'fsdp'))
- grad_first: float32 [7098368], P(('dp', 'fsdp'))
- grad_second: float32 [7098368], P(('dp', 'fsdp'))
The draws below stay inside these ranges and needn't reach their ends.
Inputs may be any that keep to these rules, and one draw needn't show every extreme that they name: Keys 0 to counts - 1 of an image are valid; some image has all 197.
All inputs are finite; a program needn't handle non-finite values.
Results may differ from the reference program's by a relative error of at most 0.015.
Values may be sent and summed in bfloat16 or wider, within the bound.
No kernel may reach another device: no remote copies, remote signals or barrier semaphores. Data moves between devices by JAX's collectives and lax.ppermute only.
A program may use at most 256 MiB of HBM per device.

```python
import math
import jax
import jax.numpy as jnp
from jax import lax

D = 768
HEADS = 12
FF = 3072
GRID = 14
SEQ = 197
RELS = 732
IMAGES = 64
PLEN = 7098368


def flat_scales():
    pieces = [(D, 0.2, 1.0), (D, 0.3, 0.0), (3 * D * D, D ** (-0.5), 0.0), (D, 0.3, 0.0), (D, 0.3, 0.0), (RELS * HEADS, 1.0, 0.0), (D * D, 4.0 * D ** (-0.5), 0.0), (D, 0.3, 0.0), (D, 0.2, 1.0), (D, 0.2, 1.0), (D, 0.3, 0.0), (D * FF, D ** (-0.5), 0.0), (FF, 0.3, 0.0), (FF * D, 1.5 * FF ** (-0.5), 0.0), (D, 0.3, 0.0), (D, 0.2, 1.0)]
    used = sum((entry[0] for entry in pieces))
    pieces.append((PLEN - used, 0.0, 0.0))
    scales = jnp.concatenate([jnp.full((entry[0],), entry[1], jnp.float32) for entry in pieces])
    offsets = jnp.concatenate([jnp.full((entry[0],), entry[2], jnp.float32) for entry in pieces])
    return (scales, offsets)


def draw_params_first(key, part):
    key = jax.random.fold_in(key, 21)
    base = jax.random.truncated_normal(key, -3.0, 3.0, (PLEN,), jnp.float32)
    scales, offsets = flat_scales()
    return (offsets + scales * base).astype(jnp.bfloat16)


def draw_params_second(key, part):
    key = jax.random.fold_in(key, 22)
    base = jax.random.truncated_normal(key, -3.0, 3.0, (PLEN,), jnp.float32)
    scales, offsets = flat_scales()
    return (offsets + scales * base).astype(jnp.bfloat16)


def draw_counts(key, part):
    key = jax.random.fold_in(key, 11)
    values = jax.random.randint(key, (IMAGES,), SEQ // 3, SEQ + 1, dtype=jnp.int32)
    return values.at[0].set(SEQ)


def level_of(own_key, dims, cuts, smallest, largest):
    def one(axis_at, parts):
        steps = jax.random.uniform(jax.random.fold_in(jax.random.fold_in(own_key, 6), axis_at), (parts,), jnp.float32, smallest / len(cuts), largest / len(cuts))
        return jnp.repeat(jnp.exp(steps), dims[axis_at] // parts).reshape((-1,) + (1,) * (len(dims) - axis_at - 1))

    loudness = one(*cuts[0])
    for cut in cuts[1:]:
        loudness = loudness * one(*cut)
    return loudness


def centred(own_key, extent, scale, limit, shards=(), held_as=jnp.bfloat16):
    array = scale * jax.random.normal(own_key, extent, jnp.float32)
    if shards:
        array = array * level_of(own_key, extent, shards, -0.22, 0.18)
    return jnp.clip(array, -limit, limit).astype(held_as)


def setup_inputs(seed: int = 0) -> dict:
    splits = jax.random.split(jax.random.key(seed), 6)
    tokens = centred(splits[0], (IMAGES, SEQ, D), 1.0, 6.0, ((0, 32),))
    counts = draw_counts(jax.random.fold_in(splits[5], 71), 0)
    params_first = draw_params_first(jax.random.fold_in(splits[5], 71), 0)
    params_second = draw_params_second(jax.random.fold_in(splits[5], 71), 0)
    cotangent = centred(splits[4], (IMAGES, SEQ, D), 1.0, 6.0, ((0, 32),))
    return dict(tokens=tokens, counts=counts, params_first=params_first, params_second=params_second, cotangent=cotangent)


EPSILON = 1e-06
NEGATIVE = -1000000000.0

@jax.custom_vjp
def low(v):
    return lax.optimization_barrier(v.astype(jnp.bfloat16)).astype(jnp.float32)

@jax.custom_vjp
def low_back(v):
    return v

def low_keep(v):
    return (low(v), None)

def low_pass(kept, grad):
    return (grad,)

def back_keep(v):
    return (v, None)

def back_low(kept, grad):
    return (low(grad),)
low.defvjp(low_keep, low_pass)
low_back.defvjp(back_keep, back_low)

def param_layout():
    return [('norm1_gain', (D,)), ('norm1_bias', (D,)), ('qkv_weight', (D, 3 * D)), ('query_bias', (D,)), ('value_bias', (D,)), ('relative_table', (RELS, HEADS)), ('proj_weight', (D, D)), ('proj_bias', (D,)), ('gamma_attn', (D,)), ('norm2_gain', (D,)), ('norm2_bias', (D,)), ('fc1_weight', (D, FF)), ('fc1_bias', (FF,)), ('fc2_weight', (FF, D)), ('fc2_bias', (D,)), ('gamma_mlp', (D,))]

def unpack_layer(flat):
    pieces = {}
    offset = 0
    for entry_name, dims_shape in param_layout():
        length = math.prod(dims_shape)
        pieces[entry_name] = flat[offset:offset + length].reshape(dims_shape)
        offset += length
    return pieces

def relative_index():
    patches = GRID * GRID
    position = jnp.arange(patches, dtype=jnp.int32)
    row_pos = position // GRID
    col_pos = position % GRID
    delta_row = row_pos[:, None] - row_pos[None, :] + (GRID - 1)
    delta_col = col_pos[:, None] - col_pos[None, :] + (GRID - 1)
    inner_index = (delta_row * (2 * GRID - 1) + delta_col).astype(jnp.int32)
    top_row = jnp.full((1, patches), RELS - 3, jnp.int32)
    left_col = jnp.full((patches, 1), RELS - 2, jnp.int32)
    corner = jnp.full((1, 1), RELS - 1, jnp.int32)
    upper = jnp.concatenate([corner, top_row], axis=1)
    lower = jnp.concatenate([left_col, inner_index], axis=1)
    return jnp.concatenate([upper, lower], axis=0)

def norm_apply(values, gain, shift):
    centre = values - lax.optimization_barrier(jnp.mean(values, axis=-1, keepdims=True))
    spread = lax.optimization_barrier(jnp.mean(centre * centre, axis=-1, keepdims=True))
    return centre * lax.rsqrt(spread + EPSILON) * gain + shift

def softmax_rows(scores):
    shifted = jnp.exp(scores - lax.optimization_barrier(jnp.max(scores, axis=-1, keepdims=True)))
    return shifted / lax.optimization_barrier(jnp.sum(shifted, axis=-1, keepdims=True))

def layer_forward(hidden, valid, params):
    highest = lax.Precision.HIGHEST
    images = hidden.shape[0]
    head_dim = D // HEADS
    factor = head_dim ** (-0.5)
    token_rows = hidden.reshape(-1, D)
    normed = low(norm_apply(token_rows, params['norm1_gain'], params['norm1_bias']))
    project = low_back(jnp.dot(normed, params['qkv_weight'], precision=highest))
    query = low((project[:, :D] + params['query_bias']) * factor).reshape(images, SEQ, HEADS, head_dim)
    key_rows = low(project[:, D:2 * D]).reshape(images, SEQ, HEADS, head_dim)
    value_rows = low(project[:, 2 * D:] + params['value_bias']).reshape(images, SEQ, HEADS, head_dim)
    table = jnp.take(params['relative_table'], relative_index().reshape(-1), axis=0)
    table = table.reshape(SEQ, SEQ, HEADS).transpose(2, 0, 1)
    visible = jnp.arange(SEQ)[None, :] < valid[:, None]
    scores = low_back(jnp.einsum('bqhd,bkhd->bhqk', query, key_rows, precision=highest)) + table[None]
    scores = jnp.where(visible[:, None, None, :], scores, NEGATIVE)
    weights = softmax_rows(scores)
    attended = jnp.einsum('bhqk,bkhd->bqhd', low(weights), value_rows, precision=highest).reshape(-1, D)
    attended = low(low_back(attended))
    branch = low_back(jnp.dot(attended, params['proj_weight'], precision=highest)) + params['proj_bias']
    middle = token_rows + params['gamma_attn'] * branch
    second_normed = low(norm_apply(middle, params['norm2_gain'], params['norm2_bias']))
    pre_act = low_back(jnp.dot(second_normed, params['fc1_weight'], precision=highest)) + params['fc1_bias']
    activ = low(jax.nn.gelu(pre_act, approximate=False))
    mlp_out = low_back(jnp.dot(activ, params['fc2_weight'], precision=highest)) + params['fc2_bias']
    return (middle + params['gamma_mlp'] * mlp_out).reshape(images, SEQ, D)

def reference(tokens, counts, params_first, params_second, cotangent):
    block_images = math.gcd(IMAGES, 16)
    groups = IMAGES // block_images

    def two_layers(hidden, valid, first_flat, second_flat):
        hidden = layer_forward(hidden, valid, unpack_layer(first_flat))
        return layer_forward(hidden, valid, unpack_layer(second_flat))
    checked = jax.checkpoint(two_layers)

    def forward_all(hidden, first_flat, second_flat):
        blocks = hidden.reshape(groups, block_images, SEQ, D)
        valid_blocks = counts.reshape(groups, block_images)
        result = lax.map(lambda packed: checked(packed[0], packed[1], first_flat, second_flat), (blocks, valid_blocks))
        return result.reshape(IMAGES, SEQ, D)
    output, pullback = jax.vjp(forward_all, tokens.astype(jnp.float32), params_first.astype(jnp.float32), params_second.astype(jnp.float32))
    grad_tokens, grad_first, grad_second = pullback(cotangent.astype(jnp.float32))
    return (output.astype(jnp.bfloat16), grad_tokens.astype(jnp.bfloat16), grad_first, grad_second)
```

```python
import functools
import math

import jax
import jax.numpy as jnp
import numpy as np
from jax import lax
from jax.experimental import pallas as pl
from jax.experimental.pallas import tpu as pltpu
from jax.sharding import PartitionSpec as P

D = 768
HEADS = 12
HEAD = D // HEADS
FF = 3072
GRID = 14
SEQ = 197
RELS = 732
ROWS = 208
LANES = 128
TILE = 16
AXES = ("dp", "fsdp")
VMEM_LIMIT = 56 * 2**20

EPSILON = 1e-06
NEGATIVE = -1000000000.0

ENTRIES = [
    ("norm1_gain", (D,)),
    ("norm1_bias", (D,)),
    ("qkv_weight", (D, 3 * D)),
    ("query_bias", (D,)),
    ("value_bias", (D,)),
    ("relative_table", (RELS, HEADS)),
    ("proj_weight", (D, D)),
    ("proj_bias", (D,)),
    ("gamma_attn", (D,)),
    ("norm2_gain", (D,)),
    ("norm2_bias", (D,)),
    ("fc1_weight", (D, FF)),
    ("fc1_bias", (FF,)),
    ("fc2_weight", (FF, D)),
    ("fc2_bias", (D,)),
    ("gamma_mlp", (D,)),
]
WEIGHTS = {name: dims for name, dims in ENTRIES if name.endswith("weight")}
SIZES = dict(ENTRIES)
VECTORS = [
    "norm1_gain",
    "norm1_bias",
    "query_bias",
    "value_bias",
    "proj_bias",
    "gamma_attn",
    "norm2_gain",
    "norm2_bias",
    "fc2_bias",
    "gamma_mlp",
]
ROW = {name: i for i, name in enumerate(VECTORS)}


def count_rows(dims):
    return -(-math.prod(dims) // LANES)


def virtual_starts():
    starts, at = {}, 0
    for name, dims in ENTRIES:
        starts[name] = at
        at += count_rows(dims)
    return starts, at


STARTS, VIRTUAL = virtual_starts()
SHIFT = RELS * HEADS % LANES
TABLE_END = STARTS["proj_weight"]


def tile_order():
    parts = []
    for name, (depth, width) in WEIGHTS.items():
        across = width // LANES
        rows = STARTS[name] + np.arange(depth * across).reshape(depth // TILE, TILE, across)
        parts.append(rows.transpose(0, 2, 1).reshape(-1))
    return np.concatenate(parts)


def small_order():
    groups = [VECTORS, ["fc1_bias"], ["relative_table"]]
    rows = []
    for group in groups:
        for name in group:
            rows += [STARTS[name] + i for i in range(count_rows(SIZES[name]))]
        rows += [-1] * (-len(rows) % 8)
    return np.array(rows)


TILE_ROWS = tile_order()
SMALL_ROWS = small_order()
TILES = len(TILE_ROWS) // TILE


def halo(block, before, after, devices):
    rows = block.shape[0]
    pieces = [block]
    for hop in range(1, -(-before // rows) + 1):
        take = min(rows, before - (hop - 1) * rows)
        perm = [(i, i + hop) for i in range(devices - hop)]
        pieces.insert(0, lax.ppermute(block[rows - take :], AXES, perm))
    for hop in range(1, -(-after // rows) + 1):
        take = min(rows, after - (hop - 1) * rows)
        perm = [(i + hop, i) for i in range(devices - hop)]
        pieces.append(lax.ppermute(block[:take], AXES, perm))
    return jnp.concatenate(pieces, axis=0)


def pick_rows(index, source):
    chosen = index[:, None] == lax.broadcasted_iota(jnp.int32, (1, source.shape[0]), 1)
    chosen = chosen.astype(jnp.bfloat16)
    if source.dtype == jnp.bfloat16:
        return jnp.dot(chosen, source, preferred_element_type=jnp.float32).astype(jnp.bfloat16)
    high = source.astype(jnp.bfloat16)
    low = (source - high.astype(jnp.float32)).astype(jnp.bfloat16)
    return jnp.dot(chosen, high, preferred_element_type=jnp.float32) + jnp.dot(
        chosen, low, preferred_element_type=jnp.float32
    )


def round_up(value, unit):
    return -(-value // unit) * unit


def owned_rows(flat, me, devices):
    length = flat.shape[0] // LANES
    share = len(TILE_ROWS) // devices
    wanted = TILE_ROWS.reshape(devices, share) - np.arange(devices)[:, None] * length
    before = round_up(max(0, -wanted.min()) + 1, TILE)
    after = round_up(max(0, wanted.max() + 1 - length), TILE)
    wanted = wanted + before - 1
    smalls = SMALL_ROWS[None] - np.arange(devices)[:, None] * length
    smalls = np.where((smalls >= 0) & (smalls < length), smalls + before - 1, -1)
    index = jnp.asarray(np.concatenate([wanted, smalls], axis=1).astype(np.int32))
    around = halo(flat.reshape(length, LANES), before, after, devices)
    shifted = jnp.concatenate([around[:-1, SHIFT:], around[1:, :SHIFT]], axis=1)
    at = me * length - before + 1 + lax.broadcasted_iota(jnp.int32, (shifted.shape[0], 1), 0)
    virtual = jnp.where(at < TABLE_END, around[1:], shifted)
    picked = pick_rows(lax.dynamic_index_in_dim(index, me, 0, keepdims=False), virtual)
    return picked[:share], picked[share:]


def flat_share(owned, smalls, me, devices, flat_length):
    length = flat_length // LANES // devices
    share = len(TILE_ROWS) // devices
    place = np.full(max(VIRTUAL, devices * length + 1), -1, np.int64)
    place[TILE_ROWS] = np.arange(len(TILE_ROWS))
    small_place = np.full(place.shape, -1, np.int64)
    small_place[SMALL_ROWS[SMALL_ROWS >= 0]] = np.flatnonzero(SMALL_ROWS >= 0)
    span = np.arange(devices)[:, None] * length + np.arange(length + 1)[None]
    relative = place[span] - np.arange(devices)[:, None] * share
    has = place[span] >= 0
    before = round_up(max(0, -relative[has].min()), TILE)
    after = round_up(max(0, relative[has].max() + 1 - share), TILE)
    smalls_at = before + share + after
    index = np.where(has, relative + before, -1)
    index = np.where(small_place[span] >= 0, small_place[span] + smalls_at, index)
    index = jnp.asarray(index.astype(np.int32))
    source = jnp.concatenate([halo(owned, before, after, devices), smalls], axis=0)
    virtual = pick_rows(lax.dynamic_index_in_dim(index, me, 0, keepdims=False), source)
    here, following = virtual[:-1], virtual[1:]
    at = me * length + lax.broadcasted_iota(jnp.int32, (length, 1), 0)
    lane = lax.broadcasted_iota(jnp.int32, (1, LANES), 1)
    shifted = jnp.concatenate([here[:, LANES - SHIFT :], following[:, : LANES - SHIFT]], axis=1)
    straight = (at < TABLE_END - 1) | ((at == TABLE_END - 1) & (lane < SHIFT))
    return jnp.where(straight, here, shifted).reshape(-1)


VECTOR_ROWS = len(VECTORS) * D // LANES
FC1_AT = round_up(VECTOR_ROWS, 8)
TABLE_AT = FC1_AT + FF // LANES
TABLE_ROWS = count_rows(SIZES["relative_table"])


def unpack_smalls(rows):
    vectors = rows[:, :VECTOR_ROWS].astype(jnp.float32).reshape(2, len(VECTORS), D)
    vectors = jnp.pad(vectors, ((0, 0), (0, 16 - len(VECTORS)), (0, 0)))
    fc1 = rows[:, FC1_AT:TABLE_AT].astype(jnp.float32).reshape(2, 1, FF)
    table = rows[:, TABLE_AT : TABLE_AT + TABLE_ROWS].reshape(2, -1)[:, : RELS * HEADS]
    return vectors, fc1, table.reshape(2, RELS, HEADS)


def pack_smalls(vectors, fc1, table):
    vectors = vectors.reshape(2, VECTOR_ROWS, LANES)
    vectors = jnp.pad(vectors, ((0, 0), (0, FC1_AT - VECTOR_ROWS), (0, 0)))
    table = jnp.pad(table.reshape(2, RELS * HEADS), ((0, 0), (0, round_up(TABLE_ROWS, 8) * LANES - RELS * HEADS)))
    return jnp.concatenate([vectors, fc1.reshape(2, -1, LANES), table.reshape(2, -1, LANES)], axis=1)


def column_choice():
    offset = np.arange(GRID)[:, None] - np.arange(GRID)[None, :] + GRID - 1
    return (np.arange(2 * GRID - 1)[:, None] == offset.reshape(1, -1)).astype(np.float32)


SIDE = 2 * GRID - 1
PATCHES = GRID * GRID
WINDOW = round_up(SIDE * GRID, LANES) + LANES
WIDE = round_up(ROWS, LANES)


def bias_kernel(spread_ref, ends_ref, bias_ref):
    lane = lax.broadcasted_iota(jnp.int32, (1, WIDE), 1)
    inner = (lane >= 1) & (lane < SEQ)
    top, left, corner = ends_ref[0, 0:1, 0:1], ends_ref[0, 1:2, 0:1], ends_ref[0, 2:3, 0:1]
    bias_ref[...] = jnp.zeros_like(bias_ref)
    bias_ref[0, 0:1] = jnp.where(inner, top, jnp.where(lane == 0, corner, 0.0))[:, :ROWS]
    spread = spread_ref[0]
    for row in range(GRID):
        start = (GRID - 1 - row) * GRID
        window = pltpu.roll(spread, (1 - start) % WINDOW, 1)[:GRID, :WIDE]
        window = jnp.where(inner, window, jnp.where(lane == 0, left, 0.0))
        bias_ref[0, 1 + row * GRID : 1 + (row + 1) * GRID] = window[:, :ROWS]


def biases_from_tables(tables):
    inner = tables[:, : SIDE * SIDE].reshape(2, SIDE, SIDE, HEADS)[:, ::-1]
    choice = jnp.asarray(column_choice(), jnp.bfloat16)
    spread = jnp.einsum("lrdh,dc->lhrc", inner, choice, preferred_element_type=jnp.float32)
    spread = spread.reshape(2 * HEADS, SIDE, GRID, GRID).transpose(0, 2, 1, 3)
    spread = spread.reshape(2 * HEADS, GRID, SIDE * GRID)
    spread = jnp.pad(spread, ((0, 0), (0, 16 - GRID), (0, WINDOW - SIDE * GRID)))
    ends = tables[:, SIDE * SIDE :].astype(jnp.float32).transpose(0, 2, 1).reshape(2 * HEADS, 3, 1)
    ends = jnp.broadcast_to(jnp.pad(ends, ((0, 0), (0, 5), (0, 0))), (2 * HEADS, 8, LANES))
    return pl.pallas_call(
        bias_kernel,
        grid=(2 * HEADS,),
        in_specs=[
            pl.BlockSpec((1, 16, WINDOW), lambda i: (i, 0, 0)),
            pl.BlockSpec((1, 8, LANES), lambda i: (i, 0, 0)),
        ],
        out_specs=pl.BlockSpec((1, ROWS, ROWS), lambda i: (i, 0, 0)),
        out_shape=jax.ShapeDtypeStruct((2 * HEADS, ROWS, ROWS), jnp.float32),
        name="bias",
    )(spread, ends)


def table_kernel(grad_ref, spread_ref, ends_ref):
    lane = lax.broadcasted_iota(jnp.int32, (1, ROWS), 1)
    inner = (lane >= 1) & (lane < SEQ)
    total = jnp.zeros((GRID, WINDOW), jnp.float32)
    left = jnp.zeros((1, 1), jnp.float32)
    for row in range(GRID):
        start = (GRID - 1 - row) * GRID
        block = grad_ref[0, 1 + row * GRID : 1 + (row + 1) * GRID]
        left = left + jnp.sum(jnp.where(lane == 0, block, 0.0), keepdims=True)
        block = jnp.where(inner, block, 0.0)
        block = jnp.concatenate([block, jnp.zeros((GRID, WINDOW - ROWS), jnp.float32)], axis=1)
        total = total + pltpu.roll(block, (start - 1) % WINDOW, 1)
    spread_ref[0, :GRID] = total
    spread_ref[0, GRID:] = jnp.zeros((16 - GRID, WINDOW), jnp.float32)
    first = grad_ref[0, 0:1]
    top = jnp.sum(jnp.where(inner, first, 0.0), keepdims=True)
    corner = jnp.sum(jnp.where(lane == 0, first, 0.0), keepdims=True)
    row = lax.broadcasted_iota(jnp.int32, (8, LANES), 0)
    ends_ref[0] = jnp.where(row == 0, top, jnp.where(row == 1, left, corner))


def tables_from_biases(grads):
    pieces = []
    for grad in grads:
        pieces.append(
            pl.pallas_call(
                table_kernel,
                grid=(HEADS,),
                in_specs=[pl.BlockSpec((1, ROWS, ROWS), lambda i: (i, 0, 0))],
                out_specs=[
                    pl.BlockSpec((1, 16, WINDOW), lambda i: (i, 0, 0)),
                    pl.BlockSpec((1, 8, LANES), lambda i: (i, 0, 0)),
                ],
                out_shape=[
                    jax.ShapeDtypeStruct((HEADS, 16, WINDOW), jnp.float32),
                    jax.ShapeDtypeStruct((HEADS, 8, LANES), jnp.float32),
                ],
                name="table_back",
            )(grad)
        )
    spread = jnp.stack([piece[0] for piece in pieces])[:, :, :GRID, : SIDE * GRID]
    ends = jnp.stack([piece[1] for piece in pieces])[:, :, :3, 0].transpose(0, 2, 1)
    spread = spread.reshape(2 * HEADS, GRID, SIDE, GRID).transpose(2, 0, 1, 3)
    spread = spread.reshape(SIDE * 2 * HEADS, PATCHES)
    choice = jnp.asarray(column_choice().T, jnp.bfloat16)
    high = spread.astype(jnp.bfloat16)
    low = (spread - high.astype(jnp.float32)).astype(jnp.bfloat16)
    table = jnp.dot(high, choice, preferred_element_type=jnp.float32) + jnp.dot(
        low, choice, preferred_element_type=jnp.float32
    )
    table = table.reshape(SIDE, 2, HEADS, SIDE)[::-1].transpose(1, 0, 3, 2).reshape(2, SIDE * SIDE, HEADS)
    return jnp.concatenate([table, ends], axis=1)


NT = (((1,), (1,)), ((), ()))
NN = (((1,), (0,)), ((), ()))
TN = (((0,), (0,)), ((), ()))


def product(left, right, dims):
    return lax.dot_general(left, right, dims, preferred_element_type=jnp.float32)


def own_lanes(head):
    lane = lax.broadcasted_iota(jnp.int32, (1, LANES), 1)
    return lane < HEAD if head == 0 else lane >= HEAD


def head_weights(query, key, bias, count, head):
    chosen = jnp.where(own_lanes(head), query, jnp.zeros_like(query))
    scores = product(chosen, key, NT) + bias
    column = lax.broadcasted_iota(jnp.int32, (1, ROWS), 1)
    scores = jnp.where(column < count, scores, NEGATIVE)
    grown = jnp.exp(scores - jnp.max(scores, axis=1, keepdims=True))
    return grown * (1.0 / jnp.sum(grown, axis=1, keepdims=True))


def attention_kernel(pairs, counts_ref, query_ref, key_ref, value_ref, bias_ref, out_ref):
    count = counts_ref[pl.program_id(1)]
    for pair in range(pairs):
        lanes = slice(pair * LANES, (pair + 1) * LANES)
        query, key, value = query_ref[:, lanes], key_ref[:, lanes], value_ref[:, lanes]
        parts = []
        for head in range(2):
            weights = head_weights(query, key, bias_ref[2 * pair + head], count, head)
            parts.append(product(weights.astype(jnp.bfloat16), value, NN))
        out_ref[:, lanes] = jnp.where(own_lanes(0), parts[0], parts[1]).astype(jnp.bfloat16)


def attention_back_kernel(pairs, counts_ref, query_ref, key_ref, value_ref, grad_ref, bias_ref, out_ref, db_ref):
    image = pl.program_id(1)
    count = counts_ref[image]

    @pl.when(image == 0)
    def _():
        db_ref[...] = jnp.zeros_like(db_ref)

    for pair in range(pairs):
        lanes = slice(pair * LANES, (pair + 1) * LANES)
        query, key, value, grad = query_ref[:, lanes], key_ref[:, lanes], value_ref[:, lanes], grad_ref[:, lanes]
        dq, dk, dv = [], [], []
        for head in range(2):
            weights = head_weights(query, key, bias_ref[2 * pair + head], count, head)
            chosen = jnp.where(own_lanes(head), grad, jnp.zeros_like(grad))
            weighted = weights * product(chosen, value, NT)
            dv.append(product(weights.astype(jnp.bfloat16), grad, TN))
            grad_scores = weighted - weights * jnp.sum(weighted, axis=1, keepdims=True)
            low = grad_scores.astype(jnp.bfloat16)
            dq.append(product(low, key, NN))
            dk.append(product(low, query, TN))
            db_ref[2 * pair + head] += grad_scores
        first = own_lanes(0)
        out_ref[0, :, lanes] = (jnp.where(first, dq[0], dq[1]) * HEAD**-0.5).astype(jnp.bfloat16)
        out_ref[1, :, lanes] = jnp.where(first, dk[0], dk[1]).astype(jnp.bfloat16)
        out_ref[2, :, lanes] = jnp.where(first, dv[0], dv[1]).astype(jnp.bfloat16)


def attention_specs(pairs, layer):
    steps = D // LANES // pairs
    lanes = [
        pl.BlockSpec((ROWS, pairs * LANES), lambda step, image, counts, part=part: (image, part * steps + step))
        for part in range(3)
    ]
    bias = pl.BlockSpec((2 * pairs, ROWS, ROWS), lambda step, image, counts: (layer * steps + step, 0, 0))
    return steps, lanes, bias


def attention(counts, qkv, biases, layer, pairs=6):
    steps, lanes, bias_spec = attention_specs(pairs, layer)
    return pl.pallas_call(
        functools.partial(attention_kernel, pairs),
        grid_spec=pltpu.PrefetchScalarGridSpec(
            num_scalar_prefetch=1,
            grid=(steps, qkv.shape[0] // ROWS),
            in_specs=lanes + [bias_spec],
            out_specs=lanes[0],
        ),
        out_shape=jax.ShapeDtypeStruct((qkv.shape[0], D), jnp.bfloat16),
        compiler_params=pltpu.CompilerParams(vmem_limit_bytes=VMEM_LIMIT),
        name="attention",
    )(counts, qkv, qkv, qkv, biases)


def attention_back(counts, qkv, grad, biases, layer, pairs=3):
    steps, lanes, bias_spec = attention_specs(pairs, layer)
    _, _, out_bias_spec = attention_specs(pairs, 0)
    return pl.pallas_call(
        functools.partial(attention_back_kernel, pairs),
        grid_spec=pltpu.PrefetchScalarGridSpec(
            num_scalar_prefetch=1,
            grid=(steps, qkv.shape[0] // ROWS),
            in_specs=lanes + [lanes[0], bias_spec],
            out_specs=[
                pl.BlockSpec((3, ROWS, pairs * LANES), lambda step, image, counts: (0, image, step)),
                out_bias_spec,
            ],
        ),
        out_shape=[
            jax.ShapeDtypeStruct((3, qkv.shape[0], D), jnp.bfloat16),
            jax.ShapeDtypeStruct((HEADS, ROWS, ROWS), jnp.float32),
        ],
        compiler_params=pltpu.CompilerParams(vmem_limit_bytes=VMEM_LIMIT),
        name="attention_back",
    )(counts, qkv, qkv, qkv, grad, biases)


def tile_starts():
    starts, at = {}, 0
    for name, (depth, width) in WEIGHTS.items():
        starts[name] = at
        at += depth // TILE * (width // LANES)
    return starts


FIRST = tile_starts()
MLP_FIRST = FIRST["proj_weight"]
SPAN = 1024


def load_weight(ref, base, name, row, rows, column, columns):
    first, across = FIRST[name] - base, WEIGHTS[name][1] // LANES
    lines = []
    for i in range(rows):
        at = first + (row + i) * across + column
        lines.append(jnp.concatenate([ref[at + j] for j in range(columns)], axis=1))
    return jnp.concatenate(lines, axis=0)


def gelu_and_slope(values):
    size = jnp.abs(values)
    step = 1.0 / (1.0 + (0.3275911 / math.sqrt(2.0)) * size)
    bell = jnp.exp(-0.5 * values * values)
    series = 1.061405429
    for term in (-1.453152027, 1.421413741, -0.284496736, 0.254829592):
        series = series * step + term
    tail = 0.5 * series * step * bell
    area = jnp.where(values < 0, tail, 1.0 - tail)
    return values * area, area + values * bell * (1.0 / math.sqrt(2.0 * math.pi))


def norm_parts(values):
    centre = values - jnp.mean(values, axis=-1, keepdims=True)
    spread = jnp.mean(centre * centre, axis=-1, keepdims=True)
    inverse = lax.rsqrt(spread + EPSILON)
    return centre * inverse, inverse


def norm_back(grad, normal, inverse, gain):
    scaled = grad * gain
    first = jnp.mean(scaled, axis=-1, keepdims=True)
    second = jnp.mean(scaled * normal, axis=-1, keepdims=True)
    return (scaled - first - normal * second) * inverse


def column_sums(values):
    return jnp.sum(values, axis=0, keepdims=True)


def vector(ref, name):
    return ref[ROW[name] : ROW[name] + 1]


def whole_spec(shape):
    return pl.BlockSpec(shape, lambda *_: (0,) * len(shape))


ANYWHERE = pl.BlockSpec(memory_space=pl.ANY)
PARAMS = pltpu.CompilerParams(vmem_limit_bytes=VMEM_LIMIT)


def low_like(*shape):
    return jax.ShapeDtypeStruct(shape, jnp.bfloat16)


def full_like(*shape):
    return jax.ShapeDtypeStruct(shape, jnp.float32)


def project_kernel(places, slots, at_ref, *refs):
    parts, refs = refs[: len(slots)], refs[len(slots) :]
    hidden_ref, vectors_ref, normed_ref, qkv_ref, tiles_ref, whole_ref, sems, out_sem = refs
    copies = copies_between(places, at_ref, parts, slots, whole_ref, sems, True)
    for copy in copies:
        copy.start()
    normal, _ = norm_parts(hidden_ref[...])
    normed_ref[...] = (normal * vector(vectors_ref, "norm1_gain") + vector(vectors_ref, "norm1_bias")).astype(
        jnp.bfloat16
    )
    for copy in copies:
        copy.wait()
    leaving = pltpu.make_async_copy(whole_ref, tiles_ref, out_sem)
    leaving.start()
    across = D // LANES
    for part in range(3):
        weight = load_weight(whole_ref, 0, "qkv_weight", 0, D // TILE, part * across, across)
        rows = product(normed_ref[...], weight, NN)
        if part == 0:
            rows = (rows + vector(vectors_ref, "query_bias")) * HEAD**-0.5
        if part == 2:
            rows = rows + vector(vectors_ref, "value_bias")
        qkv_ref[:, part * D : (part + 1) * D] = rows.astype(jnp.bfloat16)
    leaving.wait()


def project(places, position, parts, hidden, vectors):
    arrays = [array for array, _ in parts]
    slots = [listed for _, listed in parts]
    rows = hidden.shape[0]
    return pl.pallas_call(
        functools.partial(project_kernel, places, slots),
        grid_spec=pltpu.PrefetchScalarGridSpec(
            num_scalar_prefetch=1,
            grid=(1,),
            in_specs=[ANYWHERE] * len(arrays) + [whole_spec((rows, D)), whole_spec(vectors.shape)],
            out_specs=[whole_spec((rows, D)), whole_spec((rows, 3 * D)), ANYWHERE],
            scratch_shapes=[
                pltpu.VMEM((TILES, TILE, LANES), jnp.bfloat16),
                pltpu.SemaphoreType.DMA((sum(len(listed) for listed in slots),)),
                pltpu.SemaphoreType.DMA(()),
            ],
        ),
        out_shape=[low_like(rows, D), low_like(rows, 3 * D), low_like(TILES, TILE, LANES)],
        compiler_params=PARAMS,
        name="project",
    )(position, *arrays, hidden, vectors)


def mlp_weights(tiles_ref, weight_ref, sems, order):
    copies = []
    for i, name in enumerate(order):
        depth, width = WEIGHTS[name]
        count = depth // TILE * (width // LANES)
        here = weight_ref.at[pl.ds(FIRST[name] - MLP_FIRST, count)]
        copies.append(pltpu.make_async_copy(tiles_ref.at[pl.ds(FIRST[name], count)], here, sems.at[i]))
        copies[-1].start()
    return copies


def span_of(step):
    return pl.ds(pl.multiple_of(step * SPAN, SPAN), SPAN)


def mlp_kernel(
    attended_ref,
    hidden_ref,
    vectors_ref,
    fc1_bias_ref,
    tiles_ref,
    result_ref,
    branch_ref,
    middle_ref,
    normed_ref,
    activ_ref,
    slope_ref,
    mlp_ref,
    total_ref,
    weight_ref,
    sems,
):
    copies = mlp_weights(tiles_ref, weight_ref, sems, ("proj_weight", "fc1_weight", "fc2_weight"))
    copies[0].wait()
    across = D // LANES
    weight = load_weight(weight_ref, MLP_FIRST, "proj_weight", 0, D // TILE, 0, across)
    branch = product(attended_ref[...], weight, NN) + vector(vectors_ref, "proj_bias")
    branch_ref[...] = branch.astype(jnp.bfloat16)
    middle_ref[...] = hidden_ref[...] + vector(vectors_ref, "gamma_attn") * branch
    normal, _ = norm_parts(middle_ref[...])
    normed_ref[...] = (normal * vector(vectors_ref, "norm2_gain") + vector(vectors_ref, "norm2_bias")).astype(
        jnp.bfloat16
    )
    total_ref[...] = jnp.broadcast_to(vector(vectors_ref, "fc2_bias"), total_ref.shape)
    copies[1].wait()
    copies[2].wait()

    def step(i, _):
        span = span_of(i)
        weight = load_weight(weight_ref, MLP_FIRST, "fc1_weight", 0, D // TILE, i * (SPAN // LANES), SPAN // LANES)
        activ, slope = gelu_and_slope(product(normed_ref[...], weight, NN) + fc1_bias_ref[:, span])
        activ = activ.astype(jnp.bfloat16)
        activ_ref[:, span] = activ
        slope_ref[:, span] = slope.astype(jnp.bfloat16)
        weight = load_weight(weight_ref, MLP_FIRST, "fc2_weight", i * (SPAN // TILE), SPAN // TILE, 0, across)
        total_ref[...] += product(activ, weight, NN)
        return 0

    lax.fori_loop(0, FF // SPAN, step, 0)
    mlp_ref[...] = total_ref[...].astype(jnp.bfloat16)
    result_ref[...] = middle_ref[...] + vector(vectors_ref, "gamma_mlp") * total_ref[...]


def mlp_scratch(rows):
    return [
        pltpu.VMEM((rows, D), jnp.float32),
        pltpu.VMEM((TILES - MLP_FIRST, TILE, LANES), jnp.bfloat16),
        pltpu.SemaphoreType.DMA((3,)),
    ]


def mlp(attended, hidden, vectors, fc1_bias, tiles):
    rows = hidden.shape[0]
    outs = [full_like(rows, D), low_like(rows, D), full_like(rows, D), low_like(rows, D)]
    outs += [low_like(rows, FF), low_like(rows, FF), low_like(rows, D)]
    ins = [attended, hidden, vectors, fc1_bias]
    return pl.pallas_call(
        mlp_kernel,
        grid=(1,),
        in_specs=[whole_spec(array.shape) for array in ins] + [ANYWHERE],
        out_specs=[whole_spec(out.shape) for out in outs],
        out_shape=outs,
        scratch_shapes=mlp_scratch(rows),
        compiler_params=PARAMS,
        name="mlp",
    )(*ins, tiles)


def mlp_back_kernel(
    grad_ref,
    branch_ref,
    middle_ref,
    slope_ref,
    mlp_ref,
    vectors_ref,
    tiles_ref,
    grad_middle_ref,
    grad_attended_ref,
    grad_mlp_ref,
    grad_pre_ref,
    grad_branch_ref,
    sums_ref,
    fc1_sums_ref,
    total_ref,
    weight_ref,
    sems,
):
    copies = mlp_weights(tiles_ref, weight_ref, sems, ("fc2_weight", "fc1_weight", "proj_weight"))
    across = D // LANES
    grad = grad_ref[...]
    sums_ref[ROW["gamma_mlp"] - 4 : ROW["gamma_mlp"] - 3] = column_sums(grad * mlp_ref[...].astype(jnp.float32))
    grad_mlp = grad * vector(vectors_ref, "gamma_mlp")
    sums_ref[ROW["fc2_bias"] - 4 : ROW["fc2_bias"] - 3] = column_sums(grad_mlp)
    grad_mlp_ref[...] = grad_mlp.astype(jnp.bfloat16)
    total_ref[...] = jnp.zeros_like(total_ref)
    copies[0].wait()
    copies[1].wait()

    def step(i, _):
        span = span_of(i)
        weight = load_weight(weight_ref, MLP_FIRST, "fc2_weight", i * (SPAN // TILE), SPAN // TILE, 0, across)
        grad_pre = product(grad_mlp_ref[...], weight, NT) * slope_ref[:, span].astype(jnp.float32)
        fc1_sums_ref[:, span] = column_sums(grad_pre)
        grad_pre = grad_pre.astype(jnp.bfloat16)
        grad_pre_ref[:, span] = grad_pre
        weight = load_weight(weight_ref, MLP_FIRST, "fc1_weight", 0, D // TILE, i * (SPAN // LANES), SPAN // LANES)
        total_ref[...] += product(grad_pre, weight, NT)
        return 0

    lax.fori_loop(0, FF // SPAN, step, 0)
    normal, inverse = norm_parts(middle_ref[...])
    grad_normed = total_ref[...]
    sums_ref[ROW["norm2_gain"] - 4 : ROW["norm2_gain"] - 3] = column_sums(grad_normed * normal)
    sums_ref[ROW["norm2_bias"] - 4 : ROW["norm2_bias"] - 3] = column_sums(grad_normed)
    grad_middle = grad_ref[...] + norm_back(grad_normed, normal, inverse, vector(vectors_ref, "norm2_gain"))
    grad_middle_ref[...] = grad_middle
    sums_ref[ROW["gamma_attn"] - 4 : ROW["gamma_attn"] - 3] = column_sums(
        grad_middle * branch_ref[...].astype(jnp.float32)
    )
    grad_branch = grad_middle * vector(vectors_ref, "gamma_attn")
    sums_ref[ROW["proj_bias"] - 4 : ROW["proj_bias"] - 3] = column_sums(grad_branch)
    grad_branch_ref[...] = grad_branch.astype(jnp.bfloat16)
    copies[2].wait()
    weight = load_weight(weight_ref, MLP_FIRST, "proj_weight", 0, D // TILE, 0, across)
    grad_attended_ref[...] = product(grad_branch_ref[...], weight, NT).astype(jnp.bfloat16)


def mlp_back(grad, saved, vectors, tiles):
    rows = grad.shape[0]
    outs = [full_like(rows, D), low_like(rows, D), low_like(rows, D), low_like(rows, FF), low_like(rows, D)]
    outs += [full_like(8, D), full_like(1, FF)]
    ins = [grad, saved["branch"], saved["middle"], saved["slope"], saved["mlp_out"], vectors]
    return pl.pallas_call(
        mlp_back_kernel,
        grid=(1,),
        in_specs=[whole_spec(array.shape) for array in ins] + [ANYWHERE],
        out_specs=[whole_spec(out.shape) for out in outs],
        out_shape=outs,
        scratch_shapes=mlp_scratch(rows),
        compiler_params=PARAMS,
        name="mlp_back",
    )(*ins, tiles)


def weight_back_kernel(places, slots, at_ref, *refs):
    normed_ref, project_ref, attended_ref, branch_ref, normed2_ref, pre_ref, activ_ref, mlp_ref = refs[:8]
    parts, (whole_ref, sems) = refs[8 : 8 + len(slots)], refs[8 + len(slots) :]
    across, count = D // LANES, 256 // TILE

    def put(name, row, column, left, grad):
        block = product(left, grad, TN).astype(jnp.bfloat16)
        wide = WEIGHTS[name][1] // LANES
        for i in range(count):
            for j in range(across):
                at = FIRST[name] + (row + i) * wide + column + j
                whole_ref[at] = block[i * TILE : (i + 1) * TILE, j * LANES : (j + 1) * LANES]

    def columns(i):
        return pl.ds(pl.multiple_of(i * 256, 256), 256)

    def narrow(i, _):
        for part in range(3):
            put("qkv_weight", i * count, part * across, normed_ref[:, columns(i)], project_ref[part])
        put("proj_weight", i * count, 0, attended_ref[:, columns(i)], branch_ref[...])
        for part in range(FF // D):
            grad = pre_ref[:, part * D : (part + 1) * D]
            put("fc1_weight", i * count, part * across, normed2_ref[:, columns(i)], grad)
        return 0

    def wide(i, _):
        put("fc2_weight", i * count, 0, activ_ref[:, columns(i)], mlp_ref[...])
        return 0

    lax.fori_loop(0, D // 256, narrow, 0)
    lax.fori_loop(0, FF // 256, wide, 0)
    copies = copies_between(places, at_ref, parts, slots, whole_ref, sems, False)
    for copy in copies:
        copy.start()
    for copy in copies:
        copy.wait()


def weight_back(places, position, slots, ins):
    count = TILES // sum(len(listed) for listed in slots)
    return pl.pallas_call(
        functools.partial(weight_back_kernel, places, slots),
        grid_spec=pltpu.PrefetchScalarGridSpec(
            num_scalar_prefetch=1,
            grid=(1,),
            in_specs=[whole_spec(array.shape) for array in ins],
            out_specs=[ANYWHERE] * len(slots),
            scratch_shapes=[
                pltpu.VMEM((TILES, TILE, LANES), jnp.bfloat16),
                pltpu.SemaphoreType.DMA((sum(len(listed) for listed in slots),)),
            ],
        ),
        out_shape=[low_like(len(listed) * count, TILE, LANES) for listed in slots],
        compiler_params=PARAMS,
        name="weight_back",
    )(position, *ins)


def input_back_kernel(project_ref, grad_middle_ref, hidden_ref, vectors_ref, tiles_ref, out_ref, sums_ref, total_ref):
    across = D // LANES
    for part in range(3):
        weight = load_weight(tiles_ref, 0, "qkv_weight", 0, D // TILE, part * across, across)
        rows = product(project_ref[part], weight, NT)
        total_ref[...] = rows if part == 0 else total_ref[...] + rows
    normal, inverse = norm_parts(hidden_ref[...])
    grad_normed = total_ref[...]
    sums_ref[0:1] = column_sums(grad_normed * normal)
    sums_ref[1:2] = column_sums(grad_normed)
    sums_ref[2:3] = column_sums(project_ref[0].astype(jnp.float32))
    sums_ref[3:4] = column_sums(project_ref[2].astype(jnp.float32))
    out_ref[...] = grad_middle_ref[...] + norm_back(
        grad_normed, normal, inverse, vector(vectors_ref, "norm1_gain")
    )


def input_back(grad_project, grad_middle, hidden, vectors, tiles):
    rows = hidden.shape[0]
    ins = [grad_project, grad_middle, hidden, vectors]
    return pl.pallas_call(
        input_back_kernel,
        grid=(1,),
        in_specs=[whole_spec(array.shape) for array in ins] + [whole_spec((MLP_FIRST, TILE, LANES))],
        out_specs=[whole_spec((rows, D)), whole_spec((8, D))],
        out_shape=[full_like(rows, D), full_like(8, D)],
        scratch_shapes=[pltpu.VMEM((rows, D), jnp.float32)],
        compiler_params=PARAMS,
        name="input_back",
    )(*ins, tiles)


def pad_rows(images):
    padded = jnp.pad(images, ((0, 0), (0, ROWS - SEQ), (0, 0)))
    return padded.reshape(-1, D).astype(jnp.float32)


def cut_rows(rows):
    return rows.reshape(-1, ROWS, D)[:, :SEQ].astype(jnp.bfloat16)


class Places:
    def __init__(self, dp, fsdp):
        low = 2 if dp % 2 == 0 else 1
        core = 2 if fsdp % 2 == 0 else 1
        self.sizes = {"y": low, "x": dp // low, "z": fsdp // core, "c": core}
        self.count = dp * fsdp
        grid = np.arange(self.count).reshape(tuple(self.sizes.values()))
        self.grid = grid
        self.axis = {name: i for i, name in enumerate(self.sizes)}

    def send(self, block, axis, hop):
        target = np.roll(self.grid, -hop, axis=self.axis[axis])
        perm = [(int(a), int(b)) for a, b in zip(self.grid.reshape(-1), target.reshape(-1))]
        return lax.ppermute(block, AXES, perm)

    def fetch(self, block, axis, hop):
        return self.send(block, axis, -hop)

    def total(self, block):
        for axis in ("c", "z", "x", "y"):
            own = block
            for hop in range(1, self.sizes[axis]):
                block = block + self.fetch(own, axis, hop)
        return block

    def position(self, me):
        return jnp.stack([(me // int(np.prod(self.grid.shape[i + 1 :]))) % n for i, n in enumerate(self.grid.shape)])


def block_at(at_ref, places, offset):
    number = 0
    for i, size in enumerate(places.grid.shape):
        number = number * size + lax.rem(at_ref[i] + offset[i], size)
    return number


def copies_between(places, at_ref, parts, slots, whole_ref, sems, inward):
    copies = []
    for part, listed in zip(parts, slots):
        count = part.shape[0] // len(listed)
        for i, slot in enumerate(listed):
            start = 0 if slot is None else block_at(at_ref, places, slot[0]) * (TILES // places.count) + slot[1]
            here, there = part.at[pl.ds(i * count, count)], whole_ref.at[pl.ds(start, count)]
            ends = (here, there) if inward else (there, here)
            copies.append(pltpu.make_async_copy(*ends, sems.at[len(copies)]))
    return copies


def offset_of(**hops):
    return tuple(hops.get(axis, 0) for axis in ("y", "x", "z", "c"))


def tie(*trees):
    leaves, structure = jax.tree.flatten(trees)
    tied = iter(lax.optimization_barrier([leaf for leaf in leaves if isinstance(leaf, jax.Array)]))
    return structure.unflatten([next(tied) if isinstance(leaf, jax.Array) else leaf for leaf in leaves])


def join(blocks):
    return jnp.concatenate(blocks, axis=0) if len(blocks) > 1 else blocks[0]


ORDERS = (("x", "y"), ("y", "x"))


def group_of(shares, offsets):
    half = shares[0].shape[0] // 2
    return [(join([share[part * half : (part + 1) * half] for share in shares]), offsets) for part in range(2)]


def merge(*groups):
    return [(join([group[part][0] for group in groups]), sum((group[part][1] for group in groups), [])) for part in range(2)]


def fetch_column(places, share):
    hops = range(1, places.sizes["z"])
    return [places.fetch(share, "z", hop) for hop in hops], [offset_of(z=hop) for hop in hops]


def fetch_plane(places, group, step):
    arrived = []
    for (block, offsets), order in zip(group, ORDERS):
        at = places.axis[order[step]]
        hops = range(1, places.sizes[order[step]])
        moved = [offset[:at] + (hop,) + offset[at + 1 :] for hop in hops for offset in offsets]
        arrived.append((join([places.fetch(block, order[step], hop) for hop in hops]), moved))
    return arrived


def fetch_core(places, groups):
    half = TILES // places.count // 2
    blocks, slots = [], []
    for group in groups:
        for part, (block, offsets) in enumerate(group):
            blocks.append(block)
            slots.append([(offset, part * half) for offset in offsets])
    whole = join(blocks)
    listed = sum(slots, [])
    parts = [(whole, listed)]
    for hop in range(1, places.sizes["c"]):
        moved = [(offset[:3] + (hop,), first) for offset, first in listed]
        parts.append((places.fetch(whole, "c", hop), moved))
    return parts


def add_low(*blocks):
    total = blocks[0].astype(jnp.float32)
    for block in blocks[1:]:
        total = total + block.astype(jnp.float32)
    return total


def scatter_slots(places):
    half = TILES // places.count // 2
    size = places.sizes
    slots = []
    for part, (first, second) in enumerate(ORDERS):
        for core in range(size["c"]):
            listed = []
            for one in range(size[first]):
                for two in range(size[second]):
                    for z in range(size["z"]):
                        listed.append((offset_of(**{first: one, second: two, "z": z, "c": core}), part * half))
            slots.append(listed)
    return slots


def send_core(places, parts):
    cores = places.sizes["c"]
    halves = [parts[:cores], parts[cores:]]
    return [[mine] + [places.send(other, "c", hop) for hop, other in enumerate(others, 1)] for mine, *others in halves]


def send_plane(places, sums, step):
    result = []
    for blocks, order in zip(sums, ORDERS):
        axis = order[step]
        share = blocks[0].shape[0] // places.sizes[axis]
        cuts = [slice(i * share, (i + 1) * share) for i in range(places.sizes[axis])]
        totals = [add_low(*[block[cut] for block in blocks]).astype(jnp.bfloat16) for cut in cuts]
        result.append([totals[0]] + [places.send(total, axis, hop) for hop, total in enumerate(totals[1:], 1)])
    return result


def send_column(places, sums):
    count = places.sizes["z"]
    share = sums[0][0].shape[0] // count
    totals = []
    for hop in range(count):
        cut = slice(hop * share, (hop + 1) * share)
        totals.append(join([add_low(*[block[cut] for block in blocks]).astype(jnp.bfloat16) for blocks in sums]))
    return [totals[0]] + [places.send(total, "z", hop) for hop, total in enumerate(totals[1:], 1)]


class Layer:
    def __init__(self, number, places, position, counts, vectors, fc1_bias, biases):
        self.number, self.places, self.position, self.counts, self.biases = number, places, position, counts, biases
        self.vectors, self.fc1_bias = vectors[number], fc1_bias[number]

    def forward(self, hidden, parts):
        normed, qkv, self.tiles = project(self.places, self.position, parts, hidden, self.vectors)
        attended = attention(self.counts, qkv, self.biases, self.number)
        result, branch, middle, normed2, activ, slope, mlp_out = mlp(
            attended, hidden, self.vectors, self.fc1_bias, self.tiles
        )
        self.saved = dict(hidden=hidden, normed=normed, qkv=qkv, attended=attended, branch=branch, middle=middle)
        self.saved.update(normed2=normed2, activ=activ, slope=slope, mlp_out=mlp_out)
        return result

    def back_mlp(self, grad):
        return mlp_back(grad, self.saved, self.vectors, self.tiles)

    def back_attention(self, passed):
        return attention_back(self.counts, self.saved["qkv"], passed[1], self.biases, self.number)

    def back_weights(self, passed, grad_project, slots):
        _, _, grad_mlp, grad_pre, grad_branch, _, _ = passed
        saved = self.saved
        ins = [saved["normed"], grad_project, saved["attended"], grad_branch, saved["normed2"], grad_pre]
        return weight_back(self.places, self.position, slots, ins + [saved["activ"], grad_mlp])

    def back_input(self, passed, grad_project):
        return input_back(grad_project, passed[0], self.saved["hidden"], self.vectors, self.tiles)


def scatter_whole(parts):
    whole = parts[0].reshape(-1, LANES)
    return lax.psum_scatter(whole, AXES, scatter_dimension=0, tiled=True).astype(jnp.float32)


def local(dp, fsdp, tokens, counts, params_first, params_second, cotangent):
    devices = dp * fsdp
    places = Places(dp, fsdp)
    stepwise = TILES % (4 * devices) == 0
    tiles = TILES // devices
    me = lax.axis_index(AXES)
    position = places.position(me)
    own, own_smalls = owned_rows(params_first, me, devices)
    if stepwise:
        own = own.reshape(tiles, TILE, LANES)
        column, hops = fetch_column(places, own)
        near = group_of([own], [offset_of()])
        near_first = fetch_plane(places, near, 0)
    params, _ = tie(params_second, own)
    next_own, next_smalls = owned_rows(params, me, devices)
    vectors, fc1_bias, tables = unpack_smalls(places.total(jnp.stack([own_smalls, next_smalls])))
    biases = biases_from_tables(tables)
    first_layer, second_layer = [
        Layer(number, places, position, counts, vectors, fc1_bias, biases) for number in range(2)
    ]
    hidden = pad_rows(tokens)

    if stepwise:
        next_own = next_own.reshape(tiles, TILE, LANES)
        near_second = fetch_plane(places, merge(near, near_first), 1)
        far, next_own = tie(group_of(column, hops), next_own)
        next_column, next_hops = fetch_column(places, next_own)
        far_first = fetch_plane(places, far, 0)
        parts = fetch_core(places, [near, near_first, near_second, far])
        far_second = fetch_plane(places, merge(far, far_first), 1)
        parts += fetch_core(places, [far_first])
        group = group_of([next_own] + next_column, [offset_of()] + next_hops)
        far_second, group = tie(far_second, group)
        parts += fetch_core(places, [far_second])
        first = fetch_plane(places, group, 0)
        next_parts = fetch_core(places, [group])
        first, parts = tie(first, parts)
        second = fetch_plane(places, merge(group, first), 1)
        next_parts += fetch_core(places, [first])
        result = first_layer.forward(hidden, parts)
        second, result = tie(second, result)
        next_parts += fetch_core(places, [second])
    else:
        parts, next_parts = [
            [(lax.all_gather(share, AXES, axis=0, tiled=True).reshape(TILES, TILE, LANES), [None])]
            for share in (own, next_own)
        ]
        result = first_layer.forward(hidden, parts)
    result = second_layer.forward(result, next_parts)
    output = cut_rows(result)

    slots = scatter_slots(places) if stepwise else [[None]]
    next_passed = second_layer.back_mlp(pad_rows(cotangent))
    next_project, next_bias = second_layer.back_attention(next_passed)
    parts = second_layer.back_weights(next_passed, next_project, slots)
    if stepwise:
        sums = send_core(places, parts)
    else:
        next_share = scatter_whole(parts)
    grad, next_sums = second_layer.back_input(next_passed, next_project)
    passed = first_layer.back_mlp(grad)
    if stepwise:
        sums, passed = tie(sums, passed)
        sums = send_plane(places, sums, 0)
    project_grad, bias = first_layer.back_attention(passed)
    parts = first_layer.back_weights(passed, project_grad, slots)
    if stepwise:
        sums, parts = tie(sums, parts)
        sums = send_plane(places, sums, 1)
        own_sums = send_core(places, parts)
        own_sums, sums = tie(own_sums, sums)
        own_sums = send_plane(places, own_sums, 0)
        sums = send_column(places, sums)
        own_sums, sums = tie(own_sums, sums)
        next_share = add_low(*sums).reshape(-1, LANES)
        own_sums = send_column(places, send_plane(places, own_sums, 1))
        share = add_low(*own_sums).reshape(-1, LANES)
    else:
        share = scatter_whole(parts)
    grad, own_row_sums = first_layer.back_input(passed, project_grad)
    vector_grads = jnp.stack(
        [
            jnp.concatenate([row_sums[:4], later[5][: len(VECTORS) - 4]], axis=0)
            for row_sums, later in ((own_row_sums, passed), (next_sums, next_passed))
        ]
    )
    fc1_grads = jnp.stack([passed[6], next_passed[6]])
    table_grads = tables_from_biases([bias, next_bias])
    small_grads = places.total(pack_smalls(vector_grads, fc1_grads, table_grads))
    length = params_first.shape[0] * devices
    grad_first = flat_share(share, small_grads[0], me, devices, length)
    grad_second = flat_share(next_share, small_grads[1], me, devices, length)
    return output, cut_rows(grad), grad_first, grad_second


def solution(mesh):
    return jax.shard_map(
        functools.partial(local, mesh.shape["dp"], mesh.shape["fsdp"]),
        mesh=mesh,
        in_specs=(P(AXES, None, None), P(AXES), P(AXES), P(AXES), P(AXES, None, None)),
        out_specs=(P(AXES, None, None), P(AXES, None, None), P(AXES), P(AXES)),
        check_vma=False,
    )
```

```python
import functools
import math

import jax
import jax.numpy as jnp
import numpy as np
from jax import lax
from jax.experimental import pallas as pl
from jax.experimental.pallas import tpu as pltpu
from jax.sharding import PartitionSpec as P

D = 768
HEADS = 12
HEAD = D // HEADS
FF = 3072
GRID = 14
SEQ = 197
RELS = 732
ROWS = 208
LANES = 128
TILE = 16
AXES = ("dp", "fsdp")
VMEM_LIMIT = 56 * 2**20

EPSILON = 1e-06
NEGATIVE = -1000000000.0

ENTRIES = [
    ("norm1_gain", (D,)),
    ("norm1_bias", (D,)),
    ("qkv_weight", (D, 3 * D)),
    ("query_bias", (D,)),
    ("value_bias", (D,)),
    ("relative_table", (RELS, HEADS)),
    ("proj_weight", (D, D)),
    ("proj_bias", (D,)),
    ("gamma_attn", (D,)),
    ("norm2_gain", (D,)),
    ("norm2_bias", (D,)),
    ("fc1_weight", (D, FF)),
    ("fc1_bias", (FF,)),
    ("fc2_weight", (FF, D)),
    ("fc2_bias", (D,)),
    ("gamma_mlp", (D,)),
]
WEIGHTS = {name: dims for name, dims in ENTRIES if name.endswith("weight")}
SIZES = dict(ENTRIES)
VECTORS = [
    "norm1_gain",
    "norm1_bias",
    "query_bias",
    "value_bias",
    "proj_bias",
    "gamma_attn",
    "norm2_gain",
    "norm2_bias",
    "fc2_bias",
    "gamma_mlp",
]
ROW = {name: i for i, name in enumerate(VECTORS)}


def count_rows(dims):
    return -(-math.prod(dims) // LANES)


def virtual_starts():
    starts, at = {}, 0
    for name, dims in ENTRIES:
        starts[name] = at
        at += count_rows(dims)
    return starts, at


STARTS, VIRTUAL = virtual_starts()
SHIFT = RELS * HEADS % LANES
TABLE_END = STARTS["proj_weight"]


def tile_order():
    parts = []
    for name, (depth, width) in WEIGHTS.items():
        across = width // LANES
        rows = STARTS[name] + np.arange(depth * across).reshape(depth // TILE, TILE, across)
        parts.append(rows.transpose(0, 2, 1).reshape(-1))
    return np.concatenate(parts)


def small_order():
    groups = [VECTORS, ["fc1_bias"], ["relative_table"]]
    rows = []
    for group in groups:
        for name in group:
            rows += [STARTS[name] + i for i in range(count_rows(SIZES[name]))]
        rows += [-1] * (-len(rows) % 8)
    return np.array(rows)


TILE_ROWS = tile_order()
SMALL_ROWS = small_order()
TILES = len(TILE_ROWS) // TILE


def tie(*trees):
    leaves, structure = jax.tree.flatten(trees)
    tied = iter(lax.optimization_barrier([leaf for leaf in leaves if isinstance(leaf, jax.Array)]))
    return structure.unflatten([next(tied) if isinstance(leaf, jax.Array) else leaf for leaf in leaves])


def halo(block, before, after, devices, join=True):
    rows = block.shape[-2]
    pieces = [block] if join else []
    for hop in range(1, -(-before // rows) + 1):
        take = min(rows, before - (hop - 1) * rows)
        perm = [(i, i + hop) for i in range(devices - hop)]
        pieces.insert(0, lax.ppermute(block[..., rows - take :, :], AXES, perm))
    for hop in range(1, -(-after // rows) + 1):
        take = min(rows, after - (hop - 1) * rows)
        perm = [(i + hop, i) for i in range(devices - hop)]
        pieces.append(lax.ppermute(block[..., :take, :], AXES, perm))
    return jnp.concatenate(pieces, axis=-2)


def pick_rows(index, source):
    chosen = index[:, None] == lax.broadcasted_iota(jnp.int32, (1, source.shape[0]), 1)
    return jnp.dot(chosen.astype(jnp.bfloat16), source.astype(jnp.bfloat16), preferred_element_type=jnp.float32)


def round_up(value, unit):
    return -(-value // unit) * unit


class Owned:
    def __init__(self, flats, me, devices):
        length = flats[0].shape[0] // LANES
        share = len(TILE_ROWS) // devices
        starts = np.arange(devices)[:, None] * length
        wanted = TILE_ROWS.reshape(devices, share) - starts
        before = round_up(max(0, -wanted.min()) + 1, TILE)
        after = round_up(max(0, wanted.max() + 1 - length), TILE)
        smalls = SMALL_ROWS[None] - starts
        smalls = np.where((smalls >= 0) & (smalls < length), smalls + before - 1, -1)
        self.wanted = self.mine(wanted + before - 1, me)
        self.smalls = self.mine(smalls, me)
        around = halo(jnp.stack([flat.reshape(length, LANES) for flat in flats]), before, after, devices)
        shifted = jnp.concatenate([around[:, :-1, SHIFT:], around[:, 1:, :SHIFT]], axis=2)
        at = me * length - before + 1 + lax.broadcasted_iota(jnp.int32, (1, shifted.shape[1], 1), 1)
        self.virtual = jnp.where(at < TABLE_END, around[:, 1:], shifted)

    @staticmethod
    def mine(table, me):
        return lax.dynamic_index_in_dim(jnp.asarray(table.astype(np.int32)), me, 0, keepdims=False)

    def small_rows(self, *after):
        virtual, *_ = tie(self.virtual, *after)
        return jnp.stack([pick_rows(self.smalls, rows).astype(jnp.bfloat16) for rows in virtual])

    def share(self, number, *after):
        rows = self.virtual[number]
        if after:
            rows, *_ = tie(rows, *after)
        return pick_rows(self.wanted, rows).astype(jnp.bfloat16)


class FlatShare:
    def __init__(self, me, devices, flat_length):
        length = flat_length // LANES // devices
        share = len(TILE_ROWS) // devices
        place = np.full(max(VIRTUAL, devices * length + 1), -1, np.int64)
        place[TILE_ROWS] = np.arange(len(TILE_ROWS))
        small_place = np.full(place.shape, -1, np.int64)
        small_place[SMALL_ROWS[SMALL_ROWS >= 0]] = np.flatnonzero(SMALL_ROWS >= 0)
        span = np.arange(devices)[:, None] * length + np.arange(length + 1)[None]
        relative = place[span] - np.arange(devices)[:, None] * share
        has = place[span] >= 0
        self.before = round_up(max(0, -relative[has].min()), TILE)
        self.after = round_up(max(0, relative[has].max() + 1 - share), TILE)
        smalls_at = self.before + share + self.after
        index = np.where(has, relative + self.before, -1)
        index = np.where(small_place[span] >= 0, small_place[span] + smalls_at, index)
        self.index = Owned.mine(index, me)
        self.at = me * length + lax.broadcasted_iota(jnp.int32, (length, 1), 0)
        self.devices = devices

    def __call__(self, owned, smalls):
        owned = owned.astype(jnp.bfloat16)
        share = owned.shape[0]
        around = halo(owned, self.before, self.after, self.devices, join=False)
        ends = self.before + share
        here = jnp.concatenate([owned, smalls.astype(jnp.bfloat16)], axis=0)
        index = self.index - self.before
        outside = (self.index < self.before) | ((self.index >= ends) & (self.index < ends + self.after))
        index = jnp.where(outside, -1, jnp.where(self.index >= ends, index - self.after, index))
        virtual = pick_rows(index, here)
        index = jnp.where(self.index < self.before, self.index, self.index - share)
        index = jnp.where(outside, index, -1)
        virtual = virtual + pick_rows(index, around)
        here, following = virtual[:-1], virtual[1:]
        lane = lax.broadcasted_iota(jnp.int32, (1, LANES), 1)
        shifted = jnp.concatenate([here[:, LANES - SHIFT :], following[:, : LANES - SHIFT]], axis=1)
        straight = (self.at < TABLE_END - 1) | ((self.at == TABLE_END - 1) & (lane < SHIFT))
        return jnp.where(straight, here, shifted).reshape(-1)


VECTOR_ROWS = D // LANES
FC1_AT = round_up(len(VECTORS) * VECTOR_ROWS, 8)
TABLE_AT = FC1_AT + FF // LANES
TABLE_ROWS = count_rows(SIZES["relative_table"])
LATER = 4


def table_entries(rows):
    table = rows[TABLE_AT : TABLE_AT + TABLE_ROWS].reshape(-1)[: RELS * HEADS].reshape(RELS, HEADS)
    return jnp.pad(table.T, ((0, 16 - HEADS), (0, ENTRY_LANES - RELS)))


def small_gradients(first, later, tables):
    tables = tables.reshape(2, RELS * HEADS)
    tables = jnp.pad(tables, ((0, 0), (0, round_up(TABLE_ROWS, 8) * LANES - RELS * HEADS))).reshape(2, -1, LANES)
    return jnp.concatenate([jnp.stack(first), jnp.stack(later), tables], axis=1)


SIDE = 2 * GRID - 1
WINDOW = round_up(SIDE * GRID, LANES) + LANES
WIDE = round_up(ROWS, LANES)


ENTRY_LANES = round_up(RELS, LANES)
HEAD_ROWS = 2 * 16


def entry_choice(column, transposed):
    shape = (1, WINDOW) if transposed else (WINDOW, 1)
    source = lax.broadcasted_iota(jnp.int32, shape, 1 if transposed else 0)
    group = source // GRID
    target = (SIDE - 1 - group) * SIDE - (source - group * GRID) + GRID - 1 + column
    target = jnp.where(source < SIDE * GRID, target, -1)
    entries = (ENTRY_LANES, 1) if transposed else (1, ENTRY_LANES)
    entry = lax.broadcasted_iota(jnp.int32, entries, 0 if transposed else 1)
    return (entry == target).astype(jnp.float32).astype(jnp.bfloat16)


def bias_kernel(entries_ref, bias_ref, windows_ref):
    for column in range(GRID):
        windows_ref[column] = product(entries_ref[...], entry_choice(column, True), NN)
    lane = lax.broadcasted_iota(jnp.int32, (1, WIDE), 1)
    inner = (lane >= 1) & (lane < SEQ)

    def head(i, _):
        ends = entries_ref[pl.ds(pl.multiple_of(i // 16 * 16, 16), 16), :].astype(jnp.float32)
        picked = lax.broadcasted_iota(jnp.int32, (16, 1), 0) == i % 16
        ends = jnp.sum(jnp.where(picked, ends, 0.0), axis=0, keepdims=True)
        top, left, corner = [ends[:, RELS - k : RELS - k + 1] for k in (3, 2, 1)]
        bias_ref[i] = jnp.zeros(bias_ref.shape[1:], jnp.float32)
        bias_ref[i, 0:1] = jnp.where(inner, top, jnp.where(lane == 0, corner, 0.0))[:, :ROWS]
        spread = jnp.concatenate([windows_ref[column, pl.ds(i, 1)] for column in range(GRID)], axis=0)
        for row in range(GRID):
            start = (GRID - 1 - row) * GRID
            window = pltpu.roll(spread, (1 - start) % WINDOW, 1)[:, :WIDE]
            window = jnp.where(inner, window, jnp.where(lane == 0, left, 0.0))
            bias_ref[i, 1 + row * GRID : 1 + (row + 1) * GRID] = window[:, :ROWS]
        return 0

    lax.fori_loop(0, HEADS, head, 0)


def bias_of(entries):
    return pl.pallas_call(
        bias_kernel,
        grid=(1,),
        in_specs=[pl.BlockSpec(entries.shape, lambda i: (0, 0))],
        out_specs=pl.BlockSpec((HEADS, ROWS, ROWS), lambda i: (0, 0, 0)),
        out_shape=jax.ShapeDtypeStruct((HEADS, ROWS, ROWS), jnp.float32),
        scratch_shapes=[pltpu.VMEM((GRID, 16, WINDOW), jnp.float32)],
        compiler_params=pltpu.CompilerParams(vmem_limit_bytes=VMEM_LIMIT),
        name="bias",
    )(entries)


def table_kernel(first_ref, second_ref, out_ref, windows_ref, ends_ref):
    lane = lax.broadcasted_iota(jnp.int32, (1, ROWS), 1)
    inner = (lane >= 1) & (lane < SEQ)
    entry = lax.broadcasted_iota(jnp.int32, (1, ENTRY_LANES), 1)
    windows_ref[...] = jnp.zeros_like(windows_ref)
    ends_ref[...] = jnp.zeros_like(ends_ref)
    for number, grad_ref in enumerate((first_ref, second_ref)):

        def head(i, _, number=number, grad_ref=grad_ref):
            total = jnp.zeros((GRID, WINDOW), jnp.float32)
            left = jnp.zeros((1, 1), jnp.float32)
            for row in range(GRID):
                start = (GRID - 1 - row) * GRID
                block = grad_ref[i, 1 + row * GRID : 1 + (row + 1) * GRID]
                left = left + jnp.sum(jnp.where(lane == 0, block, 0.0), keepdims=True)
                block = jnp.where(inner, block, 0.0)
                block = jnp.concatenate([block, jnp.zeros((GRID, WINDOW - ROWS), jnp.float32)], axis=1)
                total = total + pltpu.roll(block, (start - 1) % WINDOW, 1)
            at = pl.ds(number * 16 + i, 1)
            for column in range(GRID):
                windows_ref[column, at] = total[column : column + 1]
            first = grad_ref[i, 0:1]
            top = jnp.sum(jnp.where(inner, first, 0.0), keepdims=True)
            corner = jnp.sum(jnp.where(lane == 0, first, 0.0), keepdims=True)
            ends = jnp.where(entry == RELS - 3, top, jnp.where(entry == RELS - 2, left, 0.0))
            ends_ref[at] = jnp.where(entry == RELS - 1, corner, ends)
            return 0

        lax.fori_loop(0, HEADS, head, 0)
    out_ref[...] = ends_ref[...]
    for column in range(GRID):
        rows = windows_ref[column]
        high = rows.astype(jnp.bfloat16)
        low = (rows - high.astype(jnp.float32)).astype(jnp.bfloat16)
        chosen = entry_choice(column, False)
        out_ref[...] += product(high, chosen, NN) + product(low, chosen, NN)


def tables_from_biases(first, second):
    entries = pl.pallas_call(
        table_kernel,
        grid=(1,),
        in_specs=[pl.BlockSpec(first.shape, lambda i: (0, 0, 0))] * 2,
        out_specs=pl.BlockSpec((HEAD_ROWS, ENTRY_LANES), lambda i: (0, 0)),
        out_shape=jax.ShapeDtypeStruct((HEAD_ROWS, ENTRY_LANES), jnp.float32),
        scratch_shapes=[
            pltpu.VMEM((GRID, HEAD_ROWS, WINDOW), jnp.float32),
            pltpu.VMEM((HEAD_ROWS, ENTRY_LANES), jnp.float32),
        ],
        compiler_params=pltpu.CompilerParams(vmem_limit_bytes=VMEM_LIMIT),
        name="table_back",
    )(first, second)
    return entries.reshape(2, 16, ENTRY_LANES)[:, :HEADS, :RELS].transpose(0, 2, 1)


NT = (((1,), (1,)), ((), ()))
NN = (((1,), (0,)), ((), ()))
TN = (((0,), (0,)), ((), ()))


def product(left, right, dims):
    return lax.dot_general(left, right, dims, preferred_element_type=jnp.float32)


def own_lanes(head):
    lane = lax.broadcasted_iota(jnp.int32, (1, LANES), 1)
    return lane < HEAD if head == 0 else lane >= HEAD


def head_weights(query, key, bias, count, head):
    chosen = jnp.where(own_lanes(head), query, jnp.zeros_like(query))
    scores = product(chosen, key, NT) + bias
    column = lax.broadcasted_iota(jnp.int32, (1, ROWS), 1)
    scores = jnp.where(column < count, scores, NEGATIVE)
    grown = jnp.exp(scores - jnp.max(scores, axis=1, keepdims=True))
    return grown * (1.0 / jnp.sum(grown, axis=1, keepdims=True))


def attention_kernel(pairs, counts_ref, query_ref, key_ref, value_ref, bias_ref, out_ref):
    count = counts_ref[pl.program_id(1)]
    for pair in range(pairs):
        lanes = slice(pair * LANES, (pair + 1) * LANES)
        query, key, value = query_ref[:, lanes], key_ref[:, lanes], value_ref[:, lanes]
        parts = []
        for head in range(2):
            weights = head_weights(query, key, bias_ref[2 * pair + head], count, head)
            parts.append(product(weights.astype(jnp.bfloat16), value, NN))
        out_ref[:, lanes] = jnp.where(own_lanes(0), parts[0], parts[1]).astype(jnp.bfloat16)


def attention_back_kernel(pairs, counts_ref, query_ref, key_ref, value_ref, grad_ref, bias_ref, out_ref, db_ref):
    image = pl.program_id(1)
    count = counts_ref[image]

    @pl.when(image == 0)
    def _():
        db_ref[...] = jnp.zeros_like(db_ref)

    for pair in range(pairs):
        lanes = slice(pair * LANES, (pair + 1) * LANES)
        query, key, value, grad = query_ref[:, lanes], key_ref[:, lanes], value_ref[:, lanes], grad_ref[:, lanes]
        dq, dk, dv = [], [], []
        for head in range(2):
            weights = head_weights(query, key, bias_ref[2 * pair + head], count, head)
            chosen = jnp.where(own_lanes(head), grad, jnp.zeros_like(grad))
            weighted = weights * product(chosen, value, NT)
            dv.append(product(weights.astype(jnp.bfloat16), grad, TN))
            grad_scores = weighted - weights * jnp.sum(weighted, axis=1, keepdims=True)
            low = grad_scores.astype(jnp.bfloat16)
            dq.append(product(low, key, NN))
            dk.append(product(low, query, TN))
            db_ref[2 * pair + head] += grad_scores
        first = own_lanes(0)
        out_ref[0, :, lanes] = (jnp.where(first, dq[0], dq[1]) * HEAD**-0.5).astype(jnp.bfloat16)
        out_ref[1, :, lanes] = jnp.where(first, dk[0], dk[1]).astype(jnp.bfloat16)
        out_ref[2, :, lanes] = jnp.where(first, dv[0], dv[1]).astype(jnp.bfloat16)


def attention_specs(pairs):
    steps = D // LANES // pairs
    lanes = [
        pl.BlockSpec((ROWS, pairs * LANES), lambda step, image, counts, part=part: (image, part * steps + step))
        for part in range(3)
    ]
    bias = pl.BlockSpec((2 * pairs, ROWS, ROWS), lambda step, image, counts: (step, 0, 0))
    return steps, lanes, bias


def attention(counts, qkv, bias, pairs=6):
    steps, lanes, bias_spec = attention_specs(pairs)
    return pl.pallas_call(
        functools.partial(attention_kernel, pairs),
        grid_spec=pltpu.PrefetchScalarGridSpec(
            num_scalar_prefetch=1,
            grid=(steps, qkv.shape[0] // ROWS),
            in_specs=lanes + [bias_spec],
            out_specs=lanes[0],
        ),
        out_shape=jax.ShapeDtypeStruct((qkv.shape[0], D), jnp.bfloat16),
        compiler_params=pltpu.CompilerParams(vmem_limit_bytes=VMEM_LIMIT),
        name="attention",
    )(counts, qkv, qkv, qkv, bias)


def attention_back(counts, qkv, grad, bias, pairs=3):
    steps, lanes, bias_spec = attention_specs(pairs)
    return pl.pallas_call(
        functools.partial(attention_back_kernel, pairs),
        grid_spec=pltpu.PrefetchScalarGridSpec(
            num_scalar_prefetch=1,
            grid=(steps, qkv.shape[0] // ROWS),
            in_specs=lanes + [lanes[0], bias_spec],
            out_specs=[
                pl.BlockSpec((3, ROWS, pairs * LANES), lambda step, image, counts: (0, image, step)),
                bias_spec,
            ],
        ),
        out_shape=[
            jax.ShapeDtypeStruct((3, qkv.shape[0], D), jnp.bfloat16),
            jax.ShapeDtypeStruct((HEADS, ROWS, ROWS), jnp.float32),
        ],
        compiler_params=pltpu.CompilerParams(vmem_limit_bytes=VMEM_LIMIT),
        name="attention_back",
    )(counts, qkv, qkv, qkv, grad, bias)


def tile_starts():
    starts, at = {}, 0
    for name, (depth, width) in WEIGHTS.items():
        starts[name] = at
        at += depth // TILE * (width // LANES)
    return starts


FIRST = tile_starts()
MLP_FIRST = FIRST["proj_weight"]
SPAN = 1024


def load_weight(ref, base, name, row, rows, column, columns):
    first, across = FIRST[name] - base, WEIGHTS[name][1] // LANES
    lines = []
    for i in range(rows):
        at = first + (row + i) * across + column
        lines.append(jnp.concatenate([ref[at + j] for j in range(columns)], axis=1))
    return jnp.concatenate(lines, axis=0)


def gelu_and_slope(values):
    size = jnp.abs(values)
    step = 1.0 / (1.0 + (0.3275911 / math.sqrt(2.0)) * size)
    bell = jnp.exp(-0.5 * values * values)
    series = 1.061405429
    for term in (-1.453152027, 1.421413741, -0.284496736, 0.254829592):
        series = series * step + term
    tail = 0.5 * series * step * bell
    area = jnp.where(values < 0, tail, 1.0 - tail)
    return values * area, area + values * bell * (1.0 / math.sqrt(2.0 * math.pi))


def norm_parts(values):
    centre = values - jnp.mean(values, axis=-1, keepdims=True)
    spread = jnp.mean(centre * centre, axis=-1, keepdims=True)
    inverse = lax.rsqrt(spread + EPSILON)
    return centre * inverse, inverse


def norm_back(grad, normal, inverse, gain):
    scaled = grad * gain
    first = jnp.mean(scaled, axis=-1, keepdims=True)
    second = jnp.mean(scaled * normal, axis=-1, keepdims=True)
    return (scaled - first - normal * second) * inverse


def wide_row(ref, first, count):
    return jnp.concatenate([ref[first + i : first + i + 1] for i in range(count)], axis=1)


def vector(ref, name):
    return wide_row(ref, ROW[name] * VECTOR_ROWS, VECTOR_ROWS)


def put_vector(ref, row, values):
    sums = jnp.sum(values, axis=0, keepdims=True)
    for i in range(sums.shape[1] // LANES):
        ref[row + i : row + i + 1] = sums[:, i * LANES : (i + 1) * LANES]


def later_row(name):
    return (ROW[name] - LATER) * VECTOR_ROWS


def whole_spec(shape):
    return pl.BlockSpec(shape, lambda *_: (0,) * len(shape))


ANYWHERE = pl.BlockSpec(memory_space=pl.ANY)
PARAMS = pltpu.CompilerParams(vmem_limit_bytes=VMEM_LIMIT)


def low_like(*shape):
    return jax.ShapeDtypeStruct(shape, jnp.bfloat16)


def full_like(*shape):
    return jax.ShapeDtypeStruct(shape, jnp.float32)


def project_kernel(places, slots, at_ref, *refs):
    parts, refs = refs[: len(slots)], refs[len(slots) :]
    hidden_ref, vectors_ref, normed_ref, qkv_ref, tiles_ref, whole_ref, sems, out_sem = refs
    copies = copies_between(places, at_ref, parts, slots, whole_ref, sems, True)
    for copy in copies:
        copy.start()
    normal, _ = norm_parts(hidden_ref[...])
    normed_ref[...] = (normal * vector(vectors_ref, "norm1_gain") + vector(vectors_ref, "norm1_bias")).astype(
        jnp.bfloat16
    )
    for copy in copies:
        copy.wait()
    leaving = pltpu.make_async_copy(whole_ref, tiles_ref, out_sem)
    leaving.start()
    across = D // LANES
    for part in range(3):
        weight = load_weight(whole_ref, 0, "qkv_weight", 0, D // TILE, part * across, across)
        rows = product(normed_ref[...], weight, NN)
        if part == 0:
            rows = (rows + vector(vectors_ref, "query_bias")) * HEAD**-0.5
        if part == 2:
            rows = rows + vector(vectors_ref, "value_bias")
        qkv_ref[:, part * D : (part + 1) * D] = rows.astype(jnp.bfloat16)
    leaving.wait()


def project(places, position, parts, hidden, vectors):
    arrays = [array for array, _ in parts]
    slots = [listed for _, listed in parts]
    rows = hidden.shape[0]
    return pl.pallas_call(
        functools.partial(project_kernel, places, slots),
        grid_spec=pltpu.PrefetchScalarGridSpec(
            num_scalar_prefetch=1,
            grid=(1,),
            in_specs=[ANYWHERE] * len(arrays) + [whole_spec((rows, D)), whole_spec(vectors.shape)],
            out_specs=[whole_spec((rows, D)), whole_spec((rows, 3 * D)), ANYWHERE],
            scratch_shapes=[
                pltpu.VMEM((TILES, TILE, LANES), jnp.bfloat16),
                pltpu.SemaphoreType.DMA((sum(len(listed) for listed in slots),)),
                pltpu.SemaphoreType.DMA(()),
            ],
        ),
        out_shape=[low_like(rows, D), low_like(rows, 3 * D), low_like(TILES, TILE, LANES)],
        compiler_params=PARAMS,
        name="project",
    )(position, *arrays, hidden, vectors)


def mlp_weights(tiles_ref, weight_ref, sems, order):
    copies = []
    for i, name in enumerate(order):
        depth, width = WEIGHTS[name]
        count = depth // TILE * (width // LANES)
        here = weight_ref.at[pl.ds(FIRST[name] - MLP_FIRST, count)]
        copies.append(pltpu.make_async_copy(tiles_ref.at[pl.ds(FIRST[name], count)], here, sems.at[i]))
        copies[-1].start()
    return copies


def span_of(step):
    return pl.ds(pl.multiple_of(step * SPAN, SPAN), SPAN)


def mlp_kernel(
    attended_ref,
    hidden_ref,
    vectors_ref,
    tiles_ref,
    result_ref,
    branch_ref,
    middle_ref,
    normed_ref,
    activ_ref,
    slope_ref,
    mlp_ref,
    total_ref,
    weight_ref,
    sems,
    fc1_bias_ref,
):
    copies = mlp_weights(tiles_ref, weight_ref, sems, ("proj_weight", "fc1_weight", "fc2_weight"))
    fc1_bias_ref[...] = wide_row(vectors_ref, FC1_AT, FF // LANES)
    copies[0].wait()
    across = D // LANES
    weight = load_weight(weight_ref, MLP_FIRST, "proj_weight", 0, D // TILE, 0, across)
    branch = product(attended_ref[...], weight, NN) + vector(vectors_ref, "proj_bias")
    branch_ref[...] = branch.astype(jnp.bfloat16)
    middle_ref[...] = hidden_ref[...] + vector(vectors_ref, "gamma_attn") * branch
    normal, _ = norm_parts(middle_ref[...])
    normed_ref[...] = (normal * vector(vectors_ref, "norm2_gain") + vector(vectors_ref, "norm2_bias")).astype(
        jnp.bfloat16
    )
    total_ref[...] = jnp.broadcast_to(vector(vectors_ref, "fc2_bias"), total_ref.shape)
    copies[1].wait()
    copies[2].wait()

    def step(i, _):
        span = span_of(i)
        weight = load_weight(weight_ref, MLP_FIRST, "fc1_weight", 0, D // TILE, i * (SPAN // LANES), SPAN // LANES)
        activ, slope = gelu_and_slope(product(normed_ref[...], weight, NN) + fc1_bias_ref[:, span])
        activ = activ.astype(jnp.bfloat16)
        activ_ref[:, span] = activ
        slope_ref[:, span] = slope.astype(jnp.bfloat16)
        weight = load_weight(weight_ref, MLP_FIRST, "fc2_weight", i * (SPAN // TILE), SPAN // TILE, 0, across)
        total_ref[...] += product(activ, weight, NN)
        return 0

    lax.fori_loop(0, FF // SPAN, step, 0)
    mlp_ref[...] = total_ref[...].astype(jnp.bfloat16)
    result_ref[...] = middle_ref[...] + vector(vectors_ref, "gamma_mlp") * total_ref[...]


def mlp_scratch(rows):
    return [
        pltpu.VMEM((rows, D), jnp.float32),
        pltpu.VMEM((TILES - MLP_FIRST, TILE, LANES), jnp.bfloat16),
        pltpu.SemaphoreType.DMA((3,)),
    ]


def mlp(attended, hidden, vectors, tiles):
    rows = hidden.shape[0]
    outs = [full_like(rows, D), low_like(rows, D), full_like(rows, D), low_like(rows, D)]
    outs += [low_like(rows, FF), low_like(rows, FF), low_like(rows, D)]
    ins = [attended, hidden, vectors]
    return pl.pallas_call(
        mlp_kernel,
        grid=(1,),
        in_specs=[whole_spec(array.shape) for array in ins] + [ANYWHERE],
        out_specs=[whole_spec(out.shape) for out in outs],
        out_shape=outs,
        scratch_shapes=mlp_scratch(rows) + [pltpu.VMEM((1, FF), jnp.float32)],
        compiler_params=PARAMS,
        name="mlp",
    )(*ins, tiles)


def mlp_back_kernel(
    grad_ref,
    branch_ref,
    middle_ref,
    slope_ref,
    mlp_ref,
    vectors_ref,
    tiles_ref,
    grad_middle_ref,
    grad_attended_ref,
    grad_mlp_ref,
    grad_pre_ref,
    grad_branch_ref,
    sums_ref,
    total_ref,
    weight_ref,
    sems,
):
    copies = mlp_weights(tiles_ref, weight_ref, sems, ("fc2_weight", "fc1_weight", "proj_weight"))
    across = D // LANES
    grad = grad_ref[...]
    sums_ref[...] = jnp.zeros_like(sums_ref)
    put_vector(sums_ref, later_row("gamma_mlp"), grad * mlp_ref[...].astype(jnp.float32))
    grad_mlp = grad * vector(vectors_ref, "gamma_mlp")
    put_vector(sums_ref, later_row("fc2_bias"), grad_mlp)
    grad_mlp_ref[...] = grad_mlp.astype(jnp.bfloat16)
    total_ref[...] = jnp.zeros_like(total_ref)
    copies[0].wait()
    copies[1].wait()

    def step(i, _):
        span = span_of(i)
        weight = load_weight(weight_ref, MLP_FIRST, "fc2_weight", i * (SPAN // TILE), SPAN // TILE, 0, across)
        grad_pre = product(grad_mlp_ref[...], weight, NT) * slope_ref[:, span].astype(jnp.float32)
        sums = jnp.sum(grad_pre, axis=0, keepdims=True)
        sums = jnp.concatenate([sums[:, k * LANES : (k + 1) * LANES] for k in range(SPAN // LANES)], axis=0)
        first = FC1_AT - LATER * VECTOR_ROWS + i * (SPAN // LANES)
        sums_ref[pl.ds(pl.multiple_of(first, SPAN // LANES), SPAN // LANES)] = sums
        grad_pre = grad_pre.astype(jnp.bfloat16)
        grad_pre_ref[:, span] = grad_pre
        weight = load_weight(weight_ref, MLP_FIRST, "fc1_weight", 0, D // TILE, i * (SPAN // LANES), SPAN // LANES)
        total_ref[...] += product(grad_pre, weight, NT)
        return 0

    lax.fori_loop(0, FF // SPAN, step, 0)
    normal, inverse = norm_parts(middle_ref[...])
    grad_normed = total_ref[...]
    put_vector(sums_ref, later_row("norm2_gain"), grad_normed * normal)
    put_vector(sums_ref, later_row("norm2_bias"), grad_normed)
    grad_middle = grad_ref[...] + norm_back(grad_normed, normal, inverse, vector(vectors_ref, "norm2_gain"))
    grad_middle_ref[...] = grad_middle
    put_vector(sums_ref, later_row("gamma_attn"), grad_middle * branch_ref[...].astype(jnp.float32))
    grad_branch = grad_middle * vector(vectors_ref, "gamma_attn")
    put_vector(sums_ref, later_row("proj_bias"), grad_branch)
    grad_branch_ref[...] = grad_branch.astype(jnp.bfloat16)
    copies[2].wait()
    weight = load_weight(weight_ref, MLP_FIRST, "proj_weight", 0, D // TILE, 0, across)
    grad_attended_ref[...] = product(grad_branch_ref[...], weight, NT).astype(jnp.bfloat16)


def mlp_back(grad, saved, vectors, tiles):
    rows = grad.shape[0]
    outs = [full_like(rows, D), low_like(rows, D), low_like(rows, D), low_like(rows, FF), low_like(rows, D)]
    outs += [full_like(TABLE_AT - LATER * VECTOR_ROWS, LANES)]
    ins = [grad, saved["branch"], saved["middle"], saved["slope"], saved["mlp_out"], vectors]
    return pl.pallas_call(
        mlp_back_kernel,
        grid=(1,),
        in_specs=[whole_spec(array.shape) for array in ins] + [ANYWHERE],
        out_specs=[whole_spec(out.shape) for out in outs],
        out_shape=outs,
        scratch_shapes=mlp_scratch(rows),
        compiler_params=PARAMS,
        name="mlp_back",
    )(*ins, tiles)


def weight_back_kernel(places, slots, at_ref, *refs):
    normed_ref, project_ref, attended_ref, branch_ref, normed2_ref, pre_ref, activ_ref, mlp_ref = refs[:8]
    parts, (whole_ref, sems) = refs[8 : 8 + len(slots)], refs[8 + len(slots) :]
    across, count = D // LANES, 256 // TILE

    def put(name, row, column, left, grad):
        block = product(left, grad, TN).astype(jnp.bfloat16)
        wide = WEIGHTS[name][1] // LANES
        for i in range(count):
            for j in range(across):
                at = FIRST[name] + (row + i) * wide + column + j
                whole_ref[at] = block[i * TILE : (i + 1) * TILE, j * LANES : (j + 1) * LANES]

    def columns(i):
        return pl.ds(pl.multiple_of(i * 256, 256), 256)

    def narrow(i, _):
        for part in range(3):
            put("qkv_weight", i * count, part * across, normed_ref[:, columns(i)], project_ref[part])
        put("proj_weight", i * count, 0, attended_ref[:, columns(i)], branch_ref[...])
        for part in range(FF // D):
            grad = pre_ref[:, part * D : (part + 1) * D]
            put("fc1_weight", i * count, part * across, normed2_ref[:, columns(i)], grad)
        return 0

    def wide(i, _):
        put("fc2_weight", i * count, 0, activ_ref[:, columns(i)], mlp_ref[...])
        return 0

    lax.fori_loop(0, D // 256, narrow, 0)
    lax.fori_loop(0, FF // 256, wide, 0)
    copies = copies_between(places, at_ref, parts, slots, whole_ref, sems, False)
    for copy in copies:
        copy.start()
    for copy in copies:
        copy.wait()


def weight_back(places, position, slots, ins):
    count = TILES // sum(len(listed) for listed in slots)
    return pl.pallas_call(
        functools.partial(weight_back_kernel, places, slots),
        grid_spec=pltpu.PrefetchScalarGridSpec(
            num_scalar_prefetch=1,
            grid=(1,),
            in_specs=[whole_spec(array.shape) for array in ins],
            out_specs=[ANYWHERE] * len(slots),
            scratch_shapes=[
                pltpu.VMEM((TILES, TILE, LANES), jnp.bfloat16),
                pltpu.SemaphoreType.DMA((sum(len(listed) for listed in slots),)),
            ],
        ),
        out_shape=[low_like(len(listed) * count, TILE, LANES) for listed in slots],
        compiler_params=PARAMS,
        name="weight_back",
    )(position, *ins)


def input_back_kernel(project_ref, grad_middle_ref, hidden_ref, vectors_ref, tiles_ref, out_ref, sums_ref, total_ref):
    across = D // LANES
    for part in range(3):
        weight = load_weight(tiles_ref, 0, "qkv_weight", 0, D // TILE, part * across, across)
        rows = product(project_ref[part], weight, NT)
        total_ref[...] = rows if part == 0 else total_ref[...] + rows
    normal, inverse = norm_parts(hidden_ref[...])
    grad_normed = total_ref[...]
    put_vector(sums_ref, 0, grad_normed * normal)
    put_vector(sums_ref, VECTOR_ROWS, grad_normed)
    put_vector(sums_ref, 2 * VECTOR_ROWS, project_ref[0].astype(jnp.float32))
    put_vector(sums_ref, 3 * VECTOR_ROWS, project_ref[2].astype(jnp.float32))
    out_ref[...] = grad_middle_ref[...] + norm_back(
        grad_normed, normal, inverse, vector(vectors_ref, "norm1_gain")
    )


def input_back(grad_project, grad_middle, hidden, vectors, tiles):
    rows = hidden.shape[0]
    ins = [grad_project, grad_middle, hidden, vectors]
    return pl.pallas_call(
        input_back_kernel,
        grid=(1,),
        in_specs=[whole_spec(array.shape) for array in ins] + [whole_spec((MLP_FIRST, TILE, LANES))],
        out_specs=[whole_spec((rows, D)), whole_spec((LATER * VECTOR_ROWS, LANES))],
        out_shape=[full_like(rows, D), full_like(LATER * VECTOR_ROWS, LANES)],
        scratch_shapes=[pltpu.VMEM((rows, D), jnp.float32)],
        compiler_params=PARAMS,
        name="input_back",
    )(*ins, tiles)


def pad_rows(images):
    padded = jnp.pad(images, ((0, 0), (0, ROWS - SEQ), (0, 0)))
    return padded.reshape(-1, D).astype(jnp.float32)


def cut_rows(rows):
    return rows.reshape(-1, ROWS, D)[:, :SEQ].astype(jnp.bfloat16)


class Places:
    def __init__(self, dp, fsdp):
        low = 2 if dp % 2 == 0 else 1
        core = 2 if fsdp % 2 == 0 else 1
        self.sizes = {"y": low, "x": dp // low, "z": fsdp // core, "c": core}
        self.count = dp * fsdp
        grid = np.arange(self.count).reshape(tuple(self.sizes.values()))
        self.grid = grid
        self.axis = {name: i for i, name in enumerate(self.sizes)}

    def exchange(self, block, axis, hop):
        size = self.sizes[axis]
        target = np.take(self.grid, np.arange(size) ^ hop, axis=self.axis[axis])
        perm = [(int(a), int(b)) for a, b in zip(self.grid.reshape(-1), target.reshape(-1))]
        return lax.ppermute(block, AXES, perm)

    def hops(self, axis):
        return range(1, self.sizes[axis])

    def powers(self, axis):
        return [1 << bit for bit in range(self.sizes[axis].bit_length() - 1)]

    def total(self, block, axes):
        for axis in axes:
            for hop in self.powers(axis):
                block = block + self.exchange(block, axis, hop)
        return block

    def position(self, me):
        return jnp.stack([(me // int(np.prod(self.grid.shape[i + 1 :]))) % n for i, n in enumerate(self.grid.shape)])


def block_at(at_ref, places, offset):
    number = 0
    for i, size in enumerate(places.grid.shape):
        number = number * size + (at_ref[i] ^ offset[i])
    return number


def copies_between(places, at_ref, parts, slots, whole_ref, sems, inward):
    copies = []
    for part, listed in zip(parts, slots):
        count = part.shape[0] // len(listed)
        for i, slot in enumerate(listed):
            start = 0 if slot is None else block_at(at_ref, places, slot[0]) * (TILES // places.count) + slot[1]
            here, there = part.at[pl.ds(i * count, count)], whole_ref.at[pl.ds(start, count)]
            ends = (here, there) if inward else (there, here)
            copies.append(pltpu.make_async_copy(*ends, sems.at[len(copies)]))
    return copies


def offset_of(**hops):
    return tuple(hops.get(axis, 0) for axis in ("y", "x", "z", "c"))


def join(blocks):
    return jnp.concatenate(blocks, axis=0) if len(blocks) > 1 else blocks[0]


ORDERS = (("x", "y"), ("y", "x"))


def group_of(shares, offsets):
    half = shares[0].shape[0] // 2
    return [(join([share[part * half : (part + 1) * half] for share in shares]), offsets) for part in range(2)]


def merge(*groups):
    return [(join([group[part][0] for group in groups]), sum((group[part][1] for group in groups), [])) for part in range(2)]


def fetch_column(places, share):
    return [places.exchange(share, "z", hop) for hop in places.hops("z")]


def column_offsets(places):
    return [offset_of(z=hop) for hop in range(places.sizes["z"])]


def fetch_plane(places, group, step):
    arrived = []
    for (block, offsets), order in zip(group, ORDERS):
        at = places.axis[order[step]]
        hops = range(1, places.sizes[order[step]])
        moved = [offset[:at] + (hop,) + offset[at + 1 :] for hop in hops for offset in offsets]
        arrived.append((join([places.exchange(block, order[step], hop) for hop in hops]), moved))
    return arrived


def fetch_plane_with(places, group, step, rows):
    (block, offsets), order = group[0], ORDERS[0]
    count, axis = block.shape[0], order[step]
    hops = range(1, places.sizes[axis])
    arrived = [places.exchange(jnp.concatenate([block, rows], axis=0), axis, hop) for hop in hops]
    moved = [tuple(hop if i == places.axis[axis] else part for i, part in enumerate(o)) for hop in hops for o in offsets]
    rows = sum([piece[count:] for piece in arrived], rows)
    other = fetch_plane(places, group, step)[1]
    return [(join([piece[:count] for piece in arrived]), moved), other], rows


def list_core(places, groups):
    parts = []
    for group in groups:
        half = TILES // places.count // 2
        parts += [(block, [(offset, part * half) for offset in offsets]) for part, (block, offsets) in enumerate(group)]
    return parts


def gather_core(places, groups):
    parts = list_core(places, groups)
    return [(join([block for block, _ in parts]), sum((slots for _, slots in parts), []))]


def fetch_core(places, parts):
    arrived = []
    for hop in range(1, places.sizes["c"]):
        for block, slots in parts:
            moved = [(offset[:3] + (hop,), first) for offset, first in slots]
            arrived.append((places.exchange(block, "c", hop), moved))
    return parts + arrived


def add_low(*blocks):
    total = blocks[0].astype(jnp.float32)
    for block in blocks[1:]:
        total = total + block.astype(jnp.float32)
    return total


def scatter_slots(places):
    half = TILES // places.count // 2
    size = places.sizes
    slots = []
    for part, (first, second) in enumerate(ORDERS):
        for core in range(size["c"]):
            listed = []
            for one in range(size[first]):
                for two in range(size[second]):
                    for z in range(size["z"]):
                        listed.append((offset_of(**{first: one, second: two, "z": z, "c": core}), part * half))
            slots.append(listed)
    return slots


def send_core(places, parts):
    cores = places.sizes["c"]
    halves = [parts[:cores], parts[cores:]]
    return [[mine] + [places.exchange(other, "c", hop) for hop, other in enumerate(others, 1)] for mine, *others in halves]


def plane_totals(places, blocks, axis):
    share = blocks[0].shape[0] // places.sizes[axis]
    cuts = [slice(i * share, (i + 1) * share) for i in range(places.sizes[axis])]
    return [add_low(*[block[cut] for block in blocks]).astype(jnp.bfloat16) for cut in cuts]


def send_totals(places, totals, axis):
    return totals[:1] + [places.exchange(total, axis, hop) for hop, total in enumerate(totals[1:], 1)]


def send_plane(places, sums, step):
    axes = [order[step] for order in ORDERS]
    return [send_totals(places, plane_totals(places, blocks, axis), axis) for blocks, axis in zip(sums, axes)]


def send_plane_tied(places, sums, step, later):
    (first, second), axes = sums, [order[step] for order in ORDERS]
    first, later = tie(first, later)
    first = plane_totals(places, first, axes[0])
    second, first, later = tie(second, first, later)
    result = [send_totals(places, first, axes[0])]
    second, later = tie(plane_totals(places, second, axes[1]), later)
    return result + [send_totals(places, second, axes[1])], later


def column_totals(places, sums):
    count = places.sizes["z"]
    share = sums[0][0].shape[0] // count
    cuts = [slice(hop * share, (hop + 1) * share) for hop in range(count)]
    return [join([add_low(*[block[cut] for block in blocks]).astype(jnp.bfloat16) for blocks in sums]) for cut in cuts]


def send_column(places, totals):
    return [totals[0]] + [places.exchange(total, "z", hop) for hop, total in enumerate(totals[1:], 1)]


class Layer:
    def __init__(self, places, position, counts, vectors):
        self.places, self.position, self.counts, self.vectors = places, position, counts, vectors

    def project(self, hidden, parts):
        normed, qkv, tiles = project(self.places, self.position, parts, hidden, self.vectors)
        self.saved = dict(hidden=hidden, normed=normed, qkv=qkv, tiles=tiles)

    def forward(self):
        saved = self.saved
        saved["attended"] = attention(self.counts, saved["qkv"], self.bias)
        names = ("branch", "middle", "normed2", "activ", "slope", "mlp_out")
        result, *kept = mlp(saved["attended"], saved["hidden"], self.vectors, saved["tiles"])
        saved.update(zip(names, kept))
        return result

    def back_mlp(self, grad):
        return mlp_back(grad, self.saved, self.vectors, self.saved["tiles"])

    def back_attention(self, passed):
        return attention_back(self.counts, self.saved["qkv"], passed[1], self.bias)

    def back_weights(self, passed, grad_project, slots):
        _, _, grad_mlp, grad_pre, grad_branch, _ = passed
        saved = self.saved
        ins = [saved["normed"], grad_project, saved["attended"], grad_branch, saved["normed2"], grad_pre]
        return weight_back(self.places, self.position, slots, ins + [saved["activ"], grad_mlp])

    def back_input(self, passed, grad_project):
        return input_back(grad_project, passed[0], self.saved["hidden"], self.vectors, self.saved["tiles"])


def scatter_whole(parts):
    whole = parts[0].reshape(-1, LANES)
    return lax.psum_scatter(whole, AXES, scatter_dimension=0, tiled=True).astype(jnp.float32)


def local(dp, fsdp, tokens, counts, params_first, params_second, cotangent):
    devices = dp * fsdp
    places = Places(dp, fsdp)
    stepwise = TILES % (4 * devices) == 0 and all(size & (size - 1) == 0 for size in places.sizes.values())
    share_rows = TILES * TILE // devices
    me = lax.axis_index(AXES)
    position = places.position(me)
    owned = Owned([params_first, params_second], me, devices)
    own = owned.share(0)
    small_rows = owned.small_rows(own)
    hidden, grad_output = pad_rows(tokens), pad_rows(cotangent)

    if stepwise:
        own = own.reshape(-1, TILE, LANES)
        column = fetch_column(places, own)
        near, small_rows = tie(group_of([own], [offset_of()]), small_rows)
        small_rows = small_rows.reshape(-1, TILE, LANES)
        near_first, small_rows = fetch_plane_with(places, near, 0, small_rows)
        near_first, small_rows = tie(near_first, small_rows)
        near_second, small_rows = fetch_plane_with(places, merge(near, near_first), 1, small_rows)
        small_rows = places.total(small_rows, "c")
        next_own, near_first = tie(owned.share(1, own), near_first)
        far, near_second = tie(group_of(column, column_offsets(places)[1:]), near_second)
        far_first = fetch_plane(places, far, 0)
        next_own, small_rows, far, hidden, grad_output = tie(next_own, small_rows, far, hidden, grad_output)
        next_own = jnp.concatenate([next_own, small_rows.reshape(-1, LANES)], axis=0)
        next_shares = [next_own] + fetch_column(places, next_own)
        small_rows = sum([rows[share_rows:] for rows in next_shares[1:]], next_own[share_rows:])
        small_rows = small_rows.reshape(2, -1, LANES)
        vectors = small_rows.astype(jnp.float32)
        next_shares = [rows[:share_rows].reshape(-1, TILE, LANES) for rows in next_shares]
        group = group_of(next_shares, column_offsets(places))
        far_second = fetch_plane(places, merge(far, far_first), 1)
        early = gather_core(places, [near, near_first, near_second, far, far_first])
    else:
        small_rows = lax.psum(small_rows, AXES)
    if stepwise:
        far_second, early, group, small_rows, vectors = tie(far_second, early, group, small_rows, vectors)
        parts = fetch_core(places, early) + fetch_core(places, list_core(places, [far_second]))
        first = fetch_plane(places, group, 0)
        first_layer = Layer(places, position, counts, vectors[0])
        first_layer.bias = bias_of(table_entries(small_rows[0]))
        parts, first_layer.bias = tie(parts, first_layer.bias)
        first_layer.project(hidden, parts)
        first, group, first_layer.saved, small_rows = tie(first, group, first_layer.saved, small_rows)
        second = fetch_plane(places, merge(group, first), 1)
        next_parts = fetch_core(places, list_core(places, [first]))
        result = first_layer.forward()
        next_parts, result, small_rows = tie(next_parts, result, small_rows)
        second_bias = bias_of(table_entries(small_rows[1]))
        next_parts += fetch_core(places, gather_core(places, [group]))
        second, next_parts, result, second_bias = tie(second, next_parts, result, second_bias)
        next_parts += fetch_core(places, list_core(places, [second]))
    else:
        vectors = small_rows.astype(jnp.float32)
        second_bias = bias_of(table_entries(small_rows[1]))
        parts, next_parts = [
            [(lax.all_gather(share, AXES, axis=0, tiled=True).reshape(TILES, TILE, LANES), [None])]
            for share in (own, owned.share(1))
        ]
        first_layer = Layer(places, position, counts, vectors[0])
        first_layer.project(hidden, parts)
        first_layer.bias = bias_of(table_entries(small_rows[0]))
        result = first_layer.forward()
    second_layer = Layer(places, position, counts, vectors[1])
    second_layer.bias = second_bias
    second_layer.project(result, next_parts)
    result = second_layer.forward()
    output = cut_rows(result)

    slots = scatter_slots(places) if stepwise else [[None]]
    next_passed = second_layer.back_mlp(grad_output)
    next_project, next_bias = second_layer.back_attention(next_passed)
    parts = second_layer.back_weights(next_passed, next_project, slots)
    if stepwise:
        sums = send_core(places, parts)
    else:
        next_share = scatter_whole(parts)
    grad, next_sums = second_layer.back_input(next_passed, next_project)
    if stepwise:
        sums, grad = send_plane_tied(places, sums, 0, grad)
    passed = first_layer.back_mlp(grad)
    project_grad, bias = first_layer.back_attention(passed)
    if stepwise:
        sums, passed, project_grad = tie(sums, passed, project_grad)
        sums = send_plane(places, sums, 1)
    parts = first_layer.back_weights(passed, project_grad, slots)
    if stepwise:
        sums, parts, passed, project_grad = tie(sums, parts, passed, project_grad)
        own_sums = send_core(places, parts)
        totals = column_totals(places, sums)
        totals, passed, project_grad = tie(totals, passed, project_grad)
    else:
        share = scatter_whole(parts)
    grad, own_row_sums = first_layer.back_input(passed, project_grad)
    if stepwise:
        own_sums, grad, own_row_sums, bias, next_bias = tie(own_sums, grad, own_row_sums, bias, next_bias)
        own_sums, bias = send_plane_tied(places, own_sums, 0, bias)
        totals, bias = tie(totals, bias)
        sums = send_column(places, totals)
    small_grads = small_gradients(
        [own_row_sums, next_sums], [passed[5], next_passed[5]], tables_from_biases(bias, next_bias)
    )
    flat_share = FlatShare(me, devices, params_first.shape[0] * devices)
    if stepwise:
        own_sums, sums, small_grads = tie(own_sums, sums, small_grads)
        own_sums = send_plane(places, own_sums, 1)
        small_grads = places.total(small_grads, "zc")
        own_sums, small_grads = tie(own_sums, small_grads)
        own_sums = send_column(places, column_totals(places, own_sums))
        small_grads = places.total(small_grads, "xy")
        small_grads, sums = tie(small_grads, sums)
        grad_second = flat_share(add_low(*sums).reshape(-1, LANES), small_grads[1])
        own_sums, grad_second, output, grad_tokens = tie(own_sums, grad_second, output, cut_rows(grad))
        share = add_low(*own_sums).reshape(-1, LANES)
    else:
        small_grads = lax.psum(small_grads, AXES)
        grad_second = flat_share(next_share, small_grads[1])
        grad_tokens = cut_rows(grad)
    grad_first = flat_share(share, small_grads[0])
    return output, grad_tokens, grad_first, grad_second


def solution(mesh):
    return jax.shard_map(
        functools.partial(local, mesh.shape["dp"], mesh.shape["fsdp"]),
        mesh=mesh,
        in_specs=(P(AXES, None, None), P(AXES), P(AXES), P(AXES), P(AXES, None, None)),
        out_specs=(P(AXES, None, None), P(AXES, None, None), P(AXES), P(AXES)),
        check_vma=False,
    )
```

```python
import functools
import math

import jax
import jax.numpy as jnp
import numpy as np
from jax import lax
from jax.experimental import pallas as pl
from jax.experimental.pallas import tpu as pltpu
from jax.sharding import PartitionSpec as P

D = 768
HEADS = 12
HEAD = D // HEADS
FF = 3072
GRID = 14
SEQ = 197
RELS = 732
ROWS = 208
LANES = 128
TILE = 16
AXES = ("dp", "fsdp")
VMEM_LIMIT = 56 * 2**20

EPSILON = 1e-06
NEGATIVE = -1000000000.0

ENTRIES = [
    ("norm1_gain", (D,)),
    ("norm1_bias", (D,)),
    ("qkv_weight", (D, 3 * D)),
    ("query_bias", (D,)),
    ("value_bias", (D,)),
    ("relative_table", (RELS, HEADS)),
    ("proj_weight", (D, D)),
    ("proj_bias", (D,)),
    ("gamma_attn", (D,)),
    ("norm2_gain", (D,)),
    ("norm2_bias", (D,)),
    ("fc1_weight", (D, FF)),
    ("fc1_bias", (FF,)),
    ("fc2_weight", (FF, D)),
    ("fc2_bias", (D,)),
    ("gamma_mlp", (D,)),
]
WEIGHTS = {name: dims for name, dims in ENTRIES if name.endswith("weight")}
SIZES = dict(ENTRIES)
VECTORS = [
    "norm1_gain",
    "norm1_bias",
    "query_bias",
    "value_bias",
    "proj_bias",
    "gamma_attn",
    "norm2_gain",
    "norm2_bias",
    "fc2_bias",
    "gamma_mlp",
]
ROW = {name: i for i, name in enumerate(VECTORS)}


def count_rows(dims):
    return -(-math.prod(dims) // LANES)


def virtual_starts():
    starts, at = {}, 0
    for name, dims in ENTRIES:
        starts[name] = at
        at += count_rows(dims)
    return starts, at


STARTS, VIRTUAL = virtual_starts()
SHIFT = RELS * HEADS % LANES
TABLE_END = STARTS["proj_weight"]


def tile_order():
    parts = []
    for name, (depth, width) in WEIGHTS.items():
        across = width // LANES
        rows = STARTS[name] + np.arange(depth * across).reshape(depth // TILE, TILE, across)
        parts.append(rows.transpose(0, 2, 1).reshape(-1))
    return np.concatenate(parts)


def small_order():
    groups = [VECTORS, ["fc1_bias"], ["relative_table"]]
    rows = []
    for group in groups:
        for name in group:
            rows += [STARTS[name] + i for i in range(count_rows(SIZES[name]))]
        rows += [-1] * (-len(rows) % 8)
    return np.array(rows)


TILE_ROWS = tile_order()
SMALL_ROWS = small_order()
TILES = len(TILE_ROWS) // TILE


def tie(*trees):
    leaves, structure = jax.tree.flatten(trees)
    tied = iter(lax.optimization_barrier([leaf for leaf in leaves if isinstance(leaf, jax.Array)]))
    return structure.unflatten([next(tied) if isinstance(leaf, jax.Array) else leaf for leaf in leaves])


def halo(block, before, after, devices, join=True):
    rows = block.shape[-2]
    pieces = [block] if join else []
    for hop in range(1, -(-before // rows) + 1):
        take = min(rows, before - (hop - 1) * rows)
        perm = [(i, i + hop) for i in range(devices - hop)]
        pieces.insert(0, lax.ppermute(block[..., rows - take :, :], AXES, perm))
    for hop in range(1, -(-after // rows) + 1):
        take = min(rows, after - (hop - 1) * rows)
        perm = [(i + hop, i) for i in range(devices - hop)]
        pieces.append(lax.ppermute(block[..., :take, :], AXES, perm))
    return jnp.concatenate(pieces, axis=-2)


def pick_rows(index, source):
    chosen = index[:, None] == lax.broadcasted_iota(jnp.int32, (1, source.shape[0]), 1)
    return jnp.dot(chosen.astype(jnp.bfloat16), source.astype(jnp.bfloat16), preferred_element_type=jnp.float32)


def round_up(value, unit):
    return -(-value // unit) * unit


class Owned:
    def __init__(self, flats, me, devices):
        length = flats[0].shape[0] // LANES
        share = len(TILE_ROWS) // devices
        starts = np.arange(devices)[:, None] * length
        wanted = TILE_ROWS.reshape(devices, share) - starts
        before = round_up(max(0, -wanted.min()) + 1, TILE)
        after = round_up(max(0, wanted.max() + 1 - length), TILE)
        smalls = SMALL_ROWS[None] - starts
        smalls = np.where((smalls >= 0) & (smalls < length), smalls + before - 1, -1)
        self.wanted = self.mine(wanted + before - 1, me)
        self.smalls = self.mine(smalls, me)
        around = halo(jnp.stack([flat.reshape(length, LANES) for flat in flats]), before, after, devices)
        shifted = jnp.concatenate([around[:, :-1, SHIFT:], around[:, 1:, :SHIFT]], axis=2)
        at = me * length - before + 1 + lax.broadcasted_iota(jnp.int32, (1, shifted.shape[1], 1), 1)
        self.virtual = jnp.where(at < TABLE_END, around[:, 1:], shifted)

    @staticmethod
    def mine(table, me):
        return lax.dynamic_index_in_dim(jnp.asarray(table.astype(np.int32)), me, 0, keepdims=False)

    def small_rows(self, *after):
        virtual, *_ = tie(self.virtual, *after)
        return jnp.stack([pick_rows(self.smalls, rows).astype(jnp.bfloat16) for rows in virtual])

    def share(self, number, *after):
        rows = self.virtual[number]
        if after:
            rows, *_ = tie(rows, *after)
        return pick_rows(self.wanted, rows).astype(jnp.bfloat16)


class FlatShare:
    def __init__(self, me, devices, flat_length):
        length = flat_length // LANES // devices
        share = len(TILE_ROWS) // devices
        place = np.full(max(VIRTUAL, devices * length + 1), -1, np.int64)
        place[TILE_ROWS] = np.arange(len(TILE_ROWS))
        small_place = np.full(place.shape, -1, np.int64)
        small_place[SMALL_ROWS[SMALL_ROWS >= 0]] = np.flatnonzero(SMALL_ROWS >= 0)
        span = np.arange(devices)[:, None] * length + np.arange(length + 1)[None]
        relative = place[span] - np.arange(devices)[:, None] * share
        has = place[span] >= 0
        self.before = round_up(max(0, -relative[has].min()), TILE)
        self.after = round_up(max(0, relative[has].max() + 1 - share), TILE)
        smalls_at = self.before + share + self.after
        index = np.where(has, relative + self.before, -1)
        index = np.where(small_place[span] >= 0, small_place[span] + smalls_at, index)
        self.index = Owned.mine(index, me)
        self.at = me * length + lax.broadcasted_iota(jnp.int32, (length, 1), 0)
        self.devices = devices

    def __call__(self, owned, smalls):
        owned = owned.astype(jnp.bfloat16)
        share = owned.shape[0]
        around = halo(owned, self.before, self.after, self.devices, join=False)
        ends = self.before + share
        here = jnp.concatenate([owned, smalls.astype(jnp.bfloat16)], axis=0)
        index = self.index - self.before
        outside = (self.index < self.before) | ((self.index >= ends) & (self.index < ends + self.after))
        index = jnp.where(outside, -1, jnp.where(self.index >= ends, index - self.after, index))
        virtual = pick_rows(index, here)
        index = jnp.where(self.index < self.before, self.index, self.index - share)
        index = jnp.where(outside, index, -1)
        virtual = virtual + pick_rows(index, around)
        here, following = virtual[:-1], virtual[1:]
        lane = lax.broadcasted_iota(jnp.int32, (1, LANES), 1)
        shifted = jnp.concatenate([here[:, LANES - SHIFT :], following[:, : LANES - SHIFT]], axis=1)
        straight = (self.at < TABLE_END - 1) | ((self.at == TABLE_END - 1) & (lane < SHIFT))
        return jnp.where(straight, here, shifted).reshape(-1)


VECTOR_ROWS = D // LANES
FC1_AT = round_up(len(VECTORS) * VECTOR_ROWS, 8)
TABLE_AT = FC1_AT + FF // LANES
TABLE_ROWS = count_rows(SIZES["relative_table"])
LATER = 4


def table_entries(rows):
    tables = rows[:, TABLE_AT : TABLE_AT + TABLE_ROWS].reshape(2, -1)[:, : RELS * HEADS].reshape(2, RELS, HEADS)
    return jnp.pad(tables.transpose(0, 2, 1), ((0, 0), (0, 16 - HEADS), (0, ENTRY_LANES - RELS)))


def small_gradients(first, later, tables):
    tables = tables.reshape(2, RELS * HEADS)
    tables = jnp.pad(tables, ((0, 0), (0, round_up(TABLE_ROWS, 8) * LANES - RELS * HEADS))).reshape(2, -1, LANES)
    return jnp.concatenate([jnp.stack(first), jnp.stack(later), tables], axis=1)


SIDE = 2 * GRID - 1
WINDOW = round_up(SIDE * GRID, LANES) + LANES
WIDE = round_up(ROWS, LANES)


ENTRY_LANES = round_up(RELS, LANES)
HEAD_ROWS = 2 * 16


def entry_choice(column, transposed):
    shape = (1, WINDOW) if transposed else (WINDOW, 1)
    source = lax.broadcasted_iota(jnp.int32, shape, 1 if transposed else 0)
    group = source // GRID
    target = (SIDE - 1 - group) * SIDE - (source - group * GRID) + GRID - 1 + column
    target = jnp.where(source < SIDE * GRID, target, -1)
    entries = (ENTRY_LANES, 1) if transposed else (1, ENTRY_LANES)
    entry = lax.broadcasted_iota(jnp.int32, entries, 0 if transposed else 1)
    return (entry == target).astype(jnp.float32).astype(jnp.bfloat16)


def bias_kernel(entries_ref, bias_ref, windows_ref):
    for column in range(GRID):
        windows_ref[column] = product(entries_ref[...], entry_choice(column, True), NN)
    lane = lax.broadcasted_iota(jnp.int32, (1, WIDE), 1)
    inner = (lane >= 1) & (lane < SEQ)

    def head(i, _):
        ends = entries_ref[pl.ds(pl.multiple_of(i // 16 * 16, 16), 16), :].astype(jnp.float32)
        picked = lax.broadcasted_iota(jnp.int32, (16, 1), 0) == i % 16
        ends = jnp.sum(jnp.where(picked, ends, 0.0), axis=0, keepdims=True)
        top, left, corner = [ends[:, RELS - k : RELS - k + 1] for k in (3, 2, 1)]
        bias_ref[i] = jnp.zeros(bias_ref.shape[1:], jnp.float32)
        bias_ref[i, 0:1] = jnp.where(inner, top, jnp.where(lane == 0, corner, 0.0))[:, :ROWS]
        spread = jnp.concatenate([windows_ref[column, pl.ds(i, 1)] for column in range(GRID)], axis=0)
        for row in range(GRID):
            start = (GRID - 1 - row) * GRID
            window = pltpu.roll(spread, (1 - start) % WINDOW, 1)[:, :WIDE]
            window = jnp.where(inner, window, jnp.where(lane == 0, left, 0.0))
            bias_ref[i, 1 + row * GRID : 1 + (row + 1) * GRID] = window[:, :ROWS]
        return 0

    lax.fori_loop(0, HEADS, head, 0)


def bias_of(entries):
    return pl.pallas_call(
        bias_kernel,
        grid=(1,),
        in_specs=[pl.BlockSpec(entries.shape, lambda i: (0, 0))],
        out_specs=pl.BlockSpec((HEADS, ROWS, ROWS), lambda i: (0, 0, 0)),
        out_shape=jax.ShapeDtypeStruct((HEADS, ROWS, ROWS), jnp.float32),
        scratch_shapes=[pltpu.VMEM((GRID, 16, WINDOW), jnp.float32)],
        compiler_params=pltpu.CompilerParams(vmem_limit_bytes=VMEM_LIMIT),
        name="bias",
    )(entries)


def table_kernel(first_ref, second_ref, out_ref, windows_ref, ends_ref):
    lane = lax.broadcasted_iota(jnp.int32, (1, ROWS), 1)
    inner = (lane >= 1) & (lane < SEQ)
    entry = lax.broadcasted_iota(jnp.int32, (1, ENTRY_LANES), 1)
    windows_ref[...] = jnp.zeros_like(windows_ref)
    ends_ref[...] = jnp.zeros_like(ends_ref)
    for number, grad_ref in enumerate((first_ref, second_ref)):

        def head(i, _, number=number, grad_ref=grad_ref):
            total = jnp.zeros((GRID, WINDOW), jnp.float32)
            left = jnp.zeros((1, 1), jnp.float32)
            for row in range(GRID):
                start = (GRID - 1 - row) * GRID
                block = grad_ref[i, 1 + row * GRID : 1 + (row + 1) * GRID]
                left = left + jnp.sum(jnp.where(lane == 0, block, 0.0), keepdims=True)
                block = jnp.where(inner, block, 0.0)
                block = jnp.concatenate([block, jnp.zeros((GRID, WINDOW - ROWS), jnp.float32)], axis=1)
                total = total + pltpu.roll(block, (start - 1) % WINDOW, 1)
            at = pl.ds(number * 16 + i, 1)
            for column in range(GRID):
                windows_ref[column, at] = total[column : column + 1]
            first = grad_ref[i, 0:1]
            top = jnp.sum(jnp.where(inner, first, 0.0), keepdims=True)
            corner = jnp.sum(jnp.where(lane == 0, first, 0.0), keepdims=True)
            ends = jnp.where(entry == RELS - 3, top, jnp.where(entry == RELS - 2, left, 0.0))
            ends_ref[at] = jnp.where(entry == RELS - 1, corner, ends)
            return 0

        lax.fori_loop(0, HEADS, head, 0)
    out_ref[...] = ends_ref[...]
    for column in range(GRID):
        rows = windows_ref[column]
        high = rows.astype(jnp.bfloat16)
        low = (rows - high.astype(jnp.float32)).astype(jnp.bfloat16)
        chosen = entry_choice(column, False)
        out_ref[...] += product(high, chosen, NN) + product(low, chosen, NN)


def tables_from_biases(first, second):
    entries = pl.pallas_call(
        table_kernel,
        grid=(1,),
        in_specs=[pl.BlockSpec(first.shape, lambda i: (0, 0, 0))] * 2,
        out_specs=pl.BlockSpec((HEAD_ROWS, ENTRY_LANES), lambda i: (0, 0)),
        out_shape=jax.ShapeDtypeStruct((HEAD_ROWS, ENTRY_LANES), jnp.float32),
        scratch_shapes=[
            pltpu.VMEM((GRID, HEAD_ROWS, WINDOW), jnp.float32),
            pltpu.VMEM((HEAD_ROWS, ENTRY_LANES), jnp.float32),
        ],
        compiler_params=pltpu.CompilerParams(vmem_limit_bytes=VMEM_LIMIT),
        name="table_back",
    )(first, second)
    return entries.reshape(2, 16, ENTRY_LANES)[:, :HEADS, :RELS].transpose(0, 2, 1)


NT = (((1,), (1,)), ((), ()))
NN = (((1,), (0,)), ((), ()))
TN = (((0,), (0,)), ((), ()))


def product(left, right, dims):
    return lax.dot_general(left, right, dims, preferred_element_type=jnp.float32)


def own_lanes(head):
    lane = lax.broadcasted_iota(jnp.int32, (1, LANES), 1)
    return lane < HEAD if head == 0 else lane >= HEAD


def head_weights(query, key, bias, count, head):
    chosen = jnp.where(own_lanes(head), query, jnp.zeros_like(query))
    scores = product(chosen, key, NT) + bias
    column = lax.broadcasted_iota(jnp.int32, (1, ROWS), 1)
    scores = jnp.where(column < count, scores, NEGATIVE)
    grown = jnp.exp(scores - jnp.max(scores, axis=1, keepdims=True))
    return grown * (1.0 / jnp.sum(grown, axis=1, keepdims=True))


def attention_kernel(pairs, counts_ref, query_ref, key_ref, value_ref, bias_ref, out_ref, weights_ref):
    count = counts_ref[pl.program_id(1)]
    for pair in range(pairs):
        lanes = slice(pair * LANES, (pair + 1) * LANES)
        query, key, value = query_ref[:, lanes], key_ref[:, lanes], value_ref[:, lanes]
        parts = []
        for head in range(2):
            weights = head_weights(query, key, bias_ref[2 * pair + head], count, head).astype(jnp.bfloat16)
            weights_ref[0, 2 * pair + head] = weights
            parts.append(product(weights, value, NN))
        out_ref[:, lanes] = jnp.where(own_lanes(0), parts[0], parts[1]).astype(jnp.bfloat16)


def attention_back_kernel(pairs, query_ref, key_ref, value_ref, grad_ref, weights_ref, out_ref, db_ref):
    image = pl.program_id(1)

    @pl.when(image == 0)
    def _():
        db_ref[...] = jnp.zeros_like(db_ref)

    for pair in range(pairs):
        lanes = slice(pair * LANES, (pair + 1) * LANES)
        query, key, value, grad = query_ref[:, lanes], key_ref[:, lanes], value_ref[:, lanes], grad_ref[:, lanes]
        dq, dk, dv = [], [], []
        for head in range(2):
            low_weights = weights_ref[0, 2 * pair + head]
            weights = low_weights.astype(jnp.float32)
            chosen = jnp.where(own_lanes(head), grad, jnp.zeros_like(grad))
            weighted = weights * product(chosen, value, NT)
            dv.append(product(low_weights, grad, TN))
            grad_scores = weighted - weights * jnp.sum(weighted, axis=1, keepdims=True)
            low = grad_scores.astype(jnp.bfloat16)
            dq.append(product(low, key, NN))
            dk.append(product(low, query, TN))
            db_ref[2 * pair + head] += grad_scores
        first = own_lanes(0)
        out_ref[0, :, lanes] = (jnp.where(first, dq[0], dq[1]) * HEAD**-0.5).astype(jnp.bfloat16)
        out_ref[1, :, lanes] = jnp.where(first, dk[0], dk[1]).astype(jnp.bfloat16)
        out_ref[2, :, lanes] = jnp.where(first, dv[0], dv[1]).astype(jnp.bfloat16)


def attention_specs(pairs):
    steps = D // LANES // pairs
    lanes = [
        pl.BlockSpec((ROWS, pairs * LANES), lambda step, image, *_, part=part: (image, part * steps + step))
        for part in range(3)
    ]
    bias = pl.BlockSpec((2 * pairs, ROWS, ROWS), lambda step, image, *_: (step, 0, 0))
    weights = pl.BlockSpec((1, 2 * pairs, ROWS, ROWS), lambda step, image, *_: (image, step, 0, 0))
    return steps, lanes, bias, weights


def attention(counts, qkv, bias, pairs=6):
    images = qkv.shape[0] // ROWS
    steps, lanes, bias_spec, weights_spec = attention_specs(pairs)
    return pl.pallas_call(
        functools.partial(attention_kernel, pairs),
        grid_spec=pltpu.PrefetchScalarGridSpec(
            num_scalar_prefetch=1,
            grid=(steps, images),
            in_specs=lanes + [bias_spec],
            out_specs=[lanes[0], weights_spec],
        ),
        out_shape=[
            jax.ShapeDtypeStruct((qkv.shape[0], D), jnp.bfloat16),
            jax.ShapeDtypeStruct((images, HEADS, ROWS, ROWS), jnp.bfloat16),
        ],
        compiler_params=pltpu.CompilerParams(vmem_limit_bytes=VMEM_LIMIT),
        name="attention",
    )(counts, qkv, qkv, qkv, bias)


def attention_back(qkv, grad, weights, pairs=3):
    images = qkv.shape[0] // ROWS
    steps, lanes, bias_spec, weights_spec = attention_specs(pairs)
    return pl.pallas_call(
        functools.partial(attention_back_kernel, pairs),
        grid=(steps, images),
        in_specs=lanes + [lanes[0], weights_spec],
        out_specs=[
            pl.BlockSpec((3, ROWS, pairs * LANES), lambda step, image: (0, image, step)),
            bias_spec,
        ],
        out_shape=[
            jax.ShapeDtypeStruct((3, qkv.shape[0], D), jnp.bfloat16),
            jax.ShapeDtypeStruct((HEADS, ROWS, ROWS), jnp.float32),
        ],
        compiler_params=pltpu.CompilerParams(vmem_limit_bytes=VMEM_LIMIT),
        name="attention_back",
    )(qkv, qkv, qkv, grad, weights)


def tile_starts():
    starts, at = {}, 0
    for name, (depth, width) in WEIGHTS.items():
        starts[name] = at
        at += depth // TILE * (width // LANES)
    return starts


FIRST = tile_starts()
MLP_FIRST = FIRST["proj_weight"]
SPAN = 1024


def load_weight(ref, base, name, row, rows, column, columns):
    first, across = FIRST[name] - base, WEIGHTS[name][1] // LANES
    lines = []
    for i in range(rows):
        at = first + (row + i) * across + column
        lines.append(jnp.concatenate([ref[at + j] for j in range(columns)], axis=1))
    return jnp.concatenate(lines, axis=0)


def gelu_and_slope(values):
    size = jnp.abs(values)
    step = 1.0 / (1.0 + (0.3275911 / math.sqrt(2.0)) * size)
    bell = jnp.exp(-0.5 * values * values)
    series = 1.061405429
    for term in (-1.453152027, 1.421413741, -0.284496736, 0.254829592):
        series = series * step + term
    tail = 0.5 * series * step * bell
    area = jnp.where(values < 0, tail, 1.0 - tail)
    return values * area, area + values * bell * (1.0 / math.sqrt(2.0 * math.pi))


def norm_parts(values):
    centre = values - jnp.mean(values, axis=-1, keepdims=True)
    spread = jnp.mean(centre * centre, axis=-1, keepdims=True)
    inverse = lax.rsqrt(spread + EPSILON)
    return centre * inverse, inverse


def norm_back(grad, normal, inverse, gain):
    scaled = grad * gain
    first = jnp.mean(scaled, axis=-1, keepdims=True)
    second = jnp.mean(scaled * normal, axis=-1, keepdims=True)
    return (scaled - first - normal * second) * inverse


def wide_row(ref, first, count):
    return jnp.concatenate([ref[first + i : first + i + 1] for i in range(count)], axis=1)


def vector(ref, name):
    return wide_row(ref, ROW[name] * VECTOR_ROWS, VECTOR_ROWS)


def put_vector(ref, row, values):
    sums = jnp.sum(values, axis=0, keepdims=True)
    for i in range(sums.shape[1] // LANES):
        ref[row + i : row + i + 1] = sums[:, i * LANES : (i + 1) * LANES]


def later_row(name):
    return (ROW[name] - LATER) * VECTOR_ROWS


def whole_spec(shape):
    return pl.BlockSpec(shape, lambda *_: (0,) * len(shape))


ANYWHERE = pl.BlockSpec(memory_space=pl.ANY)
PARAMS = pltpu.CompilerParams(vmem_limit_bytes=VMEM_LIMIT)


def low_like(*shape):
    return jax.ShapeDtypeStruct(shape, jnp.bfloat16)


def full_like(*shape):
    return jax.ShapeDtypeStruct(shape, jnp.float32)


def project_kernel(places, slots, at_ref, *refs):
    parts, refs = refs[: len(slots)], refs[len(slots) :]
    hidden_ref, vectors_ref, normed_ref, qkv_ref, tiles_ref, whole_ref, sems, out_sem = refs
    copies = copies_in(places, at_ref, parts, slots, whole_ref, sems)
    for copy in copies:
        copy.start()
    normal, _ = norm_parts(hidden_ref[...])
    normed_ref[...] = (normal * vector(vectors_ref, "norm1_gain") + vector(vectors_ref, "norm1_bias")).astype(
        jnp.bfloat16
    )
    for copy in copies:
        copy.wait()
    leaving = pltpu.make_async_copy(whole_ref, tiles_ref, out_sem)
    leaving.start()
    across = D // LANES
    for part in range(3):
        weight = load_weight(whole_ref, 0, "qkv_weight", 0, D // TILE, part * across, across)
        rows = product(normed_ref[...], weight, NN)
        if part == 0:
            rows = (rows + vector(vectors_ref, "query_bias")) * HEAD**-0.5
        if part == 2:
            rows = rows + vector(vectors_ref, "value_bias")
        qkv_ref[:, part * D : (part + 1) * D] = rows.astype(jnp.bfloat16)
    leaving.wait()


def project(places, position, parts, hidden, vectors):
    arrays = [array for array, _ in parts]
    slots = [listed for _, listed in parts]
    rows = hidden.shape[0]
    return pl.pallas_call(
        functools.partial(project_kernel, places, slots),
        grid_spec=pltpu.PrefetchScalarGridSpec(
            num_scalar_prefetch=1,
            grid=(1,),
            in_specs=[ANYWHERE] * len(arrays) + [whole_spec((rows, D)), whole_spec(vectors.shape)],
            out_specs=[whole_spec((rows, D)), whole_spec((rows, 3 * D)), ANYWHERE],
            scratch_shapes=[
                pltpu.VMEM((TILES, TILE, LANES), jnp.bfloat16),
                pltpu.SemaphoreType.DMA((sum(len(listed) for listed in slots),)),
                pltpu.SemaphoreType.DMA(()),
            ],
        ),
        out_shape=[low_like(rows, D), low_like(rows, 3 * D), low_like(TILES, TILE, LANES)],
        compiler_params=PARAMS,
        name="project",
    )(position, *arrays, hidden, vectors)


def mlp_weights(tiles_ref, weight_ref, sems, order):
    copies = []
    for i, name in enumerate(order):
        depth, width = WEIGHTS[name]
        count = depth // TILE * (width // LANES)
        here = weight_ref.at[pl.ds(FIRST[name] - MLP_FIRST, count)]
        copies.append(pltpu.make_async_copy(tiles_ref.at[pl.ds(FIRST[name], count)], here, sems.at[i]))
        copies[-1].start()
    return copies


def span_of(step):
    return slice(step * SPAN, (step + 1) * SPAN)


def mlp_kernel(
    attended_ref,
    hidden_ref,
    vectors_ref,
    tiles_ref,
    result_ref,
    branch_ref,
    middle_ref,
    normed_ref,
    activ_ref,
    slope_ref,
    mlp_ref,
    total_ref,
    weight_ref,
    sems,
    fc1_bias_ref,
):
    copies = mlp_weights(tiles_ref, weight_ref, sems, ("proj_weight", "fc1_weight", "fc2_weight"))
    fc1_bias_ref[...] = wide_row(vectors_ref, FC1_AT, FF // LANES)
    copies[0].wait()
    across = D // LANES
    weight = load_weight(weight_ref, MLP_FIRST, "proj_weight", 0, D // TILE, 0, across)
    branch = product(attended_ref[...], weight, NN) + vector(vectors_ref, "proj_bias")
    branch_ref[...] = branch.astype(jnp.bfloat16)
    middle_ref[...] = hidden_ref[...] + vector(vectors_ref, "gamma_attn") * branch
    normal, _ = norm_parts(middle_ref[...])
    normed_ref[...] = (normal * vector(vectors_ref, "norm2_gain") + vector(vectors_ref, "norm2_bias")).astype(
        jnp.bfloat16
    )
    total_ref[...] = jnp.broadcast_to(vector(vectors_ref, "fc2_bias"), total_ref.shape)
    copies[1].wait()

    def step(i, _):
        span = span_of(i)
        weight = load_weight(weight_ref, MLP_FIRST, "fc1_weight", 0, D // TILE, i * (SPAN // LANES), SPAN // LANES)
        activ, slope = gelu_and_slope(product(normed_ref[...], weight, NN) + fc1_bias_ref[:, span])
        activ = activ.astype(jnp.bfloat16)
        activ_ref[:, span] = activ
        slope_ref[:, span] = slope.astype(jnp.bfloat16)
        if i == 0:
            copies[2].wait()
        weight = load_weight(weight_ref, MLP_FIRST, "fc2_weight", i * (SPAN // TILE), SPAN // TILE, 0, across)
        total_ref[...] += product(activ, weight, NN)
        return 0

    for i in range(FF // SPAN):
        step(i, 0)
    mlp_ref[...] = total_ref[...].astype(jnp.bfloat16)
    result_ref[...] = middle_ref[...] + vector(vectors_ref, "gamma_mlp") * total_ref[...]


def mlp_scratch(rows):
    return [
        pltpu.VMEM((rows, D), jnp.float32),
        pltpu.VMEM((TILES - MLP_FIRST, TILE, LANES), jnp.bfloat16),
        pltpu.SemaphoreType.DMA((3,)),
    ]


def mlp(attended, hidden, vectors, tiles):
    rows = hidden.shape[0]
    outs = [full_like(rows, D), low_like(rows, D), full_like(rows, D), low_like(rows, D)]
    outs += [low_like(rows, FF), low_like(rows, FF), low_like(rows, D)]
    ins = [attended, hidden, vectors]
    return pl.pallas_call(
        mlp_kernel,
        grid=(1,),
        in_specs=[whole_spec(array.shape) for array in ins] + [ANYWHERE],
        out_specs=[whole_spec(out.shape) for out in outs],
        out_shape=outs,
        scratch_shapes=mlp_scratch(rows) + [pltpu.VMEM((1, FF), jnp.float32)],
        compiler_params=PARAMS,
        name="mlp",
    )(*ins, tiles)


def mlp_back_kernel(
    grad_ref,
    branch_ref,
    middle_ref,
    slope_ref,
    mlp_ref,
    vectors_ref,
    tiles_ref,
    grad_middle_ref,
    grad_attended_ref,
    grad_mlp_ref,
    grad_pre_ref,
    grad_branch_ref,
    sums_ref,
    total_ref,
    weight_ref,
    sems,
):
    copies = mlp_weights(tiles_ref, weight_ref, sems, ("fc2_weight", "fc1_weight", "proj_weight"))
    across = D // LANES
    grad = grad_ref[...]
    sums_ref[...] = jnp.zeros_like(sums_ref)
    put_vector(sums_ref, later_row("gamma_mlp"), grad * mlp_ref[...].astype(jnp.float32))
    grad_mlp = grad * vector(vectors_ref, "gamma_mlp")
    put_vector(sums_ref, later_row("fc2_bias"), grad_mlp)
    grad_mlp_ref[...] = grad_mlp.astype(jnp.bfloat16)
    total_ref[...] = jnp.zeros_like(total_ref)
    copies[0].wait()

    def step(i, _):
        span = span_of(i)
        weight = load_weight(weight_ref, MLP_FIRST, "fc2_weight", i * (SPAN // TILE), SPAN // TILE, 0, across)
        grad_pre = product(grad_mlp_ref[...], weight, NT) * slope_ref[:, span].astype(jnp.float32)
        sums = jnp.sum(grad_pre, axis=0, keepdims=True)
        sums = jnp.concatenate([sums[:, k * LANES : (k + 1) * LANES] for k in range(SPAN // LANES)], axis=0)
        first = FC1_AT - LATER * VECTOR_ROWS + i * (SPAN // LANES)
        sums_ref[first : first + SPAN // LANES] = sums
        grad_pre = grad_pre.astype(jnp.bfloat16)
        grad_pre_ref[:, span] = grad_pre
        if i == 0:
            copies[1].wait()
        weight = load_weight(weight_ref, MLP_FIRST, "fc1_weight", 0, D // TILE, i * (SPAN // LANES), SPAN // LANES)
        total_ref[...] += product(grad_pre, weight, NT)
        return 0

    for i in range(FF // SPAN):
        step(i, 0)
    normal, inverse = norm_parts(middle_ref[...])
    grad_normed = total_ref[...]
    put_vector(sums_ref, later_row("norm2_gain"), grad_normed * normal)
    put_vector(sums_ref, later_row("norm2_bias"), grad_normed)
    grad_middle = grad_ref[...] + norm_back(grad_normed, normal, inverse, vector(vectors_ref, "norm2_gain"))
    grad_middle_ref[...] = grad_middle
    put_vector(sums_ref, later_row("gamma_attn"), grad_middle * branch_ref[...].astype(jnp.float32))
    grad_branch = grad_middle * vector(vectors_ref, "gamma_attn")
    put_vector(sums_ref, later_row("proj_bias"), grad_branch)
    grad_branch_ref[...] = grad_branch.astype(jnp.bfloat16)
    copies[2].wait()
    weight = load_weight(weight_ref, MLP_FIRST, "proj_weight", 0, D // TILE, 0, across)
    grad_attended_ref[...] = product(grad_branch_ref[...], weight, NT).astype(jnp.bfloat16)


def mlp_back(grad, saved, vectors, tiles):
    rows = grad.shape[0]
    outs = [full_like(rows, D), low_like(rows, D), low_like(rows, D), low_like(rows, FF), low_like(rows, D)]
    outs += [full_like(TABLE_AT - LATER * VECTOR_ROWS, LANES)]
    ins = [grad, saved["branch"], saved["middle"], saved["slope"], saved["mlp_out"], vectors]
    return pl.pallas_call(
        mlp_back_kernel,
        grid=(1,),
        in_specs=[whole_spec(array.shape) for array in ins] + [ANYWHERE],
        out_specs=[whole_spec(out.shape) for out in outs],
        out_shape=outs,
        scratch_shapes=mlp_scratch(rows),
        compiler_params=PARAMS,
        name="mlp_back",
    )(*ins, tiles)


def scatter_place(places, at_ref, device, part):
    position = np.unravel_index(device, places.grid.shape)
    apart = {name: at_ref[i] ^ int(position[i]) for name, i in places.axis.items()}
    first, second = ORDERS[part]
    slot = (apart[first] * places.sizes[second] + apart[second]) * places.sizes["z"] + apart["z"]
    return apart["c"], slot


def weight_back_kernel(places, stepwise, at_ref, *refs):
    sources, refs = refs[:8], refs[8:]
    outs = refs[: 2 * places.sizes["c"] if stepwise else 1]
    operands, (whole_ref, in_sems, sems) = refs[len(outs) : len(outs) + 8], refs[len(outs) + 8 :]
    coming = [
        pltpu.make_async_copy(source, operand, in_sems.at[i]) for i, (source, operand) in enumerate(zip(sources, operands))
    ]
    for copy in coming:
        copy.start()
    normed_ref, project_ref, attended_ref, branch_ref, normed2_ref, pre_ref, activ_ref, mlp_ref = operands
    across = D // LANES

    def put(name, row, column, left, grad):
        block = product(left, grad, TN).astype(jnp.bfloat16)
        wide = WEIGHTS[name][1] // LANES
        for i in range(D // TILE):
            for j in range(across):
                at = FIRST[name] + (row + i) * wide + column + j
                whole_ref[at] = block[i * TILE : (i + 1) * TILE, j * LANES : (j + 1) * LANES]

    half = TILES // places.count // 2
    sent = []

    def send(ready):
        while stepwise and (len(sent) + 1) * half <= ready:
            number = len(sent)
            core, slot = scatter_place(places, at_ref, number // 2, number % 2)
            source = whole_ref.at[pl.ds(number * half, half)]
            for k in range(places.sizes["c"]):
                target = outs[number % 2 * places.sizes["c"] + k].at[pl.ds(slot * half, half)]
                copy = pltpu.make_async_copy(source, target, sems.at[number])
                pl.when(core == k)(copy.start)
            sent.append(copy)

    coming[0].wait()
    coming[1].wait()
    for part in range(3):
        put("qkv_weight", 0, part * across, normed_ref[...], project_ref[part])
    send(FIRST["proj_weight"])
    coming[2].wait()
    coming[3].wait()
    put("proj_weight", 0, 0, attended_ref[...], branch_ref[...])
    send(FIRST["fc1_weight"])
    coming[4].wait()
    coming[5].wait()
    for part in range(FF // D):
        put("fc1_weight", 0, part * across, normed2_ref[...], pre_ref[:, part * D : (part + 1) * D])
    send(FIRST["fc2_weight"])
    coming[6].wait()
    coming[7].wait()
    for part in range(FF // D):
        put("fc2_weight", part * (D // TILE), 0, activ_ref[:, part * D : (part + 1) * D], mlp_ref[...])
        send(FIRST["fc2_weight"] + (part + 1) * (D // TILE) * across)
    if not stepwise:
        sent.append(pltpu.make_async_copy(whole_ref, outs[0], sems.at[0]))
        sent[0].start()
    for copy in sent:
        copy.wait()


def weight_back(places, position, stepwise, ins):
    cores = places.sizes["c"]
    counts = [TILES // (2 * cores)] * (2 * cores) if stepwise else [TILES]
    return pl.pallas_call(
        functools.partial(weight_back_kernel, places, stepwise),
        grid_spec=pltpu.PrefetchScalarGridSpec(
            num_scalar_prefetch=1,
            grid=(1,),
            in_specs=[ANYWHERE] * len(ins),
            out_specs=[ANYWHERE] * len(counts),
            scratch_shapes=[pltpu.VMEM(array.shape, array.dtype) for array in ins]
            + [
                pltpu.VMEM((TILES, TILE, LANES), jnp.bfloat16),
                pltpu.SemaphoreType.DMA((len(ins),)),
                pltpu.SemaphoreType.DMA((2 * places.count,)),
            ],
        ),
        out_shape=[low_like(count, TILE, LANES) for count in counts],
        compiler_params=PARAMS,
        name="weight_back",
    )(position, *ins)


def input_back_kernel(project_ref, grad_middle_ref, hidden_ref, vectors_ref, tiles_ref, out_ref, sums_ref, total_ref):
    across = D // LANES
    for part in range(3):
        weight = load_weight(tiles_ref, 0, "qkv_weight", 0, D // TILE, part * across, across)
        rows = product(project_ref[part], weight, NT)
        total_ref[...] = rows if part == 0 else total_ref[...] + rows
    normal, inverse = norm_parts(hidden_ref[...])
    grad_normed = total_ref[...]
    put_vector(sums_ref, 0, grad_normed * normal)
    put_vector(sums_ref, VECTOR_ROWS, grad_normed)
    put_vector(sums_ref, 2 * VECTOR_ROWS, project_ref[0].astype(jnp.float32))
    put_vector(sums_ref, 3 * VECTOR_ROWS, project_ref[2].astype(jnp.float32))
    out_ref[...] = grad_middle_ref[...] + norm_back(
        grad_normed, normal, inverse, vector(vectors_ref, "norm1_gain")
    )


def input_back(grad_project, grad_middle, hidden, vectors, tiles):
    rows = hidden.shape[0]
    ins = [grad_project, grad_middle, hidden, vectors]
    return pl.pallas_call(
        input_back_kernel,
        grid=(1,),
        in_specs=[whole_spec(array.shape) for array in ins] + [whole_spec((MLP_FIRST, TILE, LANES))],
        out_specs=[whole_spec((rows, D)), whole_spec((LATER * VECTOR_ROWS, LANES))],
        out_shape=[full_like(rows, D), full_like(LATER * VECTOR_ROWS, LANES)],
        scratch_shapes=[pltpu.VMEM((rows, D), jnp.float32)],
        compiler_params=PARAMS,
        name="input_back",
    )(*ins, tiles)


def pad_rows(images):
    padded = jnp.pad(images, ((0, 0), (0, ROWS - SEQ), (0, 0)))
    return padded.reshape(-1, D).astype(jnp.float32)


def cut_rows(rows):
    return rows.reshape(-1, ROWS, D)[:, :SEQ].astype(jnp.bfloat16)


class Places:
    def __init__(self, dp, fsdp):
        low = 2 if dp % 2 == 0 else 1
        core = 2 if fsdp % 2 == 0 else 1
        self.sizes = {"y": low, "x": dp // low, "z": fsdp // core, "c": core}
        self.count = dp * fsdp
        grid = np.arange(self.count).reshape(tuple(self.sizes.values()))
        self.grid = grid
        self.axis = {name: i for i, name in enumerate(self.sizes)}

    def exchange(self, block, axis, hop):
        size = self.sizes[axis]
        target = np.take(self.grid, np.arange(size) ^ hop, axis=self.axis[axis])
        perm = [(int(a), int(b)) for a, b in zip(self.grid.reshape(-1), target.reshape(-1))]
        return lax.ppermute(block, AXES, perm)

    def hops(self, axis):
        return range(1, self.sizes[axis])

    def powers(self, axis):
        return [1 << bit for bit in range(self.sizes[axis].bit_length() - 1)]

    def total(self, block, axes):
        for axis in axes:
            for hop in self.powers(axis):
                block = block + self.exchange(block, axis, hop)
        return block

    def position(self, me):
        return jnp.stack([(me // int(np.prod(self.grid.shape[i + 1 :]))) % n for i, n in enumerate(self.grid.shape)])


def block_at(at_ref, places, offset):
    number = 0
    for i, size in enumerate(places.grid.shape):
        number = number * size + (at_ref[i] ^ offset[i])
    return number


def copies_in(places, at_ref, parts, slots, whole_ref, sems):
    copies = []
    for part, listed in zip(parts, slots):
        count = part.shape[0] // len(listed)
        for i, slot in enumerate(listed):
            start = 0 if slot is None else block_at(at_ref, places, slot[0]) * (TILES // places.count) + slot[1]
            target = whole_ref.at[pl.ds(start, count)]
            copies.append(pltpu.make_async_copy(part.at[pl.ds(i * count, count)], target, sems.at[len(copies)]))
    return copies


def offset_of(**hops):
    return tuple(hops.get(axis, 0) for axis in ("y", "x", "z", "c"))


def join(blocks):
    return jnp.concatenate(blocks, axis=0) if len(blocks) > 1 else blocks[0]


ORDERS = (("x", "y"), ("y", "x"))


def group_of(shares, offsets):
    half = shares[0].shape[0] // 2
    return [(join([share[part * half : (part + 1) * half] for share in shares]), offsets) for part in range(2)]


def merge(*groups):
    return [(join([group[part][0] for group in groups]), sum((group[part][1] for group in groups), [])) for part in range(2)]


def fetch_column(places, share):
    return [places.exchange(share, "z", hop) for hop in places.hops("z")]


def column_offsets(places):
    return [offset_of(z=hop) for hop in range(places.sizes["z"])]


def fetch_plane(places, group, step):
    arrived = []
    for (block, offsets), order in zip(group, ORDERS):
        at = places.axis[order[step]]
        hops = range(1, places.sizes[order[step]])
        moved = [offset[:at] + (hop,) + offset[at + 1 :] for hop in hops for offset in offsets]
        arrived.append((join([places.exchange(block, order[step], hop) for hop in hops]), moved))
    return arrived


def fetch_plane_with(places, group, step, rows):
    (block, offsets), order = group[0], ORDERS[0]
    count, axis = block.shape[0], order[step]
    hops = range(1, places.sizes[axis])
    arrived = [places.exchange(jnp.concatenate([block, rows], axis=0), axis, hop) for hop in hops]
    moved = [tuple(hop if i == places.axis[axis] else part for i, part in enumerate(o)) for hop in hops for o in offsets]
    rows = sum([piece[count:] for piece in arrived], rows)
    other = fetch_plane(places, group, step)[1]
    return [(join([piece[:count] for piece in arrived]), moved), other], rows


def list_core(places, groups):
    parts = []
    for group in groups:
        half = TILES // places.count // 2
        parts += [(block, [(offset, part * half) for offset in offsets]) for part, (block, offsets) in enumerate(group)]
    return parts


def gather_core(places, groups):
    parts = list_core(places, groups)
    return [(join([block for block, _ in parts]), sum((slots for _, slots in parts), []))]


def fetch_core(places, parts):
    arrived = []
    for hop in range(1, places.sizes["c"]):
        for block, slots in parts:
            moved = [(offset[:3] + (hop,), first) for offset, first in slots]
            arrived.append((places.exchange(block, "c", hop), moved))
    return parts + arrived


def add_low(*blocks):
    total = blocks[0].astype(jnp.float32)
    for block in blocks[1:]:
        total = total + block.astype(jnp.float32)
    return total


def send_core(places, parts):
    cores = places.sizes["c"]
    halves = [parts[:cores], parts[cores:]]
    return [[mine] + [places.exchange(other, "c", hop) for hop, other in enumerate(others, 1)] for mine, *others in halves]


def plane_totals(places, blocks, axis):
    share = blocks[0].shape[0] // places.sizes[axis]
    cuts = [slice(i * share, (i + 1) * share) for i in range(places.sizes[axis])]
    return [add_low(*[block[cut] for block in blocks]).astype(jnp.bfloat16) for cut in cuts]


def send_totals(places, totals, axis):
    return totals[:1] + [places.exchange(total, axis, hop) for hop, total in enumerate(totals[1:], 1)]


def send_plane(places, sums, step):
    axes = [order[step] for order in ORDERS]
    return [send_totals(places, plane_totals(places, blocks, axis), axis) for blocks, axis in zip(sums, axes)]


def send_plane_tied(places, sums, step, later):
    (first, second), axes = sums, [order[step] for order in ORDERS]
    first, later = tie(first, later)
    first = plane_totals(places, first, axes[0])
    second, first, later = tie(second, first, later)
    result = [send_totals(places, first, axes[0])]
    second, later = tie(plane_totals(places, second, axes[1]), later)
    return result + [send_totals(places, second, axes[1])], later


def column_totals(places, sums):
    count = places.sizes["z"]
    share = sums[0][0].shape[0] // count
    cuts = [slice(hop * share, (hop + 1) * share) for hop in range(count)]
    return [join([add_low(*[block[cut] for block in blocks]).astype(jnp.bfloat16) for blocks in sums]) for cut in cuts]


def send_column(places, totals):
    return [totals[0]] + [places.exchange(total, "z", hop) for hop, total in enumerate(totals[1:], 1)]


class Layer:
    def __init__(self, places, position, counts, vectors):
        self.places, self.position, self.counts, self.vectors = places, position, counts, vectors

    def project(self, hidden, parts):
        normed, qkv, tiles = project(self.places, self.position, parts, hidden, self.vectors)
        self.saved = dict(hidden=hidden, normed=normed, qkv=qkv, tiles=tiles)

    def forward(self):
        saved = self.saved
        saved["attended"], saved["weights"] = attention(self.counts, saved["qkv"], self.bias)
        names = ("branch", "middle", "normed2", "activ", "slope", "mlp_out")
        result, *kept = mlp(saved["attended"], saved["hidden"], self.vectors, saved["tiles"])
        saved.update(zip(names, kept))
        return result

    def back_mlp(self, grad):
        return mlp_back(grad, self.saved, self.vectors, self.saved["tiles"])

    def back_attention(self, passed):
        return attention_back(self.saved["qkv"], passed[1], self.saved["weights"])

    def back_weights(self, passed, grad_project, stepwise):
        _, _, grad_mlp, grad_pre, grad_branch, _ = passed
        saved = self.saved
        ins = [saved["normed"], grad_project, saved["attended"], grad_branch, saved["normed2"], grad_pre]
        return weight_back(self.places, self.position, stepwise, ins + [saved["activ"], grad_mlp])

    def back_input(self, passed, grad_project):
        return input_back(grad_project, passed[0], self.saved["hidden"], self.vectors, self.saved["tiles"])


def scatter_whole(parts):
    whole = parts[0].reshape(-1, LANES)
    return lax.psum_scatter(whole, AXES, scatter_dimension=0, tiled=True).astype(jnp.float32)


def local(dp, fsdp, tokens, counts, params_first, params_second, cotangent):
    devices = dp * fsdp
    places = Places(dp, fsdp)
    stepwise = TILES % (4 * devices) == 0 and all(size & (size - 1) == 0 for size in places.sizes.values())
    share_rows = TILES * TILE // devices
    me = lax.axis_index(AXES)
    position = places.position(me)
    owned = Owned([params_first, params_second], me, devices)
    own = owned.share(0)
    small_rows = owned.small_rows(own)
    hidden, grad_output = pad_rows(tokens), pad_rows(cotangent)

    if stepwise:
        own = own.reshape(-1, TILE, LANES)
        column = fetch_column(places, own)
        near, small_rows = tie(group_of([own], [offset_of()]), small_rows)
        small_rows = small_rows.reshape(-1, TILE, LANES)
        near_first, small_rows = fetch_plane_with(places, near, 0, small_rows)
        near_first, small_rows = tie(near_first, small_rows)
        near_second, small_rows = fetch_plane_with(places, merge(near, near_first), 1, small_rows)
        small_rows = places.total(small_rows, "c")
        next_own, near_first = tie(owned.share(1, own), near_first)
        far, near_second = tie(group_of(column, column_offsets(places)[1:]), near_second)
        far_first = fetch_plane(places, far, 0)
        next_own, small_rows, far, hidden, grad_output = tie(next_own, small_rows, far, hidden, grad_output)
        next_own = jnp.concatenate([next_own, small_rows.reshape(-1, LANES)], axis=0)
        next_shares = [next_own] + fetch_column(places, next_own)
        small_rows = sum([rows[share_rows:] for rows in next_shares[1:]], next_own[share_rows:])
        small_rows = small_rows.reshape(2, -1, LANES)
        vectors = small_rows.astype(jnp.float32)
        next_shares = [rows[:share_rows].reshape(-1, TILE, LANES) for rows in next_shares]
        group = group_of(next_shares, column_offsets(places))
        far_second = fetch_plane(places, merge(far, far_first), 1)
        early = gather_core(places, [near, near_first, near_second, far, far_first])
    else:
        small_rows = lax.psum(small_rows, AXES)
    if stepwise:
        far_second, early, group, small_rows, vectors = tie(far_second, early, group, small_rows, vectors)
        parts = fetch_core(places, early) + fetch_core(places, list_core(places, [far_second]))
        first = fetch_plane(places, group, 0)
        first_layer = Layer(places, position, counts, vectors[0])
        first_layer.project(hidden, parts)
        first, group, first_layer.saved, small_rows = tie(first, group, first_layer.saved, small_rows)
        second_group = merge(group, first)
        second = fetch_plane(places, second_group, 1)
        small_rows, _ = tie(small_rows, second_group)
        entries = table_entries(small_rows)
        next_parts = fetch_core(places, list_core(places, [first]))
        first_layer.bias = bias_of(entries[0])
        result = first_layer.forward()
        next_parts, result, entries = tie(next_parts, result, entries)
        second_bias = bias_of(entries[1])
        next_parts += fetch_core(places, gather_core(places, [group]))
        second, next_parts, result, second_bias = tie(second, next_parts, result, second_bias)
        next_parts += fetch_core(places, list_core(places, [second]))
    else:
        vectors = small_rows.astype(jnp.float32)
        entries = table_entries(small_rows)
        second_bias = bias_of(entries[1])
        parts, next_parts = [
            [(lax.all_gather(share, AXES, axis=0, tiled=True).reshape(TILES, TILE, LANES), [None])]
            for share in (own, owned.share(1))
        ]
        first_layer = Layer(places, position, counts, vectors[0])
        first_layer.project(hidden, parts)
        first_layer.bias = bias_of(entries[0])
        result = first_layer.forward()
    second_layer = Layer(places, position, counts, vectors[1])
    second_layer.bias = second_bias
    second_layer.project(result, next_parts)
    result = second_layer.forward()
    output = cut_rows(result)

    next_passed = second_layer.back_mlp(grad_output)
    next_project, next_bias = second_layer.back_attention(next_passed)
    parts = second_layer.back_weights(next_passed, next_project, stepwise)
    if stepwise:
        sums = send_core(places, parts)
    else:
        next_share = scatter_whole(parts)
    grad, next_sums = second_layer.back_input(next_passed, next_project)
    if stepwise:
        sums, grad = send_plane_tied(places, sums, 0, grad)
    passed = first_layer.back_mlp(grad)
    project_grad, bias = first_layer.back_attention(passed)
    if stepwise:
        sums, passed, project_grad = tie(sums, passed, project_grad)
        sums = send_plane(places, sums, 1)
    parts = first_layer.back_weights(passed, project_grad, stepwise)
    if stepwise:
        sums, parts, passed, project_grad = tie(sums, parts, passed, project_grad)
        own_sums = send_core(places, parts)
        totals = column_totals(places, sums)
    else:
        share = scatter_whole(parts)
    if stepwise:
        own_sums, later = send_plane_tied(places, own_sums, 0, (bias, passed, project_grad, totals))
        bias, passed, project_grad, totals = later
        sums = send_column(places, totals)
    grad, own_row_sums = first_layer.back_input(passed, project_grad)
    small_grads = small_gradients(
        [own_row_sums, next_sums], [passed[5], next_passed[5]], tables_from_biases(bias, next_bias)
    )
    flat_share = FlatShare(me, devices, params_first.shape[0] * devices)
    if stepwise:
        own_sums, sums, small_grads = tie(own_sums, sums, small_grads)
        own_sums = send_plane(places, own_sums, 1)
        small_grads = places.total(small_grads, "zc")
        own_sums, small_grads = tie(own_sums, small_grads)
        own_sums = send_column(places, column_totals(places, own_sums))
        small_grads = places.total(small_grads, "xy")
        small_grads, sums = tie(small_grads, sums)
        grad_second = flat_share(add_low(*sums).reshape(-1, LANES), small_grads[1])
        own_sums, grad_second, output, grad_tokens = tie(own_sums, grad_second, output, cut_rows(grad))
        share = add_low(*own_sums).reshape(-1, LANES)
    else:
        small_grads = lax.psum(small_grads, AXES)
        grad_second = flat_share(next_share, small_grads[1])
        grad_tokens = cut_rows(grad)
    grad_first = flat_share(share, small_grads[0])
    return output, grad_tokens, grad_first, grad_second


def solution(mesh):
    return jax.shard_map(
        functools.partial(local, mesh.shape["dp"], mesh.shape["fsdp"]),
        mesh=mesh,
        in_specs=(P(AXES, None, None), P(AXES), P(AXES), P(AXES), P(AXES, None, None)),
        out_specs=(P(AXES, None, None), P(AXES, None, None), P(AXES), P(AXES)),
        check_vma=False,
    )
```

```python
import functools
import math

import jax
import jax.numpy as jnp
import numpy as np
from jax import lax
from jax.experimental import pallas as pl
from jax.experimental.pallas import tpu as pltpu
from jax.sharding import PartitionSpec as P

D = 768
HEADS = 12
HEAD = D // HEADS
FF = 3072
GRID = 14
SEQ = 197
RELS = 732
ROWS = 208
LANES = 128
TILE = 16
AXES = ("dp", "fsdp")
VMEM_LIMIT = 56 * 2**20

EPSILON = 1e-06
NEGATIVE = -1000000000.0

ENTRIES = [
    ("norm1_gain", (D,)),
    ("norm1_bias", (D,)),
    ("qkv_weight", (D, 3 * D)),
    ("query_bias", (D,)),
    ("value_bias", (D,)),
    ("relative_table", (RELS, HEADS)),
    ("proj_weight", (D, D)),
    ("proj_bias", (D,)),
    ("gamma_attn", (D,)),
    ("norm2_gain", (D,)),
    ("norm2_bias", (D,)),
    ("fc1_weight", (D, FF)),
    ("fc1_bias", (FF,)),
    ("fc2_weight", (FF, D)),
    ("fc2_bias", (D,)),
    ("gamma_mlp", (D,)),
]
WEIGHTS = {name: dims for name, dims in ENTRIES if name.endswith("weight")}
SIZES = dict(ENTRIES)
VECTORS = [
    "norm1_gain",
    "norm1_bias",
    "query_bias",
    "value_bias",
    "proj_bias",
    "gamma_attn",
    "norm2_gain",
    "norm2_bias",
    "fc2_bias",
    "gamma_mlp",
]
ROW = {name: i for i, name in enumerate(VECTORS)}


def count_rows(dims):
    return -(-math.prod(dims) // LANES)


def virtual_starts():
    starts, at = {}, 0
    for name, dims in ENTRIES:
        starts[name] = at
        at += count_rows(dims)
    return starts, at


STARTS, VIRTUAL = virtual_starts()
SHIFT = RELS * HEADS % LANES
TABLE_END = STARTS["proj_weight"]


def tile_order():
    parts = []
    for name, (depth, width) in WEIGHTS.items():
        across = width // LANES
        rows = STARTS[name] + np.arange(depth * across).reshape(depth // TILE, TILE, across)
        parts.append(rows.transpose(0, 2, 1).reshape(-1))
    return np.concatenate(parts)


def small_order():
    groups = [VECTORS, ["fc1_bias"], ["relative_table"]]
    rows = []
    for group in groups:
        for name in group:
            rows += [STARTS[name] + i for i in range(count_rows(SIZES[name]))]
        rows += [-1] * (-len(rows) % 8)
    return np.array(rows)


TILE_ROWS = tile_order()
SMALL_ROWS = small_order()
TILES = len(TILE_ROWS) // TILE


def tie(*trees):
    leaves, structure = jax.tree.flatten(trees)
    tied = iter(lax.optimization_barrier([leaf for leaf in leaves if isinstance(leaf, jax.Array)]))
    return structure.unflatten([next(tied) if isinstance(leaf, jax.Array) else leaf for leaf in leaves])


def halo(block, before, after, devices, join=True):
    rows = block.shape[-2]
    pieces = [block] if join else []
    for hop in range(1, -(-before // rows) + 1):
        take = min(rows, before - (hop - 1) * rows)
        perm = [(i, i + hop) for i in range(devices - hop)]
        pieces.insert(0, lax.ppermute(block[..., rows - take :, :], AXES, perm))
    for hop in range(1, -(-after // rows) + 1):
        take = min(rows, after - (hop - 1) * rows)
        perm = [(i + hop, i) for i in range(devices - hop)]
        pieces.append(lax.ppermute(block[..., :take, :], AXES, perm))
    return jnp.concatenate(pieces, axis=-2)


def pick_rows(index, source):
    chosen = index[:, None] == lax.broadcasted_iota(jnp.int32, (1, source.shape[0]), 1)
    return jnp.dot(chosen.astype(jnp.bfloat16), source.astype(jnp.bfloat16), preferred_element_type=jnp.float32)


def round_up(value, unit):
    return -(-value // unit) * unit


class Owned:
    def __init__(self, flats, me, devices):
        length = flats[0].shape[0] // LANES
        share = len(TILE_ROWS) // devices
        starts = np.arange(devices)[:, None] * length
        wanted = TILE_ROWS.reshape(devices, share) - starts
        before = round_up(max(0, -wanted.min()) + 1, TILE)
        after = round_up(max(0, wanted.max() + 1 - length), TILE)
        smalls = SMALL_ROWS[None] - starts
        smalls = np.where((smalls >= 0) & (smalls < length), smalls + before - 1, -1)
        self.wanted = self.mine(wanted + before - 1, me)
        self.smalls = self.mine(smalls, me)
        around = halo(jnp.stack([flat.reshape(length, LANES) for flat in flats]), before, after, devices)
        shifted = jnp.concatenate([around[:, :-1, SHIFT:], around[:, 1:, :SHIFT]], axis=2)
        at = me * length - before + 1 + lax.broadcasted_iota(jnp.int32, (1, shifted.shape[1], 1), 1)
        self.virtual = jnp.where(at < TABLE_END, around[:, 1:], shifted)

    @staticmethod
    def mine(table, me):
        return lax.dynamic_index_in_dim(jnp.asarray(table.astype(np.int32)), me, 0, keepdims=False)

    def small_rows(self, *after):
        virtual, *_ = tie(self.virtual, *after)
        return jnp.stack([pick_rows(self.smalls, rows).astype(jnp.bfloat16) for rows in virtual])

    def share(self, number, *after):
        rows = self.virtual[number]
        if after:
            rows, *_ = tie(rows, *after)
        return pick_rows(self.wanted, rows).astype(jnp.bfloat16)


class FlatShare:
    def __init__(self, me, devices, flat_length):
        length = flat_length // LANES // devices
        share = len(TILE_ROWS) // devices
        place = np.full(max(VIRTUAL, devices * length + 1), -1, np.int64)
        place[TILE_ROWS] = np.arange(len(TILE_ROWS))
        small_place = np.full(place.shape, -1, np.int64)
        small_place[SMALL_ROWS[SMALL_ROWS >= 0]] = np.flatnonzero(SMALL_ROWS >= 0)
        span = np.arange(devices)[:, None] * length + np.arange(length + 1)[None]
        relative = place[span] - np.arange(devices)[:, None] * share
        has = place[span] >= 0
        self.before = round_up(max(0, -relative[has].min()), TILE)
        self.after = round_up(max(0, relative[has].max() + 1 - share), TILE)
        smalls_at = self.before + share + self.after
        index = np.where(has, relative + self.before, -1)
        index = np.where(small_place[span] >= 0, small_place[span] + smalls_at, index)
        self.index = Owned.mine(index, me)
        self.at = me * length + lax.broadcasted_iota(jnp.int32, (length, 1), 0)
        self.devices = devices

    def __call__(self, owned, smalls):
        owned = owned.astype(jnp.bfloat16)
        share = owned.shape[0]
        around = halo(owned, self.before, self.after, self.devices, join=False)
        ends = self.before + share
        here = jnp.concatenate([owned, smalls.astype(jnp.bfloat16)], axis=0)
        index = self.index - self.before
        outside = (self.index < self.before) | ((self.index >= ends) & (self.index < ends + self.after))
        index = jnp.where(outside, -1, jnp.where(self.index >= ends, index - self.after, index))
        virtual = pick_rows(index, here)
        index = jnp.where(self.index < self.before, self.index, self.index - share)
        index = jnp.where(outside, index, -1)
        virtual = virtual + pick_rows(index, around)
        here, following = virtual[:-1], virtual[1:]
        lane = lax.broadcasted_iota(jnp.int32, (1, LANES), 1)
        shifted = jnp.concatenate([here[:, LANES - SHIFT :], following[:, : LANES - SHIFT]], axis=1)
        straight = (self.at < TABLE_END - 1) | ((self.at == TABLE_END - 1) & (lane < SHIFT))
        return jnp.where(straight, here, shifted).reshape(-1)


VECTOR_ROWS = D // LANES
FC1_AT = round_up(len(VECTORS) * VECTOR_ROWS, 8)
TABLE_AT = FC1_AT + FF // LANES
TABLE_ROWS = count_rows(SIZES["relative_table"])
LATER = 4


def table_entries(rows):
    tables = rows[:, TABLE_AT : TABLE_AT + TABLE_ROWS].reshape(2, -1)[:, : RELS * HEADS].reshape(2, RELS, HEADS)
    return jnp.pad(tables.transpose(0, 2, 1), ((0, 0), (0, 16 - HEADS), (0, ENTRY_LANES - RELS)))


def small_gradients(first, later, tables):
    tables = tables.reshape(2, RELS * HEADS)
    tables = jnp.pad(tables, ((0, 0), (0, round_up(TABLE_ROWS, 8) * LANES - RELS * HEADS))).reshape(2, -1, LANES)
    return jnp.concatenate([jnp.stack(first), jnp.stack(later), tables], axis=1)


SIDE = 2 * GRID - 1
WINDOW = round_up(SIDE * GRID, LANES) + LANES
WIDE = round_up(ROWS, LANES)


ENTRY_LANES = round_up(RELS, LANES)
HEAD_ROWS = 2 * 16


def entry_choice(column, transposed):
    shape = (1, WINDOW) if transposed else (WINDOW, 1)
    source = lax.broadcasted_iota(jnp.int32, shape, 1 if transposed else 0)
    group = source // GRID
    target = (SIDE - 1 - group) * SIDE - (source - group * GRID) + GRID - 1 + column
    target = jnp.where(source < SIDE * GRID, target, -1)
    entries = (ENTRY_LANES, 1) if transposed else (1, ENTRY_LANES)
    entry = lax.broadcasted_iota(jnp.int32, entries, 0 if transposed else 1)
    return (entry == target).astype(jnp.float32).astype(jnp.bfloat16)


def bias_kernel(entries_ref, bias_ref, windows_ref):
    for column in range(GRID):
        windows_ref[column] = product(entries_ref[...], entry_choice(column, True), NN)
    lane = lax.broadcasted_iota(jnp.int32, (1, WIDE), 1)
    inner = (lane >= 1) & (lane < SEQ)

    def head(i, _):
        ends = entries_ref[pl.ds(pl.multiple_of(i // 16 * 16, 16), 16), :].astype(jnp.float32)
        picked = lax.broadcasted_iota(jnp.int32, (16, 1), 0) == i % 16
        ends = jnp.sum(jnp.where(picked, ends, 0.0), axis=0, keepdims=True)
        top, left, corner = [ends[:, RELS - k : RELS - k + 1] for k in (3, 2, 1)]
        bias_ref[i] = jnp.zeros(bias_ref.shape[1:], jnp.float32)
        bias_ref[i, 0:1] = jnp.where(inner, top, jnp.where(lane == 0, corner, 0.0))[:, :ROWS]
        spread = jnp.concatenate([windows_ref[column, pl.ds(i, 1)] for column in range(GRID)], axis=0)
        for row in range(GRID):
            start = (GRID - 1 - row) * GRID
            window = pltpu.roll(spread, (1 - start) % WINDOW, 1)[:, :WIDE]
            window = jnp.where(inner, window, jnp.where(lane == 0, left, 0.0))
            bias_ref[i, 1 + row * GRID : 1 + (row + 1) * GRID] = window[:, :ROWS]
        return 0

    lax.fori_loop(0, HEADS, head, 0)


def bias_of(entries):
    return pl.pallas_call(
        bias_kernel,
        grid=(1,),
        in_specs=[pl.BlockSpec(entries.shape, lambda i: (0, 0))],
        out_specs=pl.BlockSpec((HEADS, ROWS, ROWS), lambda i: (0, 0, 0)),
        out_shape=jax.ShapeDtypeStruct((HEADS, ROWS, ROWS), jnp.float32),
        scratch_shapes=[pltpu.VMEM((GRID, 16, WINDOW), jnp.float32)],
        compiler_params=pltpu.CompilerParams(vmem_limit_bytes=VMEM_LIMIT),
        name="bias",
    )(entries)


def table_kernel(first_ref, second_ref, out_ref, windows_ref, ends_ref):
    lane = lax.broadcasted_iota(jnp.int32, (1, ROWS), 1)
    inner = (lane >= 1) & (lane < SEQ)
    entry = lax.broadcasted_iota(jnp.int32, (1, ENTRY_LANES), 1)
    windows_ref[...] = jnp.zeros_like(windows_ref)
    ends_ref[...] = jnp.zeros_like(ends_ref)
    for number, grad_ref in enumerate((first_ref, second_ref)):

        def head(i, _, number=number, grad_ref=grad_ref):
            total = jnp.zeros((GRID, WINDOW), jnp.float32)
            left = jnp.zeros((1, 1), jnp.float32)
            for row in range(GRID):
                start = (GRID - 1 - row) * GRID
                block = grad_ref[i, 1 + row * GRID : 1 + (row + 1) * GRID]
                left = left + jnp.sum(jnp.where(lane == 0, block, 0.0), keepdims=True)
                block = jnp.where(inner, block, 0.0)
                block = jnp.concatenate([block, jnp.zeros((GRID, WINDOW - ROWS), jnp.float32)], axis=1)
                total = total + pltpu.roll(block, (start - 1) % WINDOW, 1)
            at = pl.ds(number * 16 + i, 1)
            for column in range(GRID):
                windows_ref[column, at] = total[column : column + 1]
            first = grad_ref[i, 0:1]
            top = jnp.sum(jnp.where(inner, first, 0.0), keepdims=True)
            corner = jnp.sum(jnp.where(lane == 0, first, 0.0), keepdims=True)
            ends = jnp.where(entry == RELS - 3, top, jnp.where(entry == RELS - 2, left, 0.0))
            ends_ref[at] = jnp.where(entry == RELS - 1, corner, ends)
            return 0

        lax.fori_loop(0, HEADS, head, 0)
    out_ref[...] = ends_ref[...]
    for column in range(GRID):
        rows = windows_ref[column]
        high = rows.astype(jnp.bfloat16)
        low = (rows - high.astype(jnp.float32)).astype(jnp.bfloat16)
        chosen = entry_choice(column, False)
        out_ref[...] += product(high, chosen, NN) + product(low, chosen, NN)


def tables_from_biases(first, second):
    entries = pl.pallas_call(
        table_kernel,
        grid=(1,),
        in_specs=[pl.BlockSpec(first.shape, lambda i: (0, 0, 0))] * 2,
        out_specs=pl.BlockSpec((HEAD_ROWS, ENTRY_LANES), lambda i: (0, 0)),
        out_shape=jax.ShapeDtypeStruct((HEAD_ROWS, ENTRY_LANES), jnp.float32),
        scratch_shapes=[
            pltpu.VMEM((GRID, HEAD_ROWS, WINDOW), jnp.float32),
            pltpu.VMEM((HEAD_ROWS, ENTRY_LANES), jnp.float32),
        ],
        compiler_params=pltpu.CompilerParams(vmem_limit_bytes=VMEM_LIMIT),
        name="table_back",
    )(first, second)
    return entries.reshape(2, 16, ENTRY_LANES)[:, :HEADS, :RELS].transpose(0, 2, 1)


NT = (((1,), (1,)), ((), ()))
NN = (((1,), (0,)), ((), ()))
TN = (((0,), (0,)), ((), ()))


def product(left, right, dims):
    return lax.dot_general(left, right, dims, preferred_element_type=jnp.float32)


def own_lanes(head):
    lane = lax.broadcasted_iota(jnp.int32, (1, LANES), 1)
    return lane < HEAD if head == 0 else lane >= HEAD


def head_weights(query, key, bias, count, head):
    chosen = jnp.where(own_lanes(head), query, jnp.zeros_like(query))
    scores = product(chosen, key, NT) + bias
    column = lax.broadcasted_iota(jnp.int32, (1, ROWS), 1)
    scores = jnp.where(column < count, scores, NEGATIVE)
    grown = jnp.exp(scores - jnp.max(scores, axis=1, keepdims=True))
    return grown * (1.0 / jnp.sum(grown, axis=1, keepdims=True))


def attention_kernel(pairs, counts_ref, query_ref, key_ref, value_ref, bias_ref, out_ref, weights_ref):
    count = counts_ref[pl.program_id(1)]
    for pair in range(pairs):
        lanes = slice(pair * LANES, (pair + 1) * LANES)
        query, key, value = query_ref[:, lanes], key_ref[:, lanes], value_ref[:, lanes]
        parts = []
        for head in range(2):
            weights = head_weights(query, key, bias_ref[2 * pair + head], count, head).astype(jnp.bfloat16)
            weights_ref[0, 2 * pair + head] = weights
            parts.append(product(weights, value, NN))
        out_ref[:, lanes] = jnp.where(own_lanes(0), parts[0], parts[1]).astype(jnp.bfloat16)


def attention_back_kernel(pairs, query_ref, key_ref, value_ref, grad_ref, weights_ref, out_ref, db_ref):
    image = pl.program_id(1)

    @pl.when(image == 0)
    def _():
        db_ref[...] = jnp.zeros_like(db_ref)

    for pair in range(pairs):
        lanes = slice(pair * LANES, (pair + 1) * LANES)
        query, key, value, grad = query_ref[:, lanes], key_ref[:, lanes], value_ref[:, lanes], grad_ref[:, lanes]
        dq, dk, dv = [], [], []
        for head in range(2):
            low_weights = weights_ref[0, 2 * pair + head]
            weights = low_weights.astype(jnp.float32)
            chosen = jnp.where(own_lanes(head), grad, jnp.zeros_like(grad))
            weighted = weights * product(chosen, value, NT)
            dv.append(product(low_weights, grad, TN))
            grad_scores = weighted - weights * jnp.sum(weighted, axis=1, keepdims=True)
            low = grad_scores.astype(jnp.bfloat16)
            dq.append(product(low, key, NN))
            dk.append(product(low, query, TN))
            db_ref[2 * pair + head] += grad_scores
        first = own_lanes(0)
        out_ref[0, :, lanes] = (jnp.where(first, dq[0], dq[1]) * HEAD**-0.5).astype(jnp.bfloat16)
        out_ref[1, :, lanes] = jnp.where(first, dk[0], dk[1]).astype(jnp.bfloat16)
        out_ref[2, :, lanes] = jnp.where(first, dv[0], dv[1]).astype(jnp.bfloat16)


def attention_specs(pairs):
    steps = D // LANES // pairs
    lanes = [
        pl.BlockSpec((ROWS, pairs * LANES), lambda step, image, *_, part=part: (image, part * steps + step))
        for part in range(3)
    ]
    bias = pl.BlockSpec((2 * pairs, ROWS, ROWS), lambda step, image, *_: (step, 0, 0))
    weights = pl.BlockSpec((1, 2 * pairs, ROWS, ROWS), lambda step, image, *_: (image, step, 0, 0))
    return steps, lanes, bias, weights


def attention(counts, qkv, bias, pairs=6):
    images = qkv.shape[0] // ROWS
    steps, lanes, bias_spec, weights_spec = attention_specs(pairs)
    return pl.pallas_call(
        functools.partial(attention_kernel, pairs),
        grid_spec=pltpu.PrefetchScalarGridSpec(
            num_scalar_prefetch=1,
            grid=(steps, images),
            in_specs=lanes + [bias_spec],
            out_specs=[lanes[0], weights_spec],
        ),
        out_shape=[
            jax.ShapeDtypeStruct((qkv.shape[0], D), jnp.bfloat16),
            jax.ShapeDtypeStruct((images, HEADS, ROWS, ROWS), jnp.bfloat16),
        ],
        compiler_params=pltpu.CompilerParams(vmem_limit_bytes=VMEM_LIMIT),
        name="attention",
    )(counts, qkv, qkv, qkv, bias)


def attention_back(qkv, grad, weights, pairs=3):
    images = qkv.shape[0] // ROWS
    steps, lanes, bias_spec, weights_spec = attention_specs(pairs)
    return pl.pallas_call(
        functools.partial(attention_back_kernel, pairs),
        grid=(steps, images),
        in_specs=lanes + [lanes[0], weights_spec],
        out_specs=[
            pl.BlockSpec((3, ROWS, pairs * LANES), lambda step, image: (0, image, step)),
            bias_spec,
        ],
        out_shape=[
            jax.ShapeDtypeStruct((3, qkv.shape[0], D), jnp.bfloat16),
            jax.ShapeDtypeStruct((HEADS, ROWS, ROWS), jnp.float32),
        ],
        compiler_params=pltpu.CompilerParams(vmem_limit_bytes=VMEM_LIMIT),
        name="attention_back",
    )(qkv, qkv, qkv, grad, weights)


def tile_starts():
    starts, at = {}, 0
    for name, (depth, width) in WEIGHTS.items():
        starts[name] = at
        at += depth // TILE * (width // LANES)
    return starts


FIRST = tile_starts()
MLP_FIRST = FIRST["proj_weight"]
SPAN = 1024


def load_weight(ref, base, name, row, rows, column, columns):
    first, across = FIRST[name] - base, WEIGHTS[name][1] // LANES
    lines = []
    for i in range(rows):
        at = first + (row + i) * across + column
        lines.append(jnp.concatenate([ref[at + j] for j in range(columns)], axis=1))
    return jnp.concatenate(lines, axis=0)


def gelu_and_slope(values):
    size = jnp.abs(values)
    step = 1.0 / (1.0 + (0.3275911 / math.sqrt(2.0)) * size)
    bell = jnp.exp(-0.5 * values * values)
    series = 1.061405429
    for term in (-1.453152027, 1.421413741, -0.284496736, 0.254829592):
        series = series * step + term
    tail = 0.5 * series * step * bell
    area = jnp.where(values < 0, tail, 1.0 - tail)
    return values * area, area + values * bell * (1.0 / math.sqrt(2.0 * math.pi))


def norm_parts(values):
    centre = values - jnp.mean(values, axis=-1, keepdims=True)
    spread = jnp.mean(centre * centre, axis=-1, keepdims=True)
    inverse = lax.rsqrt(spread + EPSILON)
    return centre * inverse, inverse


def norm_back(grad, normal, inverse, gain):
    scaled = grad * gain
    first = jnp.mean(scaled, axis=-1, keepdims=True)
    second = jnp.mean(scaled * normal, axis=-1, keepdims=True)
    return (scaled - first - normal * second) * inverse


def wide_row(ref, first, count):
    return jnp.concatenate([ref[first + i : first + i + 1] for i in range(count)], axis=1)


def vector(ref, name):
    return wide_row(ref, ROW[name] * VECTOR_ROWS, VECTOR_ROWS)


def put_vector(ref, row, values):
    sums = jnp.sum(values, axis=0, keepdims=True)
    for i in range(sums.shape[1] // LANES):
        ref[row + i : row + i + 1] = sums[:, i * LANES : (i + 1) * LANES]


def later_row(name):
    return (ROW[name] - LATER) * VECTOR_ROWS


def whole_spec(shape):
    return pl.BlockSpec(shape, lambda *_: (0,) * len(shape))


ANYWHERE = pl.BlockSpec(memory_space=pl.ANY)
PARAMS = pltpu.CompilerParams(vmem_limit_bytes=VMEM_LIMIT)


def low_like(*shape):
    return jax.ShapeDtypeStruct(shape, jnp.bfloat16)


def full_like(*shape):
    return jax.ShapeDtypeStruct(shape, jnp.float32)


def project_kernel(places, slots, at_ref, *refs):
    parts, refs = refs[: len(slots)], refs[len(slots) :]
    hidden_ref, vectors_ref, normed_ref, qkv_ref, tiles_ref, whole_ref, sems, out_sem = refs
    copies = copies_in(places, at_ref, parts, slots, whole_ref, sems)
    for copy in copies:
        copy.start()
    normal, _ = norm_parts(hidden_ref[...])
    normed_ref[...] = (normal * vector(vectors_ref, "norm1_gain") + vector(vectors_ref, "norm1_bias")).astype(
        jnp.bfloat16
    )
    for copy in copies:
        copy.wait()
    leaving = pltpu.make_async_copy(whole_ref, tiles_ref, out_sem)
    leaving.start()
    across = D // LANES
    for part in range(3):
        weight = load_weight(whole_ref, 0, "qkv_weight", 0, D // TILE, part * across, across)
        rows = product(normed_ref[...], weight, NN)
        if part == 0:
            rows = (rows + vector(vectors_ref, "query_bias")) * HEAD**-0.5
        if part == 2:
            rows = rows + vector(vectors_ref, "value_bias")
        qkv_ref[:, part * D : (part + 1) * D] = rows.astype(jnp.bfloat16)
    leaving.wait()


def project(places, position, parts, hidden, vectors):
    arrays = [array for array, _ in parts]
    slots = [listed for _, listed in parts]
    rows = hidden.shape[0]
    return pl.pallas_call(
        functools.partial(project_kernel, places, slots),
        grid_spec=pltpu.PrefetchScalarGridSpec(
            num_scalar_prefetch=1,
            grid=(1,),
            in_specs=[ANYWHERE] * len(arrays) + [whole_spec((rows, D)), whole_spec(vectors.shape)],
            out_specs=[whole_spec((rows, D)), whole_spec((rows, 3 * D)), ANYWHERE],
            scratch_shapes=[
                pltpu.VMEM((TILES, TILE, LANES), jnp.bfloat16),
                pltpu.SemaphoreType.DMA((sum(len(listed) for listed in slots),)),
                pltpu.SemaphoreType.DMA(()),
            ],
        ),
        out_shape=[low_like(rows, D), low_like(rows, 3 * D), low_like(TILES, TILE, LANES)],
        compiler_params=PARAMS,
        name="project",
    )(position, *arrays, hidden, vectors)


def mlp_weights(tiles_ref, weight_ref, sems, order):
    copies = []
    for i, name in enumerate(order):
        depth, width = WEIGHTS[name]
        count = depth // TILE * (width // LANES)
        here = weight_ref.at[pl.ds(FIRST[name] - MLP_FIRST, count)]
        copies.append(pltpu.make_async_copy(tiles_ref.at[pl.ds(FIRST[name], count)], here, sems.at[i]))
        copies[-1].start()
    return copies


def span_of(step):
    return slice(step * SPAN, (step + 1) * SPAN)


class Leaving:
    def __init__(self, outs, buffers, sems):
        self.outs, self.buffers, self.sems, self.copies = outs, buffers, sems, []

    def start(self, number, columns=None):
        source, target = self.buffers[number], self.outs[number]
        if columns is not None:
            source, target = source.at[:, columns], target.at[:, columns]
        self.copies.append(pltpu.make_async_copy(source, target, self.sems.at[len(self.copies)]))
        self.copies[-1].start()

    def wait(self):
        for copy in self.copies:
            copy.wait()


def mlp_kernel(attended_ref, hidden_ref, vectors_ref, tiles_ref, *refs):
    outs, buffers, (total_ref, weight_ref, sems, out_sems, fc1_bias_ref) = refs[:7], refs[7:14], refs[14:]
    result_ref, branch_ref, middle_ref, normed_ref, activ_ref, slope_ref, mlp_ref = buffers
    leaving = Leaving(outs, buffers, out_sems)
    copies = mlp_weights(tiles_ref, weight_ref, sems, ("proj_weight", "fc1_weight", "fc2_weight"))
    fc1_bias_ref[...] = wide_row(vectors_ref, FC1_AT, FF // LANES)
    copies[0].wait()
    across = D // LANES
    weight = load_weight(weight_ref, MLP_FIRST, "proj_weight", 0, D // TILE, 0, across)
    branch = product(attended_ref[...], weight, NN) + vector(vectors_ref, "proj_bias")
    branch_ref[...] = branch.astype(jnp.bfloat16)
    leaving.start(1)
    middle_ref[...] = hidden_ref[...] + vector(vectors_ref, "gamma_attn") * branch
    leaving.start(2)
    normal, _ = norm_parts(middle_ref[...])
    normed_ref[...] = (normal * vector(vectors_ref, "norm2_gain") + vector(vectors_ref, "norm2_bias")).astype(
        jnp.bfloat16
    )
    leaving.start(3)
    total_ref[...] = jnp.broadcast_to(vector(vectors_ref, "fc2_bias"), total_ref.shape)
    copies[1].wait()

    def step(i, _):
        span = span_of(i)
        weight = load_weight(weight_ref, MLP_FIRST, "fc1_weight", 0, D // TILE, i * (SPAN // LANES), SPAN // LANES)
        activ, slope = gelu_and_slope(product(normed_ref[...], weight, NN) + fc1_bias_ref[:, span])
        activ = activ.astype(jnp.bfloat16)
        activ_ref[:, span] = activ
        slope_ref[:, span] = slope.astype(jnp.bfloat16)
        leaving.start(4, span)
        leaving.start(5, span)
        if i == 0:
            copies[2].wait()
        weight = load_weight(weight_ref, MLP_FIRST, "fc2_weight", i * (SPAN // TILE), SPAN // TILE, 0, across)
        total_ref[...] += product(activ, weight, NN)
        return 0

    for i in range(FF // SPAN):
        step(i, 0)
    result_ref[...] = middle_ref[...] + vector(vectors_ref, "gamma_mlp") * total_ref[...]
    leaving.start(0)
    mlp_ref[...] = total_ref[...].astype(jnp.bfloat16)
    leaving.start(6)
    leaving.wait()


def mlp_scratch(rows, outs):
    return [pltpu.VMEM(out.shape, out.dtype) for out in outs] + [
        pltpu.VMEM((rows, D), jnp.float32),
        pltpu.VMEM((TILES - MLP_FIRST, TILE, LANES), jnp.bfloat16),
        pltpu.SemaphoreType.DMA((3,)),
        pltpu.SemaphoreType.DMA((len(outs) + 2 * (FF // SPAN),)),
    ]


def mlp(attended, hidden, vectors, tiles):
    rows = hidden.shape[0]
    outs = [full_like(rows, D), low_like(rows, D), full_like(rows, D), low_like(rows, D)]
    outs += [low_like(rows, FF), low_like(rows, FF), low_like(rows, D)]
    ins = [attended, hidden, vectors]
    return pl.pallas_call(
        mlp_kernel,
        grid=(1,),
        in_specs=[whole_spec(array.shape) for array in ins] + [ANYWHERE],
        out_specs=[ANYWHERE] * len(outs),
        out_shape=outs,
        scratch_shapes=mlp_scratch(rows, outs) + [pltpu.VMEM((1, FF), jnp.float32)],
        compiler_params=PARAMS,
        name="mlp",
    )(*ins, tiles)


def mlp_back_kernel(grad_ref, branch_ref, middle_ref, slope_ref, mlp_ref, vectors_ref, tiles_ref, *refs):
    outs, buffers, (total_ref, weight_ref, sems, out_sems) = refs[:6], refs[6:12], refs[12:]
    grad_middle_ref, grad_attended_ref, grad_mlp_ref, grad_pre_ref, grad_branch_ref, sums_ref = buffers
    leaving = Leaving(outs, buffers, out_sems)
    copies = mlp_weights(tiles_ref, weight_ref, sems, ("fc2_weight", "fc1_weight", "proj_weight"))
    across = D // LANES
    grad = grad_ref[...]
    sums_ref[...] = jnp.zeros_like(sums_ref)
    put_vector(sums_ref, later_row("gamma_mlp"), grad * mlp_ref[...].astype(jnp.float32))
    grad_mlp = grad * vector(vectors_ref, "gamma_mlp")
    put_vector(sums_ref, later_row("fc2_bias"), grad_mlp)
    grad_mlp_ref[...] = grad_mlp.astype(jnp.bfloat16)
    leaving.start(2)
    total_ref[...] = jnp.zeros_like(total_ref)
    copies[0].wait()

    def step(i, _):
        span = span_of(i)
        weight = load_weight(weight_ref, MLP_FIRST, "fc2_weight", i * (SPAN // TILE), SPAN // TILE, 0, across)
        grad_pre = product(grad_mlp_ref[...], weight, NT) * slope_ref[:, span].astype(jnp.float32)
        sums = jnp.sum(grad_pre, axis=0, keepdims=True)
        sums = jnp.concatenate([sums[:, k * LANES : (k + 1) * LANES] for k in range(SPAN // LANES)], axis=0)
        first = FC1_AT - LATER * VECTOR_ROWS + i * (SPAN // LANES)
        sums_ref[first : first + SPAN // LANES] = sums
        grad_pre = grad_pre.astype(jnp.bfloat16)
        grad_pre_ref[:, span] = grad_pre
        leaving.start(3, span)
        if i == 0:
            copies[1].wait()
        weight = load_weight(weight_ref, MLP_FIRST, "fc1_weight", 0, D // TILE, i * (SPAN // LANES), SPAN // LANES)
        total_ref[...] += product(grad_pre, weight, NT)
        return 0

    for i in range(FF // SPAN):
        step(i, 0)
    normal, inverse = norm_parts(middle_ref[...])
    grad_normed = total_ref[...]
    put_vector(sums_ref, later_row("norm2_gain"), grad_normed * normal)
    put_vector(sums_ref, later_row("norm2_bias"), grad_normed)
    grad_middle = grad_ref[...] + norm_back(grad_normed, normal, inverse, vector(vectors_ref, "norm2_gain"))
    grad_middle_ref[...] = grad_middle
    leaving.start(0)
    put_vector(sums_ref, later_row("gamma_attn"), grad_middle * branch_ref[...].astype(jnp.float32))
    grad_branch = grad_middle * vector(vectors_ref, "gamma_attn")
    put_vector(sums_ref, later_row("proj_bias"), grad_branch)
    leaving.start(5)
    grad_branch_ref[...] = grad_branch.astype(jnp.bfloat16)
    leaving.start(4)
    copies[2].wait()
    weight = load_weight(weight_ref, MLP_FIRST, "proj_weight", 0, D // TILE, 0, across)
    grad_attended_ref[...] = product(grad_branch_ref[...], weight, NT).astype(jnp.bfloat16)
    leaving.start(1)
    leaving.wait()


def mlp_back(grad, saved, vectors, tiles):
    rows = grad.shape[0]
    outs = [full_like(rows, D), low_like(rows, D), low_like(rows, D), low_like(rows, FF), low_like(rows, D)]
    outs += [full_like(TABLE_AT - LATER * VECTOR_ROWS, LANES)]
    ins = [grad, saved["branch"], saved["middle"], saved["slope"], saved["mlp_out"], vectors]
    return pl.pallas_call(
        mlp_back_kernel,
        grid=(1,),
        in_specs=[whole_spec(array.shape) for array in ins] + [ANYWHERE],
        out_specs=[ANYWHERE] * len(outs),
        out_shape=outs,
        scratch_shapes=mlp_scratch(rows, outs),
        compiler_params=PARAMS,
        name="mlp_back",
    )(*ins, tiles)


def scatter_place(places, at_ref, device, part):
    position = np.unravel_index(device, places.grid.shape)
    apart = {name: at_ref[i] ^ int(position[i]) for name, i in places.axis.items()}
    first, second = ORDERS[part]
    slot = (apart[first] * places.sizes[second] + apart[second]) * places.sizes["z"] + apart["z"]
    return apart["c"], slot


def weight_back_kernel(places, stepwise, at_ref, *refs):
    sources, refs = refs[:8], refs[8:]
    outs = refs[: 2 * places.sizes["c"] if stepwise else 1]
    operands, (whole_ref, in_sems, sems) = refs[len(outs) : len(outs) + 8], refs[len(outs) + 8 :]
    coming = [
        pltpu.make_async_copy(source, operand, in_sems.at[i]) for i, (source, operand) in enumerate(zip(sources, operands))
    ]
    for copy in coming:
        copy.start()
    normed_ref, project_ref, attended_ref, branch_ref, normed2_ref, pre_ref, activ_ref, mlp_ref = operands
    across = D // LANES

    def put(name, row, column, left, grad):
        block = product(left, grad, TN).astype(jnp.bfloat16)
        wide = WEIGHTS[name][1] // LANES
        for i in range(D // TILE):
            for j in range(across):
                at = FIRST[name] + (row + i) * wide + column + j
                whole_ref[at] = block[i * TILE : (i + 1) * TILE, j * LANES : (j + 1) * LANES]

    half = TILES // places.count // 2
    sent = []

    def send(ready):
        while stepwise and (len(sent) + 1) * half <= ready:
            number = len(sent)
            core, slot = scatter_place(places, at_ref, number // 2, number % 2)
            source = whole_ref.at[pl.ds(number * half, half)]
            for k in range(places.sizes["c"]):
                target = outs[number % 2 * places.sizes["c"] + k].at[pl.ds(slot * half, half)]
                copy = pltpu.make_async_copy(source, target, sems.at[number])
                pl.when(core == k)(copy.start)
            sent.append(copy)

    coming[0].wait()
    coming[1].wait()
    for part in range(3):
        put("qkv_weight", 0, part * across, normed_ref[...], project_ref[part])
    send(FIRST["proj_weight"])
    coming[2].wait()
    coming[3].wait()
    put("proj_weight", 0, 0, attended_ref[...], branch_ref[...])
    send(FIRST["fc1_weight"])
    coming[4].wait()
    coming[5].wait()
    for part in range(FF // D):
        put("fc1_weight", 0, part * across, normed2_ref[...], pre_ref[:, part * D : (part + 1) * D])
    send(FIRST["fc2_weight"])
    coming[6].wait()
    coming[7].wait()
    for part in range(FF // D):
        put("fc2_weight", part * (D // TILE), 0, activ_ref[:, part * D : (part + 1) * D], mlp_ref[...])
        send(FIRST["fc2_weight"] + (part + 1) * (D // TILE) * across)
    if not stepwise:
        sent.append(pltpu.make_async_copy(whole_ref, outs[0], sems.at[0]))
        sent[0].start()
    for copy in sent:
        copy.wait()


def weight_back(places, position, stepwise, ins):
    cores = places.sizes["c"]
    counts = [TILES // (2 * cores)] * (2 * cores) if stepwise else [TILES]
    return pl.pallas_call(
        functools.partial(weight_back_kernel, places, stepwise),
        grid_spec=pltpu.PrefetchScalarGridSpec(
            num_scalar_prefetch=1,
            grid=(1,),
            in_specs=[ANYWHERE] * len(ins),
            out_specs=[ANYWHERE] * len(counts),
            scratch_shapes=[pltpu.VMEM(array.shape, array.dtype) for array in ins]
            + [
                pltpu.VMEM((TILES, TILE, LANES), jnp.bfloat16),
                pltpu.SemaphoreType.DMA((len(ins),)),
                pltpu.SemaphoreType.DMA((2 * places.count,)),
            ],
        ),
        out_shape=[low_like(count, TILE, LANES) for count in counts],
        compiler_params=PARAMS,
        name="weight_back",
    )(position, *ins)


def input_back_kernel(project_ref, grad_middle_ref, hidden_ref, vectors_ref, tiles_ref, out_ref, sums_ref, total_ref):
    across = D // LANES
    for part in range(3):
        weight = load_weight(tiles_ref, 0, "qkv_weight", 0, D // TILE, part * across, across)
        rows = product(project_ref[part], weight, NT)
        total_ref[...] = rows if part == 0 else total_ref[...] + rows
    normal, inverse = norm_parts(hidden_ref[...])
    grad_normed = total_ref[...]
    put_vector(sums_ref, 0, grad_normed * normal)
    put_vector(sums_ref, VECTOR_ROWS, grad_normed)
    put_vector(sums_ref, 2 * VECTOR_ROWS, project_ref[0].astype(jnp.float32))
    put_vector(sums_ref, 3 * VECTOR_ROWS, project_ref[2].astype(jnp.float32))
    out_ref[...] = grad_middle_ref[...] + norm_back(
        grad_normed, normal, inverse, vector(vectors_ref, "norm1_gain")
    )


def input_back(grad_project, grad_middle, hidden, vectors, tiles):
    rows = hidden.shape[0]
    ins = [grad_project, grad_middle, hidden, vectors]
    return pl.pallas_call(
        input_back_kernel,
        grid=(1,),
        in_specs=[whole_spec(array.shape) for array in ins] + [whole_spec((MLP_FIRST, TILE, LANES))],
        out_specs=[whole_spec((rows, D)), whole_spec((LATER * VECTOR_ROWS, LANES))],
        out_shape=[full_like(rows, D), full_like(LATER * VECTOR_ROWS, LANES)],
        scratch_shapes=[pltpu.VMEM((rows, D), jnp.float32)],
        compiler_params=PARAMS,
        name="input_back",
    )(*ins, tiles)


def pad_rows(images):
    padded = jnp.pad(images, ((0, 0), (0, ROWS - SEQ), (0, 0)))
    return padded.reshape(-1, D).astype(jnp.float32)


def cut_rows(rows):
    return rows.reshape(-1, ROWS, D)[:, :SEQ].astype(jnp.bfloat16)


class Places:
    def __init__(self, dp, fsdp):
        low = 2 if dp % 2 == 0 else 1
        core = 2 if fsdp % 2 == 0 else 1
        self.sizes = {"y": low, "x": dp // low, "z": fsdp // core, "c": core}
        self.count = dp * fsdp
        grid = np.arange(self.count).reshape(tuple(self.sizes.values()))
        self.grid = grid
        self.axis = {name: i for i, name in enumerate(self.sizes)}

    def exchange(self, block, axis, hop):
        size = self.sizes[axis]
        target = np.take(self.grid, np.arange(size) ^ hop, axis=self.axis[axis])
        perm = [(int(a), int(b)) for a, b in zip(self.grid.reshape(-1), target.reshape(-1))]
        return lax.ppermute(block, AXES, perm)

    def hops(self, axis):
        return range(1, self.sizes[axis])

    def powers(self, axis):
        return [1 << bit for bit in range(self.sizes[axis].bit_length() - 1)]

    def total(self, block, axes):
        for axis in axes:
            for hop in self.powers(axis):
                block = block + self.exchange(block, axis, hop)
        return block

    def position(self, me):
        return jnp.stack([(me // int(np.prod(self.grid.shape[i + 1 :]))) % n for i, n in enumerate(self.grid.shape)])


def block_at(at_ref, places, offset):
    number = 0
    for i, size in enumerate(places.grid.shape):
        number = number * size + (at_ref[i] ^ offset[i])
    return number


def copies_in(places, at_ref, parts, slots, whole_ref, sems):
    copies = []
    for part, listed in zip(parts, slots):
        count = part.shape[0] // len(listed)
        for i, slot in enumerate(listed):
            start = 0 if slot is None else block_at(at_ref, places, slot[0]) * (TILES // places.count) + slot[1]
            target = whole_ref.at[pl.ds(start, count)]
            copies.append(pltpu.make_async_copy(part.at[pl.ds(i * count, count)], target, sems.at[len(copies)]))
    return copies


def offset_of(**hops):
    return tuple(hops.get(axis, 0) for axis in ("y", "x", "z", "c"))


def join(blocks):
    return jnp.concatenate(blocks, axis=0) if len(blocks) > 1 else blocks[0]


ORDERS = (("x", "y"), ("y", "x"))


def group_of(shares, offsets):
    half = shares[0].shape[0] // 2
    return [(join([share[part * half : (part + 1) * half] for share in shares]), offsets) for part in range(2)]


def merge(*groups):
    return [(join([group[part][0] for group in groups]), sum((group[part][1] for group in groups), [])) for part in range(2)]


def fetch_column(places, share):
    return [places.exchange(share, "z", hop) for hop in places.hops("z")]


def column_offsets(places):
    return [offset_of(z=hop) for hop in range(places.sizes["z"])]


def fetch_plane(places, group, step):
    arrived = []
    for (block, offsets), order in zip(group, ORDERS):
        at = places.axis[order[step]]
        hops = range(1, places.sizes[order[step]])
        moved = [offset[:at] + (hop,) + offset[at + 1 :] for hop in hops for offset in offsets]
        arrived.append((join([places.exchange(block, order[step], hop) for hop in hops]), moved))
    return arrived


def fetch_plane_with(places, group, step, rows):
    (block, offsets), order = group[0], ORDERS[0]
    count, axis = block.shape[0], order[step]
    hops = range(1, places.sizes[axis])
    arrived = [places.exchange(jnp.concatenate([block, rows], axis=0), axis, hop) for hop in hops]
    moved = [tuple(hop if i == places.axis[axis] else part for i, part in enumerate(o)) for hop in hops for o in offsets]
    rows = sum([piece[count:] for piece in arrived], rows)
    other = fetch_plane(places, group, step)[1]
    return [(join([piece[:count] for piece in arrived]), moved), other], rows


def list_core(places, groups):
    parts = []
    for group in groups:
        half = TILES // places.count // 2
        parts += [(block, [(offset, part * half) for offset in offsets]) for part, (block, offsets) in enumerate(group)]
    return parts


def gather_core(places, groups):
    parts = list_core(places, groups)
    return [(join([block for block, _ in parts]), sum((slots for _, slots in parts), []))]


def fetch_core(places, parts):
    arrived = []
    for hop in range(1, places.sizes["c"]):
        for block, slots in parts:
            moved = [(offset[:3] + (hop,), first) for offset, first in slots]
            arrived.append((places.exchange(block, "c", hop), moved))
    return parts + arrived


def add_low(*blocks):
    total = blocks[0].astype(jnp.float32)
    for block in blocks[1:]:
        total = total + block.astype(jnp.float32)
    return total


def send_core(places, parts):
    cores = places.sizes["c"]
    halves = [parts[:cores], parts[cores:]]
    return [[mine] + [places.exchange(other, "c", hop) for hop, other in enumerate(others, 1)] for mine, *others in halves]


def plane_totals(places, blocks, axis):
    share = blocks[0].shape[0] // places.sizes[axis]
    cuts = [slice(i * share, (i + 1) * share) for i in range(places.sizes[axis])]
    return [add_low(*[block[cut] for block in blocks]).astype(jnp.bfloat16) for cut in cuts]


def send_totals(places, totals, axis):
    return totals[:1] + [places.exchange(total, axis, hop) for hop, total in enumerate(totals[1:], 1)]


def send_plane(places, sums, step):
    axes = [order[step] for order in ORDERS]
    return [send_totals(places, plane_totals(places, blocks, axis), axis) for blocks, axis in zip(sums, axes)]


def send_plane_tied(places, sums, step, later):
    (first, second), axes = sums, [order[step] for order in ORDERS]
    first, later = tie(first, later)
    first = plane_totals(places, first, axes[0])
    second, first, later = tie(second, first, later)
    result = [send_totals(places, first, axes[0])]
    second, later = tie(plane_totals(places, second, axes[1]), later)
    return result + [send_totals(places, second, axes[1])], later


def column_totals(places, sums):
    count = places.sizes["z"]
    share = sums[0][0].shape[0] // count
    cuts = [slice(hop * share, (hop + 1) * share) for hop in range(count)]
    return [join([add_low(*[block[cut] for block in blocks]).astype(jnp.bfloat16) for blocks in sums]) for cut in cuts]


def send_column(places, totals):
    return [totals[0]] + [places.exchange(total, "z", hop) for hop, total in enumerate(totals[1:], 1)]


class Layer:
    def __init__(self, places, position, counts, vectors):
        self.places, self.position, self.counts, self.vectors = places, position, counts, vectors

    def project(self, hidden, parts):
        normed, qkv, tiles = project(self.places, self.position, parts, hidden, self.vectors)
        self.saved = dict(hidden=hidden, normed=normed, qkv=qkv, tiles=tiles)

    def forward(self):
        saved = self.saved
        saved["attended"], saved["weights"] = attention(self.counts, saved["qkv"], self.bias)
        names = ("branch", "middle", "normed2", "activ", "slope", "mlp_out")
        result, *kept = mlp(saved["attended"], saved["hidden"], self.vectors, saved["tiles"])
        saved.update(zip(names, kept))
        return result

    def back_mlp(self, grad):
        return mlp_back(grad, self.saved, self.vectors, self.saved["tiles"])

    def back_attention(self, passed):
        return attention_back(self.saved["qkv"], passed[1], self.saved["weights"])

    def back_weights(self, passed, grad_project, stepwise):
        _, _, grad_mlp, grad_pre, grad_branch, _ = passed
        saved = self.saved
        ins = [saved["normed"], grad_project, saved["attended"], grad_branch, saved["normed2"], grad_pre]
        return weight_back(self.places, self.position, stepwise, ins + [saved["activ"], grad_mlp])

    def back_input(self, passed, grad_project):
        return input_back(grad_project, passed[0], self.saved["hidden"], self.vectors, self.saved["tiles"])


def scatter_whole(parts):
    whole = parts[0].reshape(-1, LANES)
    return lax.psum_scatter(whole, AXES, scatter_dimension=0, tiled=True).astype(jnp.float32)


def local(dp, fsdp, tokens, counts, params_first, params_second, cotangent):
    devices = dp * fsdp
    places = Places(dp, fsdp)
    stepwise = TILES % (4 * devices) == 0 and all(size & (size - 1) == 0 for size in places.sizes.values())
    share_rows = TILES * TILE // devices
    me = lax.axis_index(AXES)
    position = places.position(me)
    owned = Owned([params_first, params_second], me, devices)
    own = owned.share(0)
    small_rows = owned.small_rows(own)
    hidden, grad_output = pad_rows(tokens), pad_rows(cotangent)

    if stepwise:
        own = own.reshape(-1, TILE, LANES)
        column = fetch_column(places, own)
        near, small_rows = tie(group_of([own], [offset_of()]), small_rows)
        small_rows = small_rows.reshape(-1, TILE, LANES)
        near_first, small_rows = fetch_plane_with(places, near, 0, small_rows)
        near_first, small_rows = tie(near_first, small_rows)
        near_second, small_rows = fetch_plane_with(places, merge(near, near_first), 1, small_rows)
        small_rows = places.total(small_rows, "c")
        next_own, near_first = tie(owned.share(1, own), near_first)
        far, near_second = tie(group_of(column, column_offsets(places)[1:]), near_second)
        far_first = fetch_plane(places, far, 0)
        next_own, small_rows, far, hidden, grad_output = tie(next_own, small_rows, far, hidden, grad_output)
        next_own = jnp.concatenate([next_own, small_rows.reshape(-1, LANES)], axis=0)
        next_shares = [next_own] + fetch_column(places, next_own)
        small_rows = sum([rows[share_rows:] for rows in next_shares[1:]], next_own[share_rows:])
        small_rows = small_rows.reshape(2, -1, LANES)
        vectors = small_rows.astype(jnp.float32)
        next_shares = [rows[:share_rows].reshape(-1, TILE, LANES) for rows in next_shares]
        group = group_of(next_shares, column_offsets(places))
        far_second = fetch_plane(places, merge(far, far_first), 1)
        early = gather_core(places, [near, near_first, near_second, far, far_first])
    else:
        small_rows = lax.psum(small_rows, AXES)
    if stepwise:
        far_second, early, group, small_rows, vectors = tie(far_second, early, group, small_rows, vectors)
        first = fetch_plane(places, group, 0)
        parts = fetch_core(places, early) + fetch_core(places, list_core(places, [far_second]))
        entries = table_entries(small_rows)
        first_layer = Layer(places, position, counts, vectors[0])
        first_layer.bias, second_bias = bias_of(entries[0]), bias_of(entries[1])
        first, group, parts, first_layer.bias, second_bias = tie(first, group, parts, first_layer.bias, second_bias)
        second_group = merge(group, first)
        second = fetch_plane(places, second_group, 1)
        parts, _ = tie(parts, second_group)
        next_parts = fetch_core(places, list_core(places, [first]))
        first_layer.project(hidden, parts)
        result = first_layer.forward()
        next_parts, result = tie(next_parts, result)
        next_parts += fetch_core(places, gather_core(places, [group]))
        second, next_parts, result, second_bias = tie(second, next_parts, result, second_bias)
        next_parts += fetch_core(places, list_core(places, [second]))
    else:
        vectors = small_rows.astype(jnp.float32)
        entries = table_entries(small_rows)
        second_bias = bias_of(entries[1])
        parts, next_parts = [
            [(lax.all_gather(share, AXES, axis=0, tiled=True).reshape(TILES, TILE, LANES), [None])]
            for share in (own, owned.share(1))
        ]
        first_layer = Layer(places, position, counts, vectors[0])
        first_layer.project(hidden, parts)
        first_layer.bias = bias_of(entries[0])
        result = first_layer.forward()
    second_layer = Layer(places, position, counts, vectors[1])
    second_layer.bias = second_bias
    second_layer.project(result, next_parts)
    result = second_layer.forward()
    output = cut_rows(result)

    next_passed = second_layer.back_mlp(grad_output)
    next_project, next_bias = second_layer.back_attention(next_passed)
    parts = second_layer.back_weights(next_passed, next_project, stepwise)
    if stepwise:
        sums = send_core(places, parts)
    else:
        next_share = scatter_whole(parts)
    grad, next_sums = second_layer.back_input(next_passed, next_project)
    if stepwise:
        sums, grad = send_plane_tied(places, sums, 0, grad)
    passed = first_layer.back_mlp(grad)
    project_grad, bias = first_layer.back_attention(passed)
    parts = first_layer.back_weights(passed, project_grad, stepwise)
    if stepwise:
        sums, parts, passed, project_grad = tie(sums, parts, passed, project_grad)
        sums = send_plane(places, sums, 1)
        own_sums = send_core(places, parts)
    else:
        share = scatter_whole(parts)
    if stepwise:
        own_sums, later = send_plane_tied(places, own_sums, 0, (bias, passed, project_grad))
        sums, (bias, passed, project_grad) = tie(sums, later)
        sums = send_column(places, column_totals(places, sums))
    grad, own_row_sums = first_layer.back_input(passed, project_grad)
    small_grads = small_gradients(
        [own_row_sums, next_sums], [passed[5], next_passed[5]], tables_from_biases(bias, next_bias)
    )
    flat_share = FlatShare(me, devices, params_first.shape[0] * devices)
    if stepwise:
        own_sums, sums, small_grads = tie(own_sums, sums, small_grads)
        own_sums = send_plane(places, own_sums, 1)
        small_grads = places.total(small_grads, "zc")
        own_sums, small_grads = tie(own_sums, small_grads)
        own_sums = send_column(places, column_totals(places, own_sums))
        small_grads = places.total(small_grads, "xy")
        small_grads, sums = tie(small_grads, sums)
        grad_second = flat_share(add_low(*sums).reshape(-1, LANES), small_grads[1])
        own_sums, grad_second, output, grad_tokens = tie(own_sums, grad_second, output, cut_rows(grad))
        share = add_low(*own_sums).reshape(-1, LANES)
    else:
        small_grads = lax.psum(small_grads, AXES)
        grad_second = flat_share(next_share, small_grads[1])
        grad_tokens = cut_rows(grad)
    grad_first = flat_share(share, small_grads[0])
    return output, grad_tokens, grad_first, grad_second


def solution(mesh):
    return jax.shard_map(
        functools.partial(local, mesh.shape["dp"], mesh.shape["fsdp"]),
        mesh=mesh,
        in_specs=(P(AXES, None, None), P(AXES), P(AXES), P(AXES), P(AXES, None, None)),
        out_specs=(P(AXES, None, None), P(AXES, None, None), P(AXES), P(AXES)),
        check_vma=False,
    )
```

```python
import functools
import math

import jax
import jax.numpy as jnp
import numpy as np
from jax import lax
from jax.experimental import pallas as pl
from jax.experimental.pallas import tpu as pltpu
from jax.sharding import PartitionSpec as P

D = 768
HEADS = 12
HEAD = D // HEADS
FF = 3072
GRID = 14
SEQ = 197
RELS = 732
ROWS = 208
LANES = 128
TILE = 16
AXES = ("dp", "fsdp")
VMEM_LIMIT = 56 * 2**20

EPSILON = 1e-06
NEGATIVE = -1000000000.0

ENTRIES = [
    ("norm1_gain", (D,)),
    ("norm1_bias", (D,)),
    ("qkv_weight", (D, 3 * D)),
    ("query_bias", (D,)),
    ("value_bias", (D,)),
    ("relative_table", (RELS, HEADS)),
    ("proj_weight", (D, D)),
    ("proj_bias", (D,)),
    ("gamma_attn", (D,)),
    ("norm2_gain", (D,)),
    ("norm2_bias", (D,)),
    ("fc1_weight", (D, FF)),
    ("fc1_bias", (FF,)),
    ("fc2_weight", (FF, D)),
    ("fc2_bias", (D,)),
    ("gamma_mlp", (D,)),
]
WEIGHTS = {name: dims for name, dims in ENTRIES if name.endswith("weight")}
SIZES = dict(ENTRIES)
VECTORS = [
    "norm1_gain",
    "norm1_bias",
    "query_bias",
    "value_bias",
    "proj_bias",
    "gamma_attn",
    "norm2_gain",
    "norm2_bias",
    "fc2_bias",
    "gamma_mlp",
]
ROW = {name: i for i, name in enumerate(VECTORS)}


def count_rows(dims):
    return -(-math.prod(dims) // LANES)


def virtual_starts():
    starts, at = {}, 0
    for name, dims in ENTRIES:
        starts[name] = at
        at += count_rows(dims)
    return starts, at


STARTS, VIRTUAL = virtual_starts()
SHIFT = RELS * HEADS % LANES
TABLE_END = STARTS["proj_weight"]


def tile_order():
    parts = []
    for name, (depth, width) in WEIGHTS.items():
        across = width // LANES
        rows = STARTS[name] + np.arange(depth * across).reshape(depth // TILE, TILE, across)
        parts.append(rows.transpose(0, 2, 1).reshape(-1))
    return np.concatenate(parts)


def small_order():
    groups = [VECTORS, ["fc1_bias"], ["relative_table"]]
    rows = []
    for group in groups:
        for name in group:
            rows += [STARTS[name] + i for i in range(count_rows(SIZES[name]))]
        rows += [-1] * (-len(rows) % 8)
    return np.array(rows)


TILE_ROWS = tile_order()
SMALL_ROWS = small_order()
TILES = len(TILE_ROWS) // TILE


def tie(*trees):
    leaves, structure = jax.tree.flatten(trees)
    tied = iter(lax.optimization_barrier([leaf for leaf in leaves if isinstance(leaf, jax.Array)]))
    return structure.unflatten([next(tied) if isinstance(leaf, jax.Array) else leaf for leaf in leaves])


def halo(block, before, after, devices, join=True):
    rows = block.shape[-2]
    pieces = [block] if join else []
    for hop in range(1, -(-before // rows) + 1):
        take = min(rows, before - (hop - 1) * rows)
        perm = [(i, i + hop) for i in range(devices - hop)]
        pieces.insert(0, lax.ppermute(block[..., rows - take :, :], AXES, perm))
    for hop in range(1, -(-after // rows) + 1):
        take = min(rows, after - (hop - 1) * rows)
        perm = [(i + hop, i) for i in range(devices - hop)]
        pieces.append(lax.ppermute(block[..., :take, :], AXES, perm))
    return jnp.concatenate(pieces, axis=-2)


def pick_rows(index, source):
    chosen = index[:, None] == lax.broadcasted_iota(jnp.int32, (1, source.shape[0]), 1)
    return jnp.dot(chosen.astype(jnp.bfloat16), source.astype(jnp.bfloat16), preferred_element_type=jnp.float32)


def round_up(value, unit):
    return -(-value // unit) * unit


class Owned:
    def __init__(self, flats, me, devices):
        length = flats[0].shape[0] // LANES
        share = len(TILE_ROWS) // devices
        starts = np.arange(devices)[:, None] * length
        wanted = TILE_ROWS.reshape(devices, share) - starts
        before = round_up(max(0, -wanted.min()) + 1, TILE)
        after = round_up(max(0, wanted.max() + 1 - length), TILE)
        smalls = SMALL_ROWS[None] - starts
        smalls = np.where((smalls >= 0) & (smalls < length), smalls + before - 1, -1)
        self.wanted = self.mine(wanted + before - 1, me)
        self.smalls = self.mine(smalls, me)
        around = halo(jnp.stack([flat.reshape(length, LANES) for flat in flats]), before, after, devices)
        shifted = jnp.concatenate([around[:, :-1, SHIFT:], around[:, 1:, :SHIFT]], axis=2)
        at = me * length - before + 1 + lax.broadcasted_iota(jnp.int32, (1, shifted.shape[1], 1), 1)
        self.virtual = jnp.where(at < TABLE_END, around[:, 1:], shifted)

    @staticmethod
    def mine(table, me):
        return lax.dynamic_index_in_dim(jnp.asarray(table.astype(np.int32)), me, 0, keepdims=False)

    def small_rows(self, *after):
        virtual, *_ = tie(self.virtual, *after)
        return jnp.stack([pick_rows(self.smalls, rows).astype(jnp.bfloat16) for rows in virtual])

    def share(self, number, *after):
        rows = self.virtual[number]
        if after:
            rows, *_ = tie(rows, *after)
        return pick_rows(self.wanted, rows).astype(jnp.bfloat16)


class FlatShare:
    def __init__(self, me, devices, flat_length):
        length = flat_length // LANES // devices
        share = len(TILE_ROWS) // devices
        place = np.full(max(VIRTUAL, devices * length + 1), -1, np.int64)
        place[TILE_ROWS] = np.arange(len(TILE_ROWS))
        small_place = np.full(place.shape, -1, np.int64)
        small_place[SMALL_ROWS[SMALL_ROWS >= 0]] = np.flatnonzero(SMALL_ROWS >= 0)
        span = np.arange(devices)[:, None] * length + np.arange(length + 1)[None]
        relative = place[span] - np.arange(devices)[:, None] * share
        has = place[span] >= 0
        self.before = round_up(max(0, -relative[has].min()), TILE)
        self.after = round_up(max(0, relative[has].max() + 1 - share), TILE)
        smalls_at = self.before + share + self.after
        index = np.where(has, relative + self.before, -1)
        index = np.where(small_place[span] >= 0, small_place[span] + smalls_at, index)
        self.index = Owned.mine(index, me)
        self.at = me * length + lax.broadcasted_iota(jnp.int32, (length, 1), 0)
        self.devices = devices

    def __call__(self, owned, smalls):
        owned = owned.astype(jnp.bfloat16)
        share = owned.shape[0]
        around = halo(owned, self.before, self.after, self.devices, join=False)
        ends = self.before + share
        here = jnp.concatenate([owned, smalls.astype(jnp.bfloat16)], axis=0)
        index = self.index - self.before
        outside = (self.index < self.before) | ((self.index >= ends) & (self.index < ends + self.after))
        index = jnp.where(outside, -1, jnp.where(self.index >= ends, index - self.after, index))
        virtual = pick_rows(index, here)
        index = jnp.where(self.index < self.before, self.index, self.index - share)
        index = jnp.where(outside, index, -1)
        virtual = virtual + pick_rows(index, around)
        here, following = virtual[:-1], virtual[1:]
        lane = lax.broadcasted_iota(jnp.int32, (1, LANES), 1)
        shifted = jnp.concatenate([here[:, LANES - SHIFT :], following[:, : LANES - SHIFT]], axis=1)
        straight = (self.at < TABLE_END - 1) | ((self.at == TABLE_END - 1) & (lane < SHIFT))
        return jnp.where(straight, here, shifted).reshape(-1)


VECTOR_ROWS = D // LANES
FC1_AT = round_up(len(VECTORS) * VECTOR_ROWS, 8)
TABLE_AT = FC1_AT + FF // LANES
TABLE_ROWS = count_rows(SIZES["relative_table"])
LATER = 4


def table_entries(rows):
    tables = rows[:, TABLE_AT : TABLE_AT + TABLE_ROWS].reshape(2, -1)[:, : RELS * HEADS].reshape(2, RELS, HEADS)
    return jnp.pad(tables.transpose(0, 2, 1), ((0, 0), (0, 16 - HEADS), (0, ENTRY_LANES - RELS)))


def small_gradients(first, later, tables):
    tables = tables.reshape(2, RELS * HEADS)
    tables = jnp.pad(tables, ((0, 0), (0, round_up(TABLE_ROWS, 8) * LANES - RELS * HEADS))).reshape(2, -1, LANES)
    return jnp.concatenate([jnp.stack(first), jnp.stack(later), tables], axis=1)


SIDE = 2 * GRID - 1
WINDOW = round_up(SIDE * GRID, LANES) + LANES
WIDE = round_up(ROWS, LANES)


ENTRY_LANES = round_up(RELS, LANES)
HEAD_ROWS = 2 * 16


def entry_choice(column, transposed):
    shape = (1, WINDOW) if transposed else (WINDOW, 1)
    source = lax.broadcasted_iota(jnp.int32, shape, 1 if transposed else 0)
    group = source // GRID
    target = (SIDE - 1 - group) * SIDE - (source - group * GRID) + GRID - 1 + column
    target = jnp.where(source < SIDE * GRID, target, -1)
    entries = (ENTRY_LANES, 1) if transposed else (1, ENTRY_LANES)
    entry = lax.broadcasted_iota(jnp.int32, entries, 0 if transposed else 1)
    return (entry == target).astype(jnp.float32).astype(jnp.bfloat16)


def bias_kernel(entries_ref, bias_ref, windows_ref):
    for column in range(GRID):
        windows_ref[column] = product(entries_ref[...], entry_choice(column, True), NN)
    lane = lax.broadcasted_iota(jnp.int32, (1, WIDE), 1)
    inner = (lane >= 1) & (lane < SEQ)

    def head(i, _):
        ends = entries_ref[pl.ds(pl.multiple_of(i // 16 * 16, 16), 16), :].astype(jnp.float32)
        picked = lax.broadcasted_iota(jnp.int32, (16, 1), 0) == i % 16
        ends = jnp.sum(jnp.where(picked, ends, 0.0), axis=0, keepdims=True)
        top, left, corner = [ends[:, RELS - k : RELS - k + 1] for k in (3, 2, 1)]
        bias_ref[i] = jnp.zeros(bias_ref.shape[1:], jnp.float32)
        bias_ref[i, 0:1] = jnp.where(inner, top, jnp.where(lane == 0, corner, 0.0))[:, :ROWS]
        spread = jnp.concatenate([windows_ref[column, pl.ds(i, 1)] for column in range(GRID)], axis=0)
        for row in range(GRID):
            start = (GRID - 1 - row) * GRID
            window = pltpu.roll(spread, (1 - start) % WINDOW, 1)[:, :WIDE]
            window = jnp.where(inner, window, jnp.where(lane == 0, left, 0.0))
            bias_ref[i, 1 + row * GRID : 1 + (row + 1) * GRID] = window[:, :ROWS]
        return 0

    lax.fori_loop(0, HEADS, head, 0)


def bias_of(entries):
    return pl.pallas_call(
        bias_kernel,
        grid=(1,),
        in_specs=[pl.BlockSpec(entries.shape, lambda i: (0, 0))],
        out_specs=pl.BlockSpec((HEADS, ROWS, ROWS), lambda i: (0, 0, 0)),
        out_shape=jax.ShapeDtypeStruct((HEADS, ROWS, ROWS), jnp.float32),
        scratch_shapes=[pltpu.VMEM((GRID, 16, WINDOW), jnp.float32)],
        compiler_params=pltpu.CompilerParams(vmem_limit_bytes=VMEM_LIMIT),
        name="bias",
    )(entries)


def table_kernel(first_ref, second_ref, out_ref, windows_ref, ends_ref):
    lane = lax.broadcasted_iota(jnp.int32, (1, ROWS), 1)
    inner = (lane >= 1) & (lane < SEQ)
    entry = lax.broadcasted_iota(jnp.int32, (1, ENTRY_LANES), 1)
    windows_ref[...] = jnp.zeros_like(windows_ref)
    ends_ref[...] = jnp.zeros_like(ends_ref)
    for number, grad_ref in enumerate((first_ref, second_ref)):

        def head(i, _, number=number, grad_ref=grad_ref):
            total = jnp.zeros((GRID, WINDOW), jnp.float32)
            left = jnp.zeros((1, 1), jnp.float32)
            for row in range(GRID):
                start = (GRID - 1 - row) * GRID
                block = grad_ref[i, 1 + row * GRID : 1 + (row + 1) * GRID]
                left = left + jnp.sum(jnp.where(lane == 0, block, 0.0), keepdims=True)
                block = jnp.where(inner, block, 0.0)
                block = jnp.concatenate([block, jnp.zeros((GRID, WINDOW - ROWS), jnp.float32)], axis=1)
                total = total + pltpu.roll(block, (start - 1) % WINDOW, 1)
            at = pl.ds(number * 16 + i, 1)
            for column in range(GRID):
                windows_ref[column, at] = total[column : column + 1]
            first = grad_ref[i, 0:1]
            top = jnp.sum(jnp.where(inner, first, 0.0), keepdims=True)
            corner = jnp.sum(jnp.where(lane == 0, first, 0.0), keepdims=True)
            ends = jnp.where(entry == RELS - 3, top, jnp.where(entry == RELS - 2, left, 0.0))
            ends_ref[at] = jnp.where(entry == RELS - 1, corner, ends)
            return 0

        lax.fori_loop(0, HEADS, head, 0)
    out_ref[...] = ends_ref[...]
    for column in range(GRID):
        rows = windows_ref[column]
        high = rows.astype(jnp.bfloat16)
        low = (rows - high.astype(jnp.float32)).astype(jnp.bfloat16)
        chosen = entry_choice(column, False)
        out_ref[...] += product(high, chosen, NN) + product(low, chosen, NN)


def tables_from_biases(first, second):
    entries = pl.pallas_call(
        table_kernel,
        grid=(1,),
        in_specs=[pl.BlockSpec(first.shape, lambda i: (0, 0, 0))] * 2,
        out_specs=pl.BlockSpec((HEAD_ROWS, ENTRY_LANES), lambda i: (0, 0)),
        out_shape=jax.ShapeDtypeStruct((HEAD_ROWS, ENTRY_LANES), jnp.float32),
        scratch_shapes=[
            pltpu.VMEM((GRID, HEAD_ROWS, WINDOW), jnp.float32),
            pltpu.VMEM((HEAD_ROWS, ENTRY_LANES), jnp.float32),
        ],
        compiler_params=pltpu.CompilerParams(vmem_limit_bytes=VMEM_LIMIT),
        name="table_back",
    )(first, second)
    return entries.reshape(2, 16, ENTRY_LANES)[:, :HEADS, :RELS].transpose(0, 2, 1)


NT = (((1,), (1,)), ((), ()))
NN = (((1,), (0,)), ((), ()))
TN = (((0,), (0,)), ((), ()))


def product(left, right, dims):
    return lax.dot_general(left, right, dims, preferred_element_type=jnp.float32)


def own_lanes(head):
    lane = lax.broadcasted_iota(jnp.int32, (1, LANES), 1)
    return lane < HEAD if head == 0 else lane >= HEAD


def head_weights(query, key, bias, count, head):
    chosen = jnp.where(own_lanes(head), query, jnp.zeros_like(query))
    scores = product(chosen, key, NT) + bias
    column = lax.broadcasted_iota(jnp.int32, (1, ROWS), 1)
    scores = jnp.where(column < count, scores, NEGATIVE)
    grown = jnp.exp(scores - jnp.max(scores, axis=1, keepdims=True))
    return grown * (1.0 / jnp.sum(grown, axis=1, keepdims=True))


def attention_kernel(pairs, counts_ref, query_ref, key_ref, value_ref, bias_ref, out_ref, weights_ref):
    count = counts_ref[pl.program_id(1)]
    for pair in range(pairs):
        lanes = slice(pair * LANES, (pair + 1) * LANES)
        query, key, value = query_ref[:, lanes], key_ref[:, lanes], value_ref[:, lanes]
        parts = []
        for head in range(2):
            weights = head_weights(query, key, bias_ref[2 * pair + head], count, head).astype(jnp.bfloat16)
            weights_ref[0, 2 * pair + head] = weights
            parts.append(product(weights, value, NN))
        out_ref[:, lanes] = jnp.where(own_lanes(0), parts[0], parts[1]).astype(jnp.bfloat16)


def attention_back_kernel(pairs, query_ref, key_ref, value_ref, grad_ref, weights_ref, out_ref, db_ref):
    image = pl.program_id(1)

    @pl.when(image == 0)
    def _():
        db_ref[...] = jnp.zeros_like(db_ref)

    for pair in range(pairs):
        lanes = slice(pair * LANES, (pair + 1) * LANES)
        query, key, value, grad = query_ref[:, lanes], key_ref[:, lanes], value_ref[:, lanes], grad_ref[:, lanes]
        dq, dk, dv = [], [], []
        for head in range(2):
            low_weights = weights_ref[0, 2 * pair + head]
            weights = low_weights.astype(jnp.float32)
            chosen = jnp.where(own_lanes(head), grad, jnp.zeros_like(grad))
            weighted = weights * product(chosen, value, NT)
            dv.append(product(low_weights, grad, TN))
            grad_scores = weighted - weights * jnp.sum(weighted, axis=1, keepdims=True)
            low = grad_scores.astype(jnp.bfloat16)
            dq.append(product(low, key, NN))
            dk.append(product(low, query, TN))
            db_ref[2 * pair + head] += grad_scores
        first = own_lanes(0)
        out_ref[0, :, lanes] = (jnp.where(first, dq[0], dq[1]) * HEAD**-0.5).astype(jnp.bfloat16)
        out_ref[1, :, lanes] = jnp.where(first, dk[0], dk[1]).astype(jnp.bfloat16)
        out_ref[2, :, lanes] = jnp.where(first, dv[0], dv[1]).astype(jnp.bfloat16)


def attention_specs(pairs):
    steps = D // LANES // pairs
    lanes = [
        pl.BlockSpec((ROWS, pairs * LANES), lambda step, image, *_, part=part: (image, part * steps + step))
        for part in range(3)
    ]
    bias = pl.BlockSpec((2 * pairs, ROWS, ROWS), lambda step, image, *_: (step, 0, 0))
    weights = pl.BlockSpec((1, 2 * pairs, ROWS, ROWS), lambda step, image, *_: (image, step, 0, 0))
    return steps, lanes, bias, weights


def attention(counts, qkv, bias, pairs=6):
    images = qkv.shape[0] // ROWS
    steps, lanes, bias_spec, weights_spec = attention_specs(pairs)
    return pl.pallas_call(
        functools.partial(attention_kernel, pairs),
        grid_spec=pltpu.PrefetchScalarGridSpec(
            num_scalar_prefetch=1,
            grid=(steps, images),
            in_specs=lanes + [bias_spec],
            out_specs=[lanes[0], weights_spec],
        ),
        out_shape=[
            jax.ShapeDtypeStruct((qkv.shape[0], D), jnp.bfloat16),
            jax.ShapeDtypeStruct((images, HEADS, ROWS, ROWS), jnp.bfloat16),
        ],
        compiler_params=pltpu.CompilerParams(vmem_limit_bytes=VMEM_LIMIT),
        name="attention",
    )(counts, qkv, qkv, qkv, bias)


def attention_back(qkv, grad, weights, pairs=3):
    images = qkv.shape[0] // ROWS
    steps, lanes, bias_spec, weights_spec = attention_specs(pairs)
    return pl.pallas_call(
        functools.partial(attention_back_kernel, pairs),
        grid=(steps, images),
        in_specs=lanes + [lanes[0], weights_spec],
        out_specs=[
            pl.BlockSpec((3, ROWS, pairs * LANES), lambda step, image: (0, image, step)),
            bias_spec,
        ],
        out_shape=[
            jax.ShapeDtypeStruct((3, qkv.shape[0], D), jnp.bfloat16),
            jax.ShapeDtypeStruct((HEADS, ROWS, ROWS), jnp.float32),
        ],
        compiler_params=pltpu.CompilerParams(vmem_limit_bytes=VMEM_LIMIT),
        name="attention_back",
    )(qkv, qkv, qkv, grad, weights)


def tile_starts():
    starts, at = {}, 0
    for name, (depth, width) in WEIGHTS.items():
        starts[name] = at
        at += depth // TILE * (width // LANES)
    return starts


FIRST = tile_starts()
MLP_FIRST = FIRST["proj_weight"]
SPAN = 1024


def load_weight(ref, base, name, row, rows, column, columns):
    first, across = FIRST[name] - base, WEIGHTS[name][1] // LANES
    lines = []
    for i in range(rows):
        at = first + (row + i) * across + column
        lines.append(jnp.concatenate([ref[at + j] for j in range(columns)], axis=1))
    return jnp.concatenate(lines, axis=0)


def gelu_and_slope(values):
    size = jnp.abs(values)
    step = 1.0 / (1.0 + (0.3275911 / math.sqrt(2.0)) * size)
    bell = jnp.exp(-0.5 * values * values)
    series = 1.061405429
    for term in (-1.453152027, 1.421413741, -0.284496736, 0.254829592):
        series = series * step + term
    tail = 0.5 * series * step * bell
    area = jnp.where(values < 0, tail, 1.0 - tail)
    return values * area, area + values * bell * (1.0 / math.sqrt(2.0 * math.pi))


def norm_parts(values):
    centre = values - jnp.mean(values, axis=-1, keepdims=True)
    spread = jnp.mean(centre * centre, axis=-1, keepdims=True)
    inverse = lax.rsqrt(spread + EPSILON)
    return centre * inverse, inverse


def norm_back(grad, normal, inverse, gain):
    scaled = grad * gain
    first = jnp.mean(scaled, axis=-1, keepdims=True)
    second = jnp.mean(scaled * normal, axis=-1, keepdims=True)
    return (scaled - first - normal * second) * inverse


def wide_row(ref, first, count):
    return jnp.concatenate([ref[first + i : first + i + 1] for i in range(count)], axis=1)


def vector(ref, name):
    return wide_row(ref, ROW[name] * VECTOR_ROWS, VECTOR_ROWS)


def put_vector(ref, row, values):
    sums = jnp.sum(values, axis=0, keepdims=True)
    for i in range(sums.shape[1] // LANES):
        ref[row + i : row + i + 1] = sums[:, i * LANES : (i + 1) * LANES]


def later_row(name):
    return (ROW[name] - LATER) * VECTOR_ROWS


def whole_spec(shape):
    return pl.BlockSpec(shape, lambda *_: (0,) * len(shape))


ANYWHERE = pl.BlockSpec(memory_space=pl.ANY)
PARAMS = pltpu.CompilerParams(vmem_limit_bytes=VMEM_LIMIT)


def low_like(*shape):
    return jax.ShapeDtypeStruct(shape, jnp.bfloat16)


def full_like(*shape):
    return jax.ShapeDtypeStruct(shape, jnp.float32)


def project_kernel(places, slots, at_ref, *refs):
    parts, refs = refs[: len(slots)], refs[len(slots) :]
    hidden_ref, vectors_ref, normed_ref, qkv_ref, tiles_ref, whole_ref, sems, out_sem = refs
    copies = copies_in(places, at_ref, parts, slots, whole_ref, sems)
    for copy in copies:
        copy.start()
    normal, _ = norm_parts(hidden_ref[...])
    normed_ref[...] = (normal * vector(vectors_ref, "norm1_gain") + vector(vectors_ref, "norm1_bias")).astype(
        jnp.bfloat16
    )
    for copy in copies:
        copy.wait()
    leaving = pltpu.make_async_copy(whole_ref, tiles_ref, out_sem)
    leaving.start()
    across = D // LANES
    for part in range(3):
        weight = load_weight(whole_ref, 0, "qkv_weight", 0, D // TILE, part * across, across)
        rows = product(normed_ref[...], weight, NN)
        if part == 0:
            rows = (rows + vector(vectors_ref, "query_bias")) * HEAD**-0.5
        if part == 2:
            rows = rows + vector(vectors_ref, "value_bias")
        qkv_ref[:, part * D : (part + 1) * D] = rows.astype(jnp.bfloat16)
    leaving.wait()


def project(places, position, parts, hidden, vectors):
    arrays = [array for array, _ in parts]
    slots = [listed for _, listed in parts]
    rows = hidden.shape[0]
    return pl.pallas_call(
        functools.partial(project_kernel, places, slots),
        grid_spec=pltpu.PrefetchScalarGridSpec(
            num_scalar_prefetch=1,
            grid=(1,),
            in_specs=[ANYWHERE] * len(arrays) + [whole_spec((rows, D)), whole_spec(vectors.shape)],
            out_specs=[whole_spec((rows, D)), whole_spec((rows, 3 * D)), ANYWHERE],
            scratch_shapes=[
                pltpu.VMEM((TILES, TILE, LANES), jnp.bfloat16),
                pltpu.SemaphoreType.DMA((sum(len(listed) for listed in slots),)),
                pltpu.SemaphoreType.DMA(()),
            ],
        ),
        out_shape=[low_like(rows, D), low_like(rows, 3 * D), low_like(TILES, TILE, LANES)],
        compiler_params=PARAMS,
        name="project",
    )(position, *arrays, hidden, vectors)


def mlp_weights(tiles_ref, weight_ref, sems, order):
    copies = []
    for i, name in enumerate(order):
        depth, width = WEIGHTS[name]
        count = depth // TILE * (width // LANES)
        here = weight_ref.at[pl.ds(FIRST[name] - MLP_FIRST, count)]
        copies.append(pltpu.make_async_copy(tiles_ref.at[pl.ds(FIRST[name], count)], here, sems.at[i]))
        copies[-1].start()
    return copies


def span_of(step):
    return slice(step * SPAN, (step + 1) * SPAN)


class Leaving:
    def __init__(self, outs, buffers, sems):
        self.outs, self.buffers, self.sems, self.copies = outs, buffers, sems, []

    def start(self, number, columns=None):
        source, target = self.buffers[number], self.outs[number]
        if columns is not None:
            source, target = source.at[:, columns], target.at[:, columns]
        self.copies.append(pltpu.make_async_copy(source, target, self.sems.at[len(self.copies)]))
        self.copies[-1].start()

    def wait(self):
        for copy in self.copies:
            copy.wait()


def mlp_kernel(attended_ref, hidden_ref, vectors_ref, tiles_ref, *refs):
    outs, buffers, (total_ref, weight_ref, sems, out_sems, fc1_bias_ref) = refs[:7], refs[7:14], refs[14:]
    result_ref, branch_ref, middle_ref, normed_ref, activ_ref, slope_ref, mlp_ref = buffers
    leaving = Leaving(outs, buffers, out_sems)
    copies = mlp_weights(tiles_ref, weight_ref, sems, ("proj_weight", "fc1_weight", "fc2_weight"))
    fc1_bias_ref[...] = wide_row(vectors_ref, FC1_AT, FF // LANES)
    copies[0].wait()
    across = D // LANES
    weight = load_weight(weight_ref, MLP_FIRST, "proj_weight", 0, D // TILE, 0, across)
    branch = product(attended_ref[...], weight, NN) + vector(vectors_ref, "proj_bias")
    branch_ref[...] = branch.astype(jnp.bfloat16)
    leaving.start(1)
    middle_ref[...] = hidden_ref[...] + vector(vectors_ref, "gamma_attn") * branch
    leaving.start(2)
    normal, _ = norm_parts(middle_ref[...])
    normed_ref[...] = (normal * vector(vectors_ref, "norm2_gain") + vector(vectors_ref, "norm2_bias")).astype(
        jnp.bfloat16
    )
    leaving.start(3)
    total_ref[...] = jnp.broadcast_to(vector(vectors_ref, "fc2_bias"), total_ref.shape)
    copies[1].wait()

    def step(i, _):
        span = span_of(i)
        weight = load_weight(weight_ref, MLP_FIRST, "fc1_weight", 0, D // TILE, i * (SPAN // LANES), SPAN // LANES)
        activ, slope = gelu_and_slope(product(normed_ref[...], weight, NN) + fc1_bias_ref[:, span])
        activ = activ.astype(jnp.bfloat16)
        activ_ref[:, span] = activ
        slope_ref[:, span] = slope.astype(jnp.bfloat16)
        leaving.start(4, span)
        leaving.start(5, span)
        if i == 0:
            copies[2].wait()
        weight = load_weight(weight_ref, MLP_FIRST, "fc2_weight", i * (SPAN // TILE), SPAN // TILE, 0, across)
        total_ref[...] += product(activ, weight, NN)
        return 0

    for i in range(FF // SPAN):
        step(i, 0)
    result_ref[...] = middle_ref[...] + vector(vectors_ref, "gamma_mlp") * total_ref[...]
    leaving.start(0)
    mlp_ref[...] = total_ref[...].astype(jnp.bfloat16)
    leaving.start(6)
    leaving.wait()


def mlp_scratch(rows, outs):
    return [pltpu.VMEM(out.shape, out.dtype) for out in outs] + [
        pltpu.VMEM((rows, D), jnp.float32),
        pltpu.VMEM((TILES - MLP_FIRST, TILE, LANES), jnp.bfloat16),
        pltpu.SemaphoreType.DMA((3,)),
        pltpu.SemaphoreType.DMA((len(outs) + 2 * (FF // SPAN),)),
    ]


def mlp(attended, hidden, vectors, tiles):
    rows = hidden.shape[0]
    outs = [full_like(rows, D), low_like(rows, D), full_like(rows, D), low_like(rows, D)]
    outs += [low_like(rows, FF), low_like(rows, FF), low_like(rows, D)]
    ins = [attended, hidden, vectors]
    return pl.pallas_call(
        mlp_kernel,
        grid=(1,),
        in_specs=[whole_spec(array.shape) for array in ins] + [ANYWHERE],
        out_specs=[ANYWHERE] * len(outs),
        out_shape=outs,
        scratch_shapes=mlp_scratch(rows, outs) + [pltpu.VMEM((1, FF), jnp.float32)],
        compiler_params=PARAMS,
        name="mlp",
    )(*ins, tiles)


def mlp_back_kernel(grad_ref, branch_ref, middle_ref, slope_ref, mlp_ref, vectors_ref, tiles_ref, *refs):
    outs, buffers, (total_ref, weight_ref, sems, out_sems) = refs[:6], refs[6:12], refs[12:]
    grad_middle_ref, grad_attended_ref, grad_mlp_ref, grad_pre_ref, grad_branch_ref, sums_ref = buffers
    leaving = Leaving(outs, buffers, out_sems)
    copies = mlp_weights(tiles_ref, weight_ref, sems, ("fc2_weight", "fc1_weight", "proj_weight"))
    across = D // LANES
    grad = grad_ref[...]
    sums_ref[...] = jnp.zeros_like(sums_ref)
    put_vector(sums_ref, later_row("gamma_mlp"), grad * mlp_ref[...].astype(jnp.float32))
    grad_mlp = grad * vector(vectors_ref, "gamma_mlp")
    put_vector(sums_ref, later_row("fc2_bias"), grad_mlp)
    grad_mlp_ref[...] = grad_mlp.astype(jnp.bfloat16)
    leaving.start(2)
    total_ref[...] = jnp.zeros_like(total_ref)
    copies[0].wait()

    def step(i, _):
        span = span_of(i)
        weight = load_weight(weight_ref, MLP_FIRST, "fc2_weight", i * (SPAN // TILE), SPAN // TILE, 0, across)
        grad_pre = product(grad_mlp_ref[...], weight, NT) * slope_ref[:, span].astype(jnp.float32)
        sums = jnp.sum(grad_pre, axis=0, keepdims=True)
        sums = jnp.concatenate([sums[:, k * LANES : (k + 1) * LANES] for k in range(SPAN // LANES)], axis=0)
        first = FC1_AT - LATER * VECTOR_ROWS + i * (SPAN // LANES)
        sums_ref[first : first + SPAN // LANES] = sums
        grad_pre = grad_pre.astype(jnp.bfloat16)
        grad_pre_ref[:, span] = grad_pre
        leaving.start(3, span)
        if i == 0:
            copies[1].wait()
        weight = load_weight(weight_ref, MLP_FIRST, "fc1_weight", 0, D // TILE, i * (SPAN // LANES), SPAN // LANES)
        total_ref[...] += product(grad_pre, weight, NT)
        return 0

    for i in range(FF // SPAN):
        step(i, 0)
    normal, inverse = norm_parts(middle_ref[...])
    grad_normed = total_ref[...]
    put_vector(sums_ref, later_row("norm2_gain"), grad_normed * normal)
    put_vector(sums_ref, later_row("norm2_bias"), grad_normed)
    grad_middle = grad_ref[...] + norm_back(grad_normed, normal, inverse, vector(vectors_ref, "norm2_gain"))
    grad_middle_ref[...] = grad_middle
    leaving.start(0)
    put_vector(sums_ref, later_row("gamma_attn"), grad_middle * branch_ref[...].astype(jnp.float32))
    grad_branch = grad_middle * vector(vectors_ref, "gamma_attn")
    put_vector(sums_ref, later_row("proj_bias"), grad_branch)
    leaving.start(5)
    grad_branch_ref[...] = grad_branch.astype(jnp.bfloat16)
    leaving.start(4)
    copies[2].wait()
    weight = load_weight(weight_ref, MLP_FIRST, "proj_weight", 0, D // TILE, 0, across)
    grad_attended_ref[...] = product(grad_branch_ref[...], weight, NT).astype(jnp.bfloat16)
    leaving.start(1)
    leaving.wait()


def mlp_back(grad, saved, vectors, tiles):
    rows = grad.shape[0]
    outs = [full_like(rows, D), low_like(rows, D), low_like(rows, D), low_like(rows, FF), low_like(rows, D)]
    outs += [full_like(TABLE_AT - LATER * VECTOR_ROWS, LANES)]
    ins = [grad, saved["branch"], saved["middle"], saved["slope"], saved["mlp_out"], vectors]
    return pl.pallas_call(
        mlp_back_kernel,
        grid=(1,),
        in_specs=[whole_spec(array.shape) for array in ins] + [ANYWHERE],
        out_specs=[ANYWHERE] * len(outs),
        out_shape=outs,
        scratch_shapes=mlp_scratch(rows, outs),
        compiler_params=PARAMS,
        name="mlp_back",
    )(*ins, tiles)


def scatter_place(places, at_ref, device, part):
    position = np.unravel_index(device, places.grid.shape)
    apart = {name: at_ref[i] ^ int(position[i]) for name, i in places.axis.items()}
    first, second = ORDERS[part]
    slot = (apart[first] * places.sizes[second] + apart[second]) * places.sizes["z"] + apart["z"]
    return apart["c"], slot


def weight_back_kernel(places, stepwise, at_ref, *refs):
    sources, refs = refs[:8], refs[8:]
    outs = refs[: 2 * places.sizes["c"] if stepwise else 1]
    operands, (whole_ref, in_sems, sems) = refs[len(outs) : len(outs) + 8], refs[len(outs) + 8 :]
    coming = [
        pltpu.make_async_copy(source, operand, in_sems.at[i]) for i, (source, operand) in enumerate(zip(sources, operands))
    ]
    for copy in coming:
        copy.start()
    normed_ref, project_ref, attended_ref, branch_ref, normed2_ref, pre_ref, activ_ref, mlp_ref = operands
    across = D // LANES

    def put(name, row, column, left, grad):
        block = product(left, grad, TN).astype(jnp.bfloat16)
        wide = WEIGHTS[name][1] // LANES
        for i in range(D // TILE):
            for j in range(across):
                at = FIRST[name] + (row + i) * wide + column + j
                whole_ref[at] = block[i * TILE : (i + 1) * TILE, j * LANES : (j + 1) * LANES]

    half = TILES // places.count // 2
    sent = []

    def send(ready):
        while stepwise and (len(sent) + 1) * half <= ready:
            number = len(sent)
            core, slot = scatter_place(places, at_ref, number // 2, number % 2)
            source = whole_ref.at[pl.ds(number * half, half)]
            for k in range(places.sizes["c"]):
                target = outs[number % 2 * places.sizes["c"] + k].at[pl.ds(slot * half, half)]
                copy = pltpu.make_async_copy(source, target, sems.at[number])
                pl.when(core == k)(copy.start)
            sent.append(copy)

    coming[0].wait()
    coming[1].wait()
    for part in range(3):
        put("qkv_weight", 0, part * across, normed_ref[...], project_ref[part])
    send(FIRST["proj_weight"])
    coming[2].wait()
    coming[3].wait()
    put("proj_weight", 0, 0, attended_ref[...], branch_ref[...])
    send(FIRST["fc1_weight"])
    coming[4].wait()
    coming[5].wait()
    for part in range(FF // D):
        put("fc1_weight", 0, part * across, normed2_ref[...], pre_ref[:, part * D : (part + 1) * D])
    send(FIRST["fc2_weight"])
    coming[6].wait()
    coming[7].wait()
    for part in range(FF // D):
        put("fc2_weight", part * (D // TILE), 0, activ_ref[:, part * D : (part + 1) * D], mlp_ref[...])
        send(FIRST["fc2_weight"] + (part + 1) * (D // TILE) * across)
    if not stepwise:
        sent.append(pltpu.make_async_copy(whole_ref, outs[0], sems.at[0]))
        sent[0].start()
    for copy in sent:
        copy.wait()


def weight_back(places, position, stepwise, ins):
    cores = places.sizes["c"]
    counts = [TILES // (2 * cores)] * (2 * cores) if stepwise else [TILES]
    return pl.pallas_call(
        functools.partial(weight_back_kernel, places, stepwise),
        grid_spec=pltpu.PrefetchScalarGridSpec(
            num_scalar_prefetch=1,
            grid=(1,),
            in_specs=[ANYWHERE] * len(ins),
            out_specs=[ANYWHERE] * len(counts),
            scratch_shapes=[pltpu.VMEM(array.shape, array.dtype) for array in ins]
            + [
                pltpu.VMEM((TILES, TILE, LANES), jnp.bfloat16),
                pltpu.SemaphoreType.DMA((len(ins),)),
                pltpu.SemaphoreType.DMA((2 * places.count,)),
            ],
        ),
        out_shape=[low_like(count, TILE, LANES) for count in counts],
        compiler_params=PARAMS,
        name="weight_back",
    )(position, *ins)


def input_back_kernel(project_ref, grad_middle_ref, hidden_ref, vectors_ref, tiles_ref, out_ref, sums_ref, total_ref):
    across = D // LANES
    for part in range(3):
        weight = load_weight(tiles_ref, 0, "qkv_weight", 0, D // TILE, part * across, across)
        rows = product(project_ref[part], weight, NT)
        total_ref[...] = rows if part == 0 else total_ref[...] + rows
    normal, inverse = norm_parts(hidden_ref[...])
    grad_normed = total_ref[...]
    put_vector(sums_ref, 0, grad_normed * normal)
    put_vector(sums_ref, VECTOR_ROWS, grad_normed)
    put_vector(sums_ref, 2 * VECTOR_ROWS, project_ref[0].astype(jnp.float32))
    put_vector(sums_ref, 3 * VECTOR_ROWS, project_ref[2].astype(jnp.float32))
    out_ref[...] = grad_middle_ref[...] + norm_back(
        grad_normed, normal, inverse, vector(vectors_ref, "norm1_gain")
    )


def input_back(grad_project, grad_middle, hidden, vectors, tiles):
    rows = hidden.shape[0]
    ins = [grad_project, grad_middle, hidden, vectors]
    return pl.pallas_call(
        input_back_kernel,
        grid=(1,),
        in_specs=[whole_spec(array.shape) for array in ins] + [whole_spec((MLP_FIRST, TILE, LANES))],
        out_specs=[whole_spec((rows, D)), whole_spec((LATER * VECTOR_ROWS, LANES))],
        out_shape=[full_like(rows, D), full_like(LATER * VECTOR_ROWS, LANES)],
        scratch_shapes=[pltpu.VMEM((rows, D), jnp.float32)],
        compiler_params=PARAMS,
        name="input_back",
    )(*ins, tiles)


def pad_rows(images):
    padded = jnp.pad(images, ((0, 0), (0, ROWS - SEQ), (0, 0)))
    return padded.reshape(-1, D).astype(jnp.float32)


def cut_rows(rows):
    return rows.reshape(-1, ROWS, D)[:, :SEQ].astype(jnp.bfloat16)


class Places:
    def __init__(self, dp, fsdp):
        low = 2 if dp % 2 == 0 else 1
        core = 2 if fsdp % 2 == 0 else 1
        self.sizes = {"y": low, "x": dp // low, "z": fsdp // core, "c": core}
        self.count = dp * fsdp
        grid = np.arange(self.count).reshape(tuple(self.sizes.values()))
        self.grid = grid
        self.axis = {name: i for i, name in enumerate(self.sizes)}

    def exchange(self, block, axis, hop):
        size = self.sizes[axis]
        target = np.take(self.grid, np.arange(size) ^ hop, axis=self.axis[axis])
        perm = [(int(a), int(b)) for a, b in zip(self.grid.reshape(-1), target.reshape(-1))]
        return lax.ppermute(block, AXES, perm)

    def hops(self, axis):
        return range(1, self.sizes[axis])

    def powers(self, axis):
        return [1 << bit for bit in range(self.sizes[axis].bit_length() - 1)]

    def total(self, block, axes):
        for axis in axes:
            for hop in self.powers(axis):
                block = block + self.exchange(block, axis, hop)
        return block

    def position(self, me):
        return jnp.stack([(me // int(np.prod(self.grid.shape[i + 1 :]))) % n for i, n in enumerate(self.grid.shape)])


def block_at(at_ref, places, offset):
    number = 0
    for i, size in enumerate(places.grid.shape):
        number = number * size + (at_ref[i] ^ offset[i])
    return number


def copies_in(places, at_ref, parts, slots, whole_ref, sems):
    copies = []
    for part, listed in zip(parts, slots):
        count = part.shape[0] // len(listed)
        for i, slot in enumerate(listed):
            start = 0 if slot is None else block_at(at_ref, places, slot[0]) * (TILES // places.count) + slot[1]
            target = whole_ref.at[pl.ds(start, count)]
            copies.append(pltpu.make_async_copy(part.at[pl.ds(i * count, count)], target, sems.at[len(copies)]))
    return copies


def offset_of(**hops):
    return tuple(hops.get(axis, 0) for axis in ("y", "x", "z", "c"))


def join(blocks):
    return jnp.concatenate(blocks, axis=0) if len(blocks) > 1 else blocks[0]


ORDERS = (("x", "y"), ("y", "x"))


def group_of(shares, offsets):
    half = shares[0].shape[0] // 2
    return [(join([share[part * half : (part + 1) * half] for share in shares]), offsets) for part in range(2)]


def merge(*groups):
    return [(join([group[part][0] for group in groups]), sum((group[part][1] for group in groups), [])) for part in range(2)]


def fetch_column(places, share):
    return [places.exchange(share, "z", hop) for hop in places.hops("z")]


def column_offsets(places):
    return [offset_of(z=hop) for hop in range(places.sizes["z"])]


def fetch_plane(places, group, step):
    arrived = []
    for (block, offsets), order in zip(group, ORDERS):
        at = places.axis[order[step]]
        hops = range(1, places.sizes[order[step]])
        moved = [offset[:at] + (hop,) + offset[at + 1 :] for hop in hops for offset in offsets]
        arrived.append((join([places.exchange(block, order[step], hop) for hop in hops]), moved))
    return arrived


def fetch_plane_with(places, group, step, rows):
    (block, offsets), order = group[0], ORDERS[0]
    count, axis = block.shape[0], order[step]
    hops = range(1, places.sizes[axis])
    arrived = [places.exchange(jnp.concatenate([block, rows], axis=0), axis, hop) for hop in hops]
    moved = [tuple(hop if i == places.axis[axis] else part for i, part in enumerate(o)) for hop in hops for o in offsets]
    rows = sum([piece[count:] for piece in arrived], rows)
    other = fetch_plane(places, group, step)[1]
    return [(join([piece[:count] for piece in arrived]), moved), other], rows


def list_core(places, groups):
    parts = []
    for group in groups:
        half = TILES // places.count // 2
        parts += [(block, [(offset, part * half) for offset in offsets]) for part, (block, offsets) in enumerate(group)]
    return parts


def gather_core(places, groups):
    parts = list_core(places, groups)
    return [(join([block for block, _ in parts]), sum((slots for _, slots in parts), []))]


def fetch_core(places, parts):
    arrived = []
    for hop in range(1, places.sizes["c"]):
        for block, slots in parts:
            moved = [(offset[:3] + (hop,), first) for offset, first in slots]
            arrived.append((places.exchange(block, "c", hop), moved))
    return parts + arrived


def add_low(*blocks):
    total = blocks[0].astype(jnp.float32)
    for block in blocks[1:]:
        total = total + block.astype(jnp.float32)
    return total


def send_core(places, parts):
    cores = places.sizes["c"]
    halves = [parts[:cores], parts[cores:]]
    return [[mine] + [places.exchange(other, "c", hop) for hop, other in enumerate(others, 1)] for mine, *others in halves]


def plane_totals(places, blocks, axis):
    share = blocks[0].shape[0] // places.sizes[axis]
    cuts = [slice(i * share, (i + 1) * share) for i in range(places.sizes[axis])]
    return [add_low(*[block[cut] for block in blocks]).astype(jnp.bfloat16) for cut in cuts]


def send_totals(places, totals, axis):
    return totals[:1] + [places.exchange(total, axis, hop) for hop, total in enumerate(totals[1:], 1)]


def send_plane(places, sums, step):
    axes = [order[step] for order in ORDERS]
    return [send_totals(places, plane_totals(places, blocks, axis), axis) for blocks, axis in zip(sums, axes)]


def send_plane_tied(places, sums, step, later):
    (first, second), axes = sums, [order[step] for order in ORDERS]
    first, later = tie(first, later)
    first = plane_totals(places, first, axes[0])
    second, first, later = tie(second, first, later)
    result = [send_totals(places, first, axes[0])]
    second, later = tie(plane_totals(places, second, axes[1]), later)
    return result + [send_totals(places, second, axes[1])], later


def column_totals(places, sums):
    count = places.sizes["z"]
    share = sums[0][0].shape[0] // count
    cuts = [slice(hop * share, (hop + 1) * share) for hop in range(count)]
    return [join([add_low(*[block[cut] for block in blocks]).astype(jnp.bfloat16) for blocks in sums]) for cut in cuts]


def send_column(places, totals):
    return [totals[0]] + [places.exchange(total, "z", hop) for hop, total in enumerate(totals[1:], 1)]


class Layer:
    def __init__(self, places, position, counts, vectors):
        self.places, self.position, self.counts, self.vectors = places, position, counts, vectors

    def project(self, hidden, parts):
        normed, qkv, tiles = project(self.places, self.position, parts, hidden, self.vectors)
        self.saved = dict(hidden=hidden, normed=normed, qkv=qkv, tiles=tiles)

    def attend(self):
        saved = self.saved
        saved["attended"], saved["weights"] = attention(self.counts, saved["qkv"], self.bias)

    def finish(self):
        saved = self.saved
        names = ("branch", "middle", "normed2", "activ", "slope", "mlp_out")
        result, *kept = mlp(saved["attended"], saved["hidden"], self.vectors, saved["tiles"])
        saved.update(zip(names, kept))
        return result

    def back_mlp(self, grad):
        return mlp_back(grad, self.saved, self.vectors, self.saved["tiles"])

    def back_attention(self, passed):
        return attention_back(self.saved["qkv"], passed[1], self.saved["weights"])

    def back_weights(self, passed, grad_project, stepwise):
        _, _, grad_mlp, grad_pre, grad_branch, _ = passed
        saved = self.saved
        ins = [saved["normed"], grad_project, saved["attended"], grad_branch, saved["normed2"], grad_pre]
        return weight_back(self.places, self.position, stepwise, ins + [saved["activ"], grad_mlp])

    def back_input(self, passed, grad_project):
        return input_back(grad_project, passed[0], self.saved["hidden"], self.vectors, self.saved["tiles"])


def scatter_whole(parts):
    whole = parts[0].reshape(-1, LANES)
    return lax.psum_scatter(whole, AXES, scatter_dimension=0, tiled=True).astype(jnp.float32)


def local(dp, fsdp, tokens, counts, params_first, params_second, cotangent):
    devices = dp * fsdp
    places = Places(dp, fsdp)
    stepwise = TILES % (4 * devices) == 0 and all(size & (size - 1) == 0 for size in places.sizes.values())
    share_rows = TILES * TILE // devices
    me = lax.axis_index(AXES)
    position = places.position(me)
    owned = Owned([params_first, params_second], me, devices)
    own = owned.share(0)
    small_rows = owned.small_rows(own)
    hidden, grad_output = pad_rows(tokens), pad_rows(cotangent)

    if stepwise:
        own = own.reshape(-1, TILE, LANES)
        column = fetch_column(places, own)
        near, small_rows = tie(group_of([own], [offset_of()]), small_rows)
        small_rows = small_rows.reshape(-1, TILE, LANES)
        near_first, small_rows = fetch_plane_with(places, near, 0, small_rows)
        near_first, small_rows = tie(near_first, small_rows)
        near_second, small_rows = fetch_plane_with(places, merge(near, near_first), 1, small_rows)
        small_rows = places.total(small_rows, "c")
        next_own, near_first = tie(owned.share(1, own), near_first)
        far, near_second = tie(group_of(column, column_offsets(places)[1:]), near_second)
        far_first = fetch_plane(places, far, 0)
        next_own, small_rows, far, hidden, grad_output = tie(next_own, small_rows, far, hidden, grad_output)
        next_own = jnp.concatenate([next_own, small_rows.reshape(-1, LANES)], axis=0)
        next_shares = [next_own] + fetch_column(places, next_own)
        small_rows = sum([rows[share_rows:] for rows in next_shares[1:]], next_own[share_rows:])
        small_rows = small_rows.reshape(2, -1, LANES)
        vectors = small_rows.astype(jnp.float32)
        next_shares = [rows[:share_rows].reshape(-1, TILE, LANES) for rows in next_shares]
        group = group_of(next_shares, column_offsets(places))
        far_second = fetch_plane(places, merge(far, far_first), 1)
        early = gather_core(places, [near, near_first, near_second, far, far_first])
    else:
        small_rows = lax.psum(small_rows, AXES)
    if stepwise:
        far_second, early, group, small_rows, vectors = tie(far_second, early, group, small_rows, vectors)
        first = fetch_plane(places, group, 0)
        parts = fetch_core(places, early) + fetch_core(places, list_core(places, [far_second]))
        first_layer = Layer(places, position, counts, vectors[0])
        parts, group = tie(parts, group)
        second_early = fetch_plane(places, group, 1)
        first_layer.project(hidden, parts)
        entries, first_layer.saved = tie(table_entries(small_rows), first_layer.saved)
        first_layer.bias, second_bias = bias_of(entries[0]), bias_of(entries[1])
        first, second_early, first_layer.bias, second_bias = tie(first, second_early, first_layer.bias, second_bias)
        second = fetch_plane(places, first, 1)
        next_parts = fetch_core(places, list_core(places, [first, second_early]))
        first_layer.attend()
        result = first_layer.finish()
        next_parts, result = tie(next_parts, result)
        next_parts += fetch_core(places, gather_core(places, [group]))
        second, next_parts, result = tie(second, next_parts, result)
        next_parts += fetch_core(places, list_core(places, [second]))
    else:
        vectors = small_rows.astype(jnp.float32)
        entries = table_entries(small_rows)
        second_bias = bias_of(entries[1])
        parts, next_parts = [
            [(lax.all_gather(share, AXES, axis=0, tiled=True).reshape(TILES, TILE, LANES), [None])]
            for share in (own, owned.share(1))
        ]
        first_layer = Layer(places, position, counts, vectors[0])
        first_layer.project(hidden, parts)
        first_layer.bias = bias_of(entries[0])
        first_layer.attend()
        result = first_layer.finish()
    second_layer = Layer(places, position, counts, vectors[1])
    second_layer.bias = second_bias
    second_layer.project(result, next_parts)
    second_layer.attend()
    result = second_layer.finish()
    output = cut_rows(result)

    next_passed = second_layer.back_mlp(grad_output)
    next_project, next_bias = second_layer.back_attention(next_passed)
    parts = second_layer.back_weights(next_passed, next_project, stepwise)
    if stepwise:
        sums = send_core(places, parts)
    else:
        next_share = scatter_whole(parts)
    grad, next_sums = second_layer.back_input(next_passed, next_project)
    if stepwise:
        sums, grad = send_plane_tied(places, sums, 0, grad)
    passed = first_layer.back_mlp(grad)
    project_grad, bias = first_layer.back_attention(passed)
    parts = first_layer.back_weights(passed, project_grad, stepwise)
    if stepwise:
        sums, parts, passed, project_grad = tie(sums, parts, passed, project_grad)
        sums = send_plane(places, sums, 1)
        own_sums = send_core(places, parts)
    else:
        share = scatter_whole(parts)
    if stepwise:
        own_sums, later = send_plane_tied(places, own_sums, 0, (bias, passed, project_grad))
        sums, (bias, passed, project_grad) = tie(sums, later)
        sums = send_column(places, column_totals(places, sums))
    grad, own_row_sums = first_layer.back_input(passed, project_grad)
    small_grads = small_gradients(
        [own_row_sums, next_sums], [passed[5], next_passed[5]], tables_from_biases(bias, next_bias)
    )
    flat_share = FlatShare(me, devices, params_first.shape[0] * devices)
    if stepwise:
        own_sums, sums, small_grads = tie(own_sums, sums, small_grads)
        own_sums = send_plane(places, own_sums, 1)
        small_grads = places.total(small_grads, "zc")
        own_sums, small_grads = tie(own_sums, small_grads)
        own_sums = send_column(places, column_totals(places, own_sums))
        small_grads = places.total(small_grads, "xy")
        small_grads, sums = tie(small_grads, sums)
        grad_second = flat_share(add_low(*sums).reshape(-1, LANES), small_grads[1])
        own_sums, grad_second, output, grad_tokens = tie(own_sums, grad_second, output, cut_rows(grad))
        share = add_low(*own_sums).reshape(-1, LANES)
    else:
        small_grads = lax.psum(small_grads, AXES)
        grad_second = flat_share(next_share, small_grads[1])
        grad_tokens = cut_rows(grad)
    grad_first = flat_share(share, small_grads[0])
    return output, grad_tokens, grad_first, grad_second


def solution(mesh):
    return jax.shard_map(
        functools.partial(local, mesh.shape["dp"], mesh.shape["fsdp"]),
        mesh=mesh,
        in_specs=(P(AXES, None, None), P(AXES), P(AXES), P(AXES), P(AXES, None, None)),
        out_specs=(P(AXES, None, None), P(AXES, None, None), P(AXES), P(AXES)),
        check_vma=False,
    )
```

```python
import functools
import math

import jax
import jax.numpy as jnp
import numpy as np
from jax import lax
from jax.experimental import pallas as pl
from jax.experimental.pallas import tpu as pltpu
from jax.sharding import PartitionSpec as P

D = 768
HEADS = 12
HEAD = D // HEADS
FF = 3072
GRID = 14
SEQ = 197
RELS = 732
ROWS = 208
LANES = 128
TILE = 16
AXES = ("dp", "fsdp")
VMEM_LIMIT = 56 * 2**20

EPSILON = 1e-06
NEGATIVE = -1000000000.0

ENTRIES = [
    ("norm1_gain", (D,)),
    ("norm1_bias", (D,)),
    ("qkv_weight", (D, 3 * D)),
    ("query_bias", (D,)),
    ("value_bias", (D,)),
    ("relative_table", (RELS, HEADS)),
    ("proj_weight", (D, D)),
    ("proj_bias", (D,)),
    ("gamma_attn", (D,)),
    ("norm2_gain", (D,)),
    ("norm2_bias", (D,)),
    ("fc1_weight", (D, FF)),
    ("fc1_bias", (FF,)),
    ("fc2_weight", (FF, D)),
    ("fc2_bias", (D,)),
    ("gamma_mlp", (D,)),
]
WEIGHTS = {name: dims for name, dims in ENTRIES if name.endswith("weight")}
SIZES = dict(ENTRIES)
VECTORS = [
    "norm1_gain",
    "norm1_bias",
    "query_bias",
    "value_bias",
    "proj_bias",
    "gamma_attn",
    "norm2_gain",
    "norm2_bias",
    "fc2_bias",
    "gamma_mlp",
]
ROW = {name: i for i, name in enumerate(VECTORS)}


def count_rows(dims):
    return -(-math.prod(dims) // LANES)


def virtual_starts():
    starts, at = {}, 0
    for name, dims in ENTRIES:
        starts[name] = at
        at += count_rows(dims)
    return starts, at


STARTS, VIRTUAL = virtual_starts()
SHIFT = RELS * HEADS % LANES
TABLE_END = STARTS["proj_weight"]


def tile_order():
    parts = []
    for name, (depth, width) in WEIGHTS.items():
        across = width // LANES
        rows = STARTS[name] + np.arange(depth * across).reshape(depth // TILE, TILE, across)
        parts.append(rows.transpose(0, 2, 1).reshape(-1))
    return np.concatenate(parts)


def small_order():
    groups = [VECTORS, ["fc1_bias"], ["relative_table"]]
    rows = []
    for group in groups:
        for name in group:
            rows += [STARTS[name] + i for i in range(count_rows(SIZES[name]))]
        rows += [-1] * (-len(rows) % 8)
    return np.array(rows)


TILE_ROWS = tile_order()
SMALL_ROWS = small_order()
TILES = len(TILE_ROWS) // TILE


def tie(*trees):
    leaves, structure = jax.tree.flatten(trees)
    tied = iter(lax.optimization_barrier([leaf for leaf in leaves if isinstance(leaf, jax.Array)]))
    return structure.unflatten([next(tied) if isinstance(leaf, jax.Array) else leaf for leaf in leaves])


def halo(block, before, after, devices, join=True):
    rows = block.shape[-2]
    pieces = [block] if join else []
    for hop in range(1, -(-before // rows) + 1):
        take = min(rows, before - (hop - 1) * rows)
        perm = [(i, i + hop) for i in range(devices - hop)]
        pieces.insert(0, lax.ppermute(block[..., rows - take :, :], AXES, perm))
    for hop in range(1, -(-after // rows) + 1):
        take = min(rows, after - (hop - 1) * rows)
        perm = [(i + hop, i) for i in range(devices - hop)]
        pieces.append(lax.ppermute(block[..., :take, :], AXES, perm))
    return jnp.concatenate(pieces, axis=-2)


def pick_rows(index, source):
    chosen = index[:, None] == lax.broadcasted_iota(jnp.int32, (1, source.shape[0]), 1)
    return jnp.dot(chosen.astype(jnp.bfloat16), source.astype(jnp.bfloat16), preferred_element_type=jnp.float32)


def round_up(value, unit):
    return -(-value // unit) * unit


class Owned:
    def __init__(self, flats, me, devices):
        length = flats[0].shape[0] // LANES
        share = len(TILE_ROWS) // devices
        starts = np.arange(devices)[:, None] * length
        wanted = TILE_ROWS.reshape(devices, share) - starts
        before = round_up(max(0, -wanted.min()) + 1, TILE)
        after = round_up(max(0, wanted.max() + 1 - length), TILE)
        smalls = SMALL_ROWS[None] - starts
        smalls = np.where((smalls >= 0) & (smalls < length), smalls + before - 1, -1)
        self.wanted = self.mine(wanted + before - 1, me)
        self.smalls = self.mine(smalls, me)
        around = halo(jnp.stack([flat.reshape(length, LANES) for flat in flats]), before, after, devices)
        shifted = jnp.concatenate([around[:, :-1, SHIFT:], around[:, 1:, :SHIFT]], axis=2)
        at = me * length - before + 1 + lax.broadcasted_iota(jnp.int32, (1, shifted.shape[1], 1), 1)
        self.virtual = jnp.where(at < TABLE_END, around[:, 1:], shifted)

    @staticmethod
    def mine(table, me):
        return lax.dynamic_index_in_dim(jnp.asarray(table.astype(np.int32)), me, 0, keepdims=False)

    def small_rows(self, *after):
        virtual, *_ = tie(self.virtual, *after)
        return jnp.stack([pick_rows(self.smalls, rows).astype(jnp.bfloat16) for rows in virtual])

    def share(self, number, *after):
        rows = self.virtual[number]
        if after:
            rows, *_ = tie(rows, *after)
        return pick_rows(self.wanted, rows).astype(jnp.bfloat16)


class FlatShare:
    def __init__(self, me, devices, flat_length):
        length = flat_length // LANES // devices
        share = len(TILE_ROWS) // devices
        place = np.full(max(VIRTUAL, devices * length + 1), -1, np.int64)
        place[TILE_ROWS] = np.arange(len(TILE_ROWS))
        small_place = np.full(place.shape, -1, np.int64)
        small_place[SMALL_ROWS[SMALL_ROWS >= 0]] = np.flatnonzero(SMALL_ROWS >= 0)
        span = np.arange(devices)[:, None] * length + np.arange(length + 1)[None]
        relative = place[span] - np.arange(devices)[:, None] * share
        has = place[span] >= 0
        self.before = round_up(max(0, -relative[has].min()), TILE)
        self.after = round_up(max(0, relative[has].max() + 1 - share), TILE)
        smalls_at = self.before + share + self.after
        index = np.where(has, relative + self.before, -1)
        index = np.where(small_place[span] >= 0, small_place[span] + smalls_at, index)
        self.index = Owned.mine(index, me)
        self.at = me * length + lax.broadcasted_iota(jnp.int32, (length, 1), 0)
        self.devices = devices

    def __call__(self, owned, smalls):
        owned = owned.astype(jnp.bfloat16)
        share = owned.shape[0]
        around = halo(owned, self.before, self.after, self.devices, join=False)
        ends = self.before + share
        here = jnp.concatenate([owned, smalls.astype(jnp.bfloat16)], axis=0)
        index = self.index - self.before
        outside = (self.index < self.before) | ((self.index >= ends) & (self.index < ends + self.after))
        index = jnp.where(outside, -1, jnp.where(self.index >= ends, index - self.after, index))
        virtual = pick_rows(index, here)
        index = jnp.where(self.index < self.before, self.index, self.index - share)
        index = jnp.where(outside, index, -1)
        virtual = virtual + pick_rows(index, around)
        here, following = virtual[:-1], virtual[1:]
        lane = lax.broadcasted_iota(jnp.int32, (1, LANES), 1)
        shifted = jnp.concatenate([here[:, LANES - SHIFT :], following[:, : LANES - SHIFT]], axis=1)
        straight = (self.at < TABLE_END - 1) | ((self.at == TABLE_END - 1) & (lane < SHIFT))
        return jnp.where(straight, here, shifted).reshape(-1)


VECTOR_ROWS = D // LANES
FC1_AT = round_up(len(VECTORS) * VECTOR_ROWS, 8)
TABLE_AT = FC1_AT + FF // LANES
TABLE_ROWS = count_rows(SIZES["relative_table"])
LATER = 4


def table_entries(rows):
    tables = rows[:, TABLE_AT : TABLE_AT + TABLE_ROWS].reshape(2, -1)[:, : RELS * HEADS].reshape(2, RELS, HEADS)
    return jnp.pad(tables.transpose(0, 2, 1), ((0, 0), (0, 16 - HEADS), (0, ENTRY_LANES - RELS)))


def small_gradients(first, later, tables):
    tables = tables.reshape(2, RELS * HEADS)
    tables = jnp.pad(tables, ((0, 0), (0, round_up(TABLE_ROWS, 8) * LANES - RELS * HEADS))).reshape(2, -1, LANES)
    return jnp.concatenate([jnp.stack(first), jnp.stack(later), tables], axis=1)


SIDE = 2 * GRID - 1
WINDOW = round_up(SIDE * GRID, LANES) + LANES
WIDE = round_up(ROWS, LANES)


ENTRY_LANES = round_up(RELS, LANES)
HEAD_ROWS = 2 * 16


def entry_choice(column, transposed):
    shape = (1, WINDOW) if transposed else (WINDOW, 1)
    source = lax.broadcasted_iota(jnp.int32, shape, 1 if transposed else 0)
    group = source // GRID
    target = (SIDE - 1 - group) * SIDE - (source - group * GRID) + GRID - 1 + column
    target = jnp.where(source < SIDE * GRID, target, -1)
    entries = (ENTRY_LANES, 1) if transposed else (1, ENTRY_LANES)
    entry = lax.broadcasted_iota(jnp.int32, entries, 0 if transposed else 1)
    return (entry == target).astype(jnp.float32).astype(jnp.bfloat16)


def bias_kernel(entries_ref, bias_ref, windows_ref):
    for column in range(GRID):
        windows_ref[column] = product(entries_ref[...], entry_choice(column, True), NN)
    lane = lax.broadcasted_iota(jnp.int32, (1, WIDE), 1)
    inner = (lane >= 1) & (lane < SEQ)

    def head(i, _):
        ends = entries_ref[pl.ds(pl.multiple_of(i // 16 * 16, 16), 16), :].astype(jnp.float32)
        picked = lax.broadcasted_iota(jnp.int32, (16, 1), 0) == i % 16
        ends = jnp.sum(jnp.where(picked, ends, 0.0), axis=0, keepdims=True)
        top, left, corner = [ends[:, RELS - k : RELS - k + 1] for k in (3, 2, 1)]
        bias_ref[i] = jnp.zeros(bias_ref.shape[1:], jnp.float32)
        bias_ref[i, 0:1] = jnp.where(inner, top, jnp.where(lane == 0, corner, 0.0))[:, :ROWS]
        spread = jnp.concatenate([windows_ref[column, pl.ds(i, 1)] for column in range(GRID)], axis=0)
        for row in range(GRID):
            start = (GRID - 1 - row) * GRID
            window = pltpu.roll(spread, (1 - start) % WINDOW, 1)[:, :WIDE]
            window = jnp.where(inner, window, jnp.where(lane == 0, left, 0.0))
            bias_ref[i, 1 + row * GRID : 1 + (row + 1) * GRID] = window[:, :ROWS]
        return 0

    lax.fori_loop(0, HEADS, head, 0)


def bias_of(entries):
    return pl.pallas_call(
        bias_kernel,
        grid=(1,),
        in_specs=[pl.BlockSpec(entries.shape, lambda i: (0, 0))],
        out_specs=pl.BlockSpec((HEADS, ROWS, ROWS), lambda i: (0, 0, 0)),
        out_shape=jax.ShapeDtypeStruct((HEADS, ROWS, ROWS), jnp.float32),
        scratch_shapes=[pltpu.VMEM((GRID, 16, WINDOW), jnp.float32)],
        compiler_params=pltpu.CompilerParams(vmem_limit_bytes=VMEM_LIMIT),
        name="bias",
    )(entries)


def table_kernel(first_ref, second_ref, out_ref, windows_ref, ends_ref):
    lane = lax.broadcasted_iota(jnp.int32, (1, ROWS), 1)
    inner = (lane >= 1) & (lane < SEQ)
    entry = lax.broadcasted_iota(jnp.int32, (1, ENTRY_LANES), 1)
    windows_ref[...] = jnp.zeros_like(windows_ref)
    ends_ref[...] = jnp.zeros_like(ends_ref)
    for number, grad_ref in enumerate((first_ref, second_ref)):

        def head(i, _, number=number, grad_ref=grad_ref):
            total = jnp.zeros((GRID, WINDOW), jnp.float32)
            left = jnp.zeros((1, 1), jnp.float32)
            for row in range(GRID):
                start = (GRID - 1 - row) * GRID
                block = grad_ref[i, 1 + row * GRID : 1 + (row + 1) * GRID]
                left = left + jnp.sum(jnp.where(lane == 0, block, 0.0), keepdims=True)
                block = jnp.where(inner, block, 0.0)
                block = jnp.concatenate([block, jnp.zeros((GRID, WINDOW - ROWS), jnp.float32)], axis=1)
                total = total + pltpu.roll(block, (start - 1) % WINDOW, 1)
            at = pl.ds(number * 16 + i, 1)
            for column in range(GRID):
                windows_ref[column, at] = total[column : column + 1]
            first = grad_ref[i, 0:1]
            top = jnp.sum(jnp.where(inner, first, 0.0), keepdims=True)
            corner = jnp.sum(jnp.where(lane == 0, first, 0.0), keepdims=True)
            ends = jnp.where(entry == RELS - 3, top, jnp.where(entry == RELS - 2, left, 0.0))
            ends_ref[at] = jnp.where(entry == RELS - 1, corner, ends)
            return 0

        lax.fori_loop(0, HEADS, head, 0)
    out_ref[...] = ends_ref[...]
    for column in range(GRID):
        rows = windows_ref[column]
        high = rows.astype(jnp.bfloat16)
        low = (rows - high.astype(jnp.float32)).astype(jnp.bfloat16)
        chosen = entry_choice(column, False)
        out_ref[...] += product(high, chosen, NN) + product(low, chosen, NN)


def tables_from_biases(first, second):
    entries = pl.pallas_call(
        table_kernel,
        grid=(1,),
        in_specs=[pl.BlockSpec(first.shape, lambda i: (0, 0, 0))] * 2,
        out_specs=pl.BlockSpec((HEAD_ROWS, ENTRY_LANES), lambda i: (0, 0)),
        out_shape=jax.ShapeDtypeStruct((HEAD_ROWS, ENTRY_LANES), jnp.float32),
        scratch_shapes=[
            pltpu.VMEM((GRID, HEAD_ROWS, WINDOW), jnp.float32),
            pltpu.VMEM((HEAD_ROWS, ENTRY_LANES), jnp.float32),
        ],
        compiler_params=pltpu.CompilerParams(vmem_limit_bytes=VMEM_LIMIT),
        name="table_back",
    )(first, second)
    return entries.reshape(2, 16, ENTRY_LANES)[:, :HEADS, :RELS].transpose(0, 2, 1)


NT = (((1,), (1,)), ((), ()))
NN = (((1,), (0,)), ((), ()))
TN = (((0,), (0,)), ((), ()))


def product(left, right, dims):
    return lax.dot_general(left, right, dims, preferred_element_type=jnp.float32)


def own_lanes(head):
    lane = lax.broadcasted_iota(jnp.int32, (1, LANES), 1)
    return lane < HEAD if head == 0 else lane >= HEAD


def head_weights(query, key, bias, count, head):
    chosen = jnp.where(own_lanes(head), query, jnp.zeros_like(query))
    scores = product(chosen, key, NT) + bias
    column = lax.broadcasted_iota(jnp.int32, (1, ROWS), 1)
    scores = jnp.where(column < count, scores, NEGATIVE)
    grown = jnp.exp(scores - jnp.max(scores, axis=1, keepdims=True))
    return grown * (1.0 / jnp.sum(grown, axis=1, keepdims=True))


def attention_kernel(pairs, counts_ref, query_ref, key_ref, value_ref, bias_ref, out_ref, weights_ref):
    count = counts_ref[pl.program_id(1)]
    for pair in range(pairs):
        lanes = slice(pair * LANES, (pair + 1) * LANES)
        query, key, value = query_ref[:, lanes], key_ref[:, lanes], value_ref[:, lanes]
        parts = []
        for head in range(2):
            weights = head_weights(query, key, bias_ref[2 * pair + head], count, head).astype(jnp.bfloat16)
            weights_ref[0, 2 * pair + head] = weights
            parts.append(product(weights, value, NN))
        out_ref[:, lanes] = jnp.where(own_lanes(0), parts[0], parts[1]).astype(jnp.bfloat16)


def attention_back_kernel(pairs, query_ref, key_ref, value_ref, grad_ref, weights_ref, out_ref, db_ref):
    image = pl.program_id(1)

    @pl.when(image == 0)
    def _():
        db_ref[...] = jnp.zeros_like(db_ref)

    for pair in range(pairs):
        lanes = slice(pair * LANES, (pair + 1) * LANES)
        query, key, value, grad = query_ref[:, lanes], key_ref[:, lanes], value_ref[:, lanes], grad_ref[:, lanes]
        dq, dk, dv = [], [], []
        for head in range(2):
            low_weights = weights_ref[0, 2 * pair + head]
            weights = low_weights.astype(jnp.float32)
            chosen = jnp.where(own_lanes(head), grad, jnp.zeros_like(grad))
            weighted = weights * product(chosen, value, NT)
            dv.append(product(low_weights, grad, TN))
            grad_scores = weighted - weights * jnp.sum(weighted, axis=1, keepdims=True)
            low = grad_scores.astype(jnp.bfloat16)
            dq.append(product(low, key, NN))
            dk.append(product(low, query, TN))
            db_ref[2 * pair + head] += grad_scores
        first = own_lanes(0)
        out_ref[0, :, lanes] = (jnp.where(first, dq[0], dq[1]) * HEAD**-0.5).astype(jnp.bfloat16)
        out_ref[1, :, lanes] = jnp.where(first, dk[0], dk[1]).astype(jnp.bfloat16)
        out_ref[2, :, lanes] = jnp.where(first, dv[0], dv[1]).astype(jnp.bfloat16)


def attention_specs(pairs):
    steps = D // LANES // pairs
    lanes = [
        pl.BlockSpec((ROWS, pairs * LANES), lambda step, image, *_, part=part: (image, part * steps + step))
        for part in range(3)
    ]
    bias = pl.BlockSpec((2 * pairs, ROWS, ROWS), lambda step, image, *_: (step, 0, 0))
    weights = pl.BlockSpec((1, 2 * pairs, ROWS, ROWS), lambda step, image, *_: (image, step, 0, 0))
    return steps, lanes, bias, weights


def attention(counts, qkv, bias, pairs=6):
    images = qkv.shape[0] // ROWS
    steps, lanes, bias_spec, weights_spec = attention_specs(pairs)
    return pl.pallas_call(
        functools.partial(attention_kernel, pairs),
        grid_spec=pltpu.PrefetchScalarGridSpec(
            num_scalar_prefetch=1,
            grid=(steps, images),
            in_specs=lanes + [bias_spec],
            out_specs=[lanes[0], weights_spec],
        ),
        out_shape=[
            jax.ShapeDtypeStruct((qkv.shape[0], D), jnp.bfloat16),
            jax.ShapeDtypeStruct((images, HEADS, ROWS, ROWS), jnp.bfloat16),
        ],
        compiler_params=pltpu.CompilerParams(vmem_limit_bytes=VMEM_LIMIT),
        name="attention",
    )(counts, qkv, qkv, qkv, bias)


def attention_back(qkv, grad, weights, pairs=3):
    images = qkv.shape[0] // ROWS
    steps, lanes, bias_spec, weights_spec = attention_specs(pairs)
    return pl.pallas_call(
        functools.partial(attention_back_kernel, pairs),
        grid=(steps, images),
        in_specs=lanes + [lanes[0], weights_spec],
        out_specs=[
            pl.BlockSpec((3, ROWS, pairs * LANES), lambda step, image: (0, image, step)),
            bias_spec,
        ],
        out_shape=[
            jax.ShapeDtypeStruct((3, qkv.shape[0], D), jnp.bfloat16),
            jax.ShapeDtypeStruct((HEADS, ROWS, ROWS), jnp.float32),
        ],
        compiler_params=pltpu.CompilerParams(vmem_limit_bytes=VMEM_LIMIT),
        name="attention_back",
    )(qkv, qkv, qkv, grad, weights)


def tile_starts():
    starts, at = {}, 0
    for name, (depth, width) in WEIGHTS.items():
        starts[name] = at
        at += depth // TILE * (width // LANES)
    return starts


FIRST = tile_starts()
MLP_FIRST = FIRST["proj_weight"]
SPAN = 1024


def load_weight(ref, base, name, row, rows, column, columns):
    first, across = FIRST[name] - base, WEIGHTS[name][1] // LANES
    lines = []
    for i in range(rows):
        at = first + (row + i) * across + column
        lines.append(jnp.concatenate([ref[at + j] for j in range(columns)], axis=1))
    return jnp.concatenate(lines, axis=0)


def gelu_and_slope(values):
    size = jnp.abs(values)
    step = 1.0 / (1.0 + (0.3275911 / math.sqrt(2.0)) * size)
    bell = jnp.exp(-0.5 * values * values)
    series = 1.061405429
    for term in (-1.453152027, 1.421413741, -0.284496736, 0.254829592):
        series = series * step + term
    tail = 0.5 * series * step * bell
    area = jnp.where(values < 0, tail, 1.0 - tail)
    return values * area, area + values * bell * (1.0 / math.sqrt(2.0 * math.pi))


def norm_parts(values):
    centre = values - jnp.mean(values, axis=-1, keepdims=True)
    spread = jnp.mean(centre * centre, axis=-1, keepdims=True)
    inverse = lax.rsqrt(spread + EPSILON)
    return centre * inverse, inverse


def norm_back(grad, normal, inverse, gain):
    scaled = grad * gain
    first = jnp.mean(scaled, axis=-1, keepdims=True)
    second = jnp.mean(scaled * normal, axis=-1, keepdims=True)
    return (scaled - first - normal * second) * inverse


def wide_row(ref, first, count):
    return jnp.concatenate([ref[first + i : first + i + 1] for i in range(count)], axis=1)


def vector(ref, name):
    return wide_row(ref, ROW[name] * VECTOR_ROWS, VECTOR_ROWS)


def put_vector(ref, row, values):
    sums = jnp.sum(values, axis=0, keepdims=True)
    for i in range(sums.shape[1] // LANES):
        ref[row + i : row + i + 1] = sums[:, i * LANES : (i + 1) * LANES]


def later_row(name):
    return (ROW[name] - LATER) * VECTOR_ROWS


def whole_spec(shape):
    return pl.BlockSpec(shape, lambda *_: (0,) * len(shape))


ANYWHERE = pl.BlockSpec(memory_space=pl.ANY)
PARAMS = pltpu.CompilerParams(vmem_limit_bytes=VMEM_LIMIT)


def low_like(*shape):
    return jax.ShapeDtypeStruct(shape, jnp.bfloat16)


def full_like(*shape):
    return jax.ShapeDtypeStruct(shape, jnp.float32)


def project_kernel(places, slots, at_ref, *refs):
    parts, refs = refs[: len(slots)], refs[len(slots) :]
    hidden_ref, vectors_ref, normed_ref, qkv_ref, tiles_ref, whole_ref, sems, out_sem = refs
    copies = copies_in(places, at_ref, parts, slots, whole_ref, sems)
    for copy in copies:
        copy.start()
    normal, _ = norm_parts(hidden_ref[...])
    normed_ref[...] = (normal * vector(vectors_ref, "norm1_gain") + vector(vectors_ref, "norm1_bias")).astype(
        jnp.bfloat16
    )
    for copy in copies:
        copy.wait()
    leaving = pltpu.make_async_copy(whole_ref, tiles_ref, out_sem)
    leaving.start()
    across = D // LANES
    for part in range(3):
        weight = load_weight(whole_ref, 0, "qkv_weight", 0, D // TILE, part * across, across)
        rows = product(normed_ref[...], weight, NN)
        if part == 0:
            rows = (rows + vector(vectors_ref, "query_bias")) * HEAD**-0.5
        if part == 2:
            rows = rows + vector(vectors_ref, "value_bias")
        qkv_ref[:, part * D : (part + 1) * D] = rows.astype(jnp.bfloat16)
    leaving.wait()


def project(places, position, parts, hidden, vectors):
    arrays = [array for array, _ in parts]
    slots = [listed for _, listed in parts]
    rows = hidden.shape[0]
    return pl.pallas_call(
        functools.partial(project_kernel, places, slots),
        grid_spec=pltpu.PrefetchScalarGridSpec(
            num_scalar_prefetch=1,
            grid=(1,),
            in_specs=[ANYWHERE] * len(arrays) + [whole_spec((rows, D)), whole_spec(vectors.shape)],
            out_specs=[whole_spec((rows, D)), whole_spec((rows, 3 * D)), ANYWHERE],
            scratch_shapes=[
                pltpu.VMEM((TILES, TILE, LANES), jnp.bfloat16),
                pltpu.SemaphoreType.DMA((sum(len(listed) for listed in slots),)),
                pltpu.SemaphoreType.DMA(()),
            ],
        ),
        out_shape=[low_like(rows, D), low_like(rows, 3 * D), low_like(TILES, TILE, LANES)],
        compiler_params=PARAMS,
        name="project",
    )(position, *arrays, hidden, vectors)


def mlp_weights(tiles_ref, weight_ref, sems, order):
    copies = []
    for i, name in enumerate(order):
        depth, width = WEIGHTS[name]
        count = depth // TILE * (width // LANES)
        here = weight_ref.at[pl.ds(FIRST[name] - MLP_FIRST, count)]
        copies.append(pltpu.make_async_copy(tiles_ref.at[pl.ds(FIRST[name], count)], here, sems.at[i]))
        copies[-1].start()
    return copies


def span_of(step):
    return slice(step * SPAN, (step + 1) * SPAN)


class Leaving:
    def __init__(self, outs, buffers, sems):
        self.outs, self.buffers, self.sems, self.copies = outs, buffers, sems, []

    def start(self, number, columns=None):
        source, target = self.buffers[number], self.outs[number]
        if columns is not None:
            source, target = source.at[:, columns], target.at[:, columns]
        self.copies.append(pltpu.make_async_copy(source, target, self.sems.at[len(self.copies)]))
        self.copies[-1].start()

    def wait(self):
        for copy in self.copies:
            copy.wait()


def mlp_kernel(attended_ref, hidden_ref, vectors_ref, tiles_ref, *refs):
    outs, buffers, (total_ref, weight_ref, sems, out_sems, fc1_bias_ref) = refs[:7], refs[7:14], refs[14:]
    result_ref, branch_ref, middle_ref, normed_ref, activ_ref, slope_ref, mlp_ref = buffers
    leaving = Leaving(outs, buffers, out_sems)
    copies = mlp_weights(tiles_ref, weight_ref, sems, ("proj_weight", "fc1_weight", "fc2_weight"))
    fc1_bias_ref[...] = wide_row(vectors_ref, FC1_AT, FF // LANES)
    copies[0].wait()
    across = D // LANES
    weight = load_weight(weight_ref, MLP_FIRST, "proj_weight", 0, D // TILE, 0, across)
    branch = product(attended_ref[...], weight, NN) + vector(vectors_ref, "proj_bias")
    branch_ref[...] = branch.astype(jnp.bfloat16)
    leaving.start(1)
    middle_ref[...] = hidden_ref[...] + vector(vectors_ref, "gamma_attn") * branch
    leaving.start(2)
    normal, _ = norm_parts(middle_ref[...])
    normed_ref[...] = (normal * vector(vectors_ref, "norm2_gain") + vector(vectors_ref, "norm2_bias")).astype(
        jnp.bfloat16
    )
    leaving.start(3)
    total_ref[...] = jnp.broadcast_to(vector(vectors_ref, "fc2_bias"), total_ref.shape)
    copies[1].wait()

    def step(i, _):
        span = span_of(i)
        weight = load_weight(weight_ref, MLP_FIRST, "fc1_weight", 0, D // TILE, i * (SPAN // LANES), SPAN // LANES)
        activ, slope = gelu_and_slope(product(normed_ref[...], weight, NN) + fc1_bias_ref[:, span])
        activ = activ.astype(jnp.bfloat16)
        activ_ref[:, span] = activ
        slope_ref[:, span] = slope.astype(jnp.bfloat16)
        leaving.start(4, span)
        leaving.start(5, span)
        if i == 0:
            copies[2].wait()
        weight = load_weight(weight_ref, MLP_FIRST, "fc2_weight", i * (SPAN // TILE), SPAN // TILE, 0, across)
        total_ref[...] += product(activ, weight, NN)
        return 0

    for i in range(FF // SPAN):
        step(i, 0)
    result_ref[...] = middle_ref[...] + vector(vectors_ref, "gamma_mlp") * total_ref[...]
    leaving.start(0)
    mlp_ref[...] = total_ref[...].astype(jnp.bfloat16)
    leaving.start(6)
    leaving.wait()


def mlp_scratch(rows, outs):
    return [pltpu.VMEM(out.shape, out.dtype) for out in outs] + [
        pltpu.VMEM((rows, D), jnp.float32),
        pltpu.VMEM((TILES - MLP_FIRST, TILE, LANES), jnp.bfloat16),
        pltpu.SemaphoreType.DMA((3,)),
        pltpu.SemaphoreType.DMA((len(outs) + 2 * (FF // SPAN),)),
    ]


def mlp(attended, hidden, vectors, tiles):
    rows = hidden.shape[0]
    outs = [full_like(rows, D), low_like(rows, D), full_like(rows, D), low_like(rows, D)]
    outs += [low_like(rows, FF), low_like(rows, FF), low_like(rows, D)]
    ins = [attended, hidden, vectors]
    return pl.pallas_call(
        mlp_kernel,
        grid=(1,),
        in_specs=[whole_spec(array.shape) for array in ins] + [ANYWHERE],
        out_specs=[ANYWHERE] * len(outs),
        out_shape=outs,
        scratch_shapes=mlp_scratch(rows, outs) + [pltpu.VMEM((1, FF), jnp.float32)],
        compiler_params=PARAMS,
        name="mlp",
    )(*ins, tiles)


def mlp_back_kernel(grad_ref, branch_ref, middle_ref, slope_ref, mlp_ref, vectors_ref, tiles_ref, *refs):
    outs, buffers, (total_ref, weight_ref, sems, out_sems) = refs[:6], refs[6:12], refs[12:]
    grad_middle_ref, grad_attended_ref, grad_mlp_ref, grad_pre_ref, grad_branch_ref, sums_ref = buffers
    leaving = Leaving(outs, buffers, out_sems)
    copies = mlp_weights(tiles_ref, weight_ref, sems, ("fc2_weight", "fc1_weight", "proj_weight"))
    across = D // LANES
    grad = grad_ref[...]
    sums_ref[...] = jnp.zeros_like(sums_ref)
    put_vector(sums_ref, later_row("gamma_mlp"), grad * mlp_ref[...].astype(jnp.float32))
    grad_mlp = grad * vector(vectors_ref, "gamma_mlp")
    put_vector(sums_ref, later_row("fc2_bias"), grad_mlp)
    grad_mlp_ref[...] = grad_mlp.astype(jnp.bfloat16)
    leaving.start(2)
    total_ref[...] = jnp.zeros_like(total_ref)
    copies[0].wait()

    def step(i, _):
        span = span_of(i)
        weight = load_weight(weight_ref, MLP_FIRST, "fc2_weight", i * (SPAN // TILE), SPAN // TILE, 0, across)
        grad_pre = product(grad_mlp_ref[...], weight, NT) * slope_ref[:, span].astype(jnp.float32)
        sums = jnp.sum(grad_pre, axis=0, keepdims=True)
        sums = jnp.concatenate([sums[:, k * LANES : (k + 1) * LANES] for k in range(SPAN // LANES)], axis=0)
        first = FC1_AT - LATER * VECTOR_ROWS + i * (SPAN // LANES)
        sums_ref[first : first + SPAN // LANES] = sums
        grad_pre = grad_pre.astype(jnp.bfloat16)
        grad_pre_ref[:, span] = grad_pre
        leaving.start(3, span)
        if i == 0:
            copies[1].wait()
        weight = load_weight(weight_ref, MLP_FIRST, "fc1_weight", 0, D // TILE, i * (SPAN // LANES), SPAN // LANES)
        total_ref[...] += product(grad_pre, weight, NT)
        return 0

    for i in range(FF // SPAN):
        step(i, 0)
    normal, inverse = norm_parts(middle_ref[...])
    grad_normed = total_ref[...]
    put_vector(sums_ref, later_row("norm2_gain"), grad_normed * normal)
    put_vector(sums_ref, later_row("norm2_bias"), grad_normed)
    grad_middle = grad_ref[...] + norm_back(grad_normed, normal, inverse, vector(vectors_ref, "norm2_gain"))
    grad_middle_ref[...] = grad_middle
    leaving.start(0)
    put_vector(sums_ref, later_row("gamma_attn"), grad_middle * branch_ref[...].astype(jnp.float32))
    grad_branch = grad_middle * vector(vectors_ref, "gamma_attn")
    put_vector(sums_ref, later_row("proj_bias"), grad_branch)
    leaving.start(5)
    grad_branch_ref[...] = grad_branch.astype(jnp.bfloat16)
    leaving.start(4)
    copies[2].wait()
    weight = load_weight(weight_ref, MLP_FIRST, "proj_weight", 0, D // TILE, 0, across)
    grad_attended_ref[...] = product(grad_branch_ref[...], weight, NT).astype(jnp.bfloat16)
    leaving.start(1)
    leaving.wait()


def mlp_back(grad, saved, vectors, tiles):
    rows = grad.shape[0]
    outs = [full_like(rows, D), low_like(rows, D), low_like(rows, D), low_like(rows, FF), low_like(rows, D)]
    outs += [full_like(TABLE_AT - LATER * VECTOR_ROWS, LANES)]
    ins = [grad, saved["branch"], saved["middle"], saved["slope"], saved["mlp_out"], vectors]
    return pl.pallas_call(
        mlp_back_kernel,
        grid=(1,),
        in_specs=[whole_spec(array.shape) for array in ins] + [ANYWHERE],
        out_specs=[ANYWHERE] * len(outs),
        out_shape=outs,
        scratch_shapes=mlp_scratch(rows, outs),
        compiler_params=PARAMS,
        name="mlp_back",
    )(*ins, tiles)


def scatter_place(places, at_ref, device, part):
    position = np.unravel_index(device, places.grid.shape)
    apart = {name: at_ref[i] ^ int(position[i]) for name, i in places.axis.items()}
    first, second = ORDERS[part]
    slot = (apart[first] * places.sizes[second] + apart[second]) * places.sizes["z"] + apart["z"]
    return apart["c"], slot


def weight_back_kernel(places, stepwise, at_ref, *refs):
    sources, refs = refs[:8], refs[8:]
    outs = refs[: 2 * places.sizes["c"] if stepwise else 1]
    operands, (whole_ref, in_sems, sems) = refs[len(outs) : len(outs) + 8], refs[len(outs) + 8 :]
    coming = [
        pltpu.make_async_copy(source, operand, in_sems.at[i]) for i, (source, operand) in enumerate(zip(sources, operands))
    ]
    for copy in coming:
        copy.start()
    normed_ref, project_ref, attended_ref, branch_ref, normed2_ref, pre_ref, activ_ref, mlp_ref = operands
    across = D // LANES

    def put(name, row, column, left, grad):
        block = product(left, grad, TN).astype(jnp.bfloat16)
        wide = WEIGHTS[name][1] // LANES
        for i in range(D // TILE):
            for j in range(across):
                at = FIRST[name] + (row + i) * wide + column + j
                whole_ref[at] = block[i * TILE : (i + 1) * TILE, j * LANES : (j + 1) * LANES]

    half = TILES // places.count // 2
    sent = []

    def send(ready):
        while stepwise and (len(sent) + 1) * half <= ready:
            number = len(sent)
            core, slot = scatter_place(places, at_ref, number // 2, number % 2)
            source = whole_ref.at[pl.ds(number * half, half)]
            for k in range(places.sizes["c"]):
                target = outs[number % 2 * places.sizes["c"] + k].at[pl.ds(slot * half, half)]
                copy = pltpu.make_async_copy(source, target, sems.at[number])
                pl.when(core == k)(copy.start)
            sent.append(copy)

    coming[0].wait()
    coming[1].wait()
    for part in range(3):
        put("qkv_weight", 0, part * across, normed_ref[...], project_ref[part])
    send(FIRST["proj_weight"])
    coming[2].wait()
    coming[3].wait()
    put("proj_weight", 0, 0, attended_ref[...], branch_ref[...])
    send(FIRST["fc1_weight"])
    coming[4].wait()
    coming[5].wait()
    for part in range(FF // D):
        put("fc1_weight", 0, part * across, normed2_ref[...], pre_ref[:, part * D : (part + 1) * D])
    send(FIRST["fc2_weight"])
    coming[6].wait()
    coming[7].wait()
    for part in range(FF // D):
        put("fc2_weight", part * (D // TILE), 0, activ_ref[:, part * D : (part + 1) * D], mlp_ref[...])
        send(FIRST["fc2_weight"] + (part + 1) * (D // TILE) * across)
    if not stepwise:
        sent.append(pltpu.make_async_copy(whole_ref, outs[0], sems.at[0]))
        sent[0].start()
    for copy in sent:
        copy.wait()


def weight_back(places, position, stepwise, ins):
    cores = places.sizes["c"]
    counts = [TILES // (2 * cores)] * (2 * cores) if stepwise else [TILES]
    return pl.pallas_call(
        functools.partial(weight_back_kernel, places, stepwise),
        grid_spec=pltpu.PrefetchScalarGridSpec(
            num_scalar_prefetch=1,
            grid=(1,),
            in_specs=[ANYWHERE] * len(ins),
            out_specs=[ANYWHERE] * len(counts),
            scratch_shapes=[pltpu.VMEM(array.shape, array.dtype) for array in ins]
            + [
                pltpu.VMEM((TILES, TILE, LANES), jnp.bfloat16),
                pltpu.SemaphoreType.DMA((len(ins),)),
                pltpu.SemaphoreType.DMA((2 * places.count,)),
            ],
        ),
        out_shape=[low_like(count, TILE, LANES) for count in counts],
        compiler_params=PARAMS,
        name="weight_back",
    )(position, *ins)


def input_back_kernel(project_ref, grad_middle_ref, hidden_ref, vectors_ref, tiles_ref, out_ref, sums_ref, total_ref):
    across = D // LANES
    for part in range(3):
        weight = load_weight(tiles_ref, 0, "qkv_weight", 0, D // TILE, part * across, across)
        rows = product(project_ref[part], weight, NT)
        total_ref[...] = rows if part == 0 else total_ref[...] + rows
    normal, inverse = norm_parts(hidden_ref[...])
    grad_normed = total_ref[...]
    put_vector(sums_ref, 0, grad_normed * normal)
    put_vector(sums_ref, VECTOR_ROWS, grad_normed)
    put_vector(sums_ref, 2 * VECTOR_ROWS, project_ref[0].astype(jnp.float32))
    put_vector(sums_ref, 3 * VECTOR_ROWS, project_ref[2].astype(jnp.float32))
    out_ref[...] = grad_middle_ref[...] + norm_back(
        grad_normed, normal, inverse, vector(vectors_ref, "norm1_gain")
    )


def input_back(grad_project, grad_middle, hidden, vectors, tiles):
    rows = hidden.shape[0]
    ins = [grad_project, grad_middle, hidden, vectors]
    return pl.pallas_call(
        input_back_kernel,
        grid=(1,),
        in_specs=[whole_spec(array.shape) for array in ins] + [whole_spec((MLP_FIRST, TILE, LANES))],
        out_specs=[whole_spec((rows, D)), whole_spec((LATER * VECTOR_ROWS, LANES))],
        out_shape=[full_like(rows, D), full_like(LATER * VECTOR_ROWS, LANES)],
        scratch_shapes=[pltpu.VMEM((rows, D), jnp.float32)],
        compiler_params=PARAMS,
        name="input_back",
    )(*ins, tiles)


def pad_kernel(images_ref, rows_ref):
    rows_ref[:SEQ] = images_ref[0].astype(jnp.float32)
    rows_ref[SEQ:] = jnp.zeros((ROWS - SEQ, D), jnp.float32)


def pad_rows(images):
    count = images.shape[0]
    return pl.pallas_call(
        pad_kernel,
        grid=(count,),
        in_specs=[pl.BlockSpec((1, SEQ, D), lambda i: (i, 0, 0))],
        out_specs=pl.BlockSpec((ROWS, D), lambda i: (i, 0)),
        out_shape=jax.ShapeDtypeStruct((count * ROWS, D), jnp.float32),
        name="pad_rows",
    )(images)


def cut_rows(rows):
    return rows.reshape(-1, ROWS, D)[:, :SEQ].astype(jnp.bfloat16)


class Places:
    def __init__(self, dp, fsdp):
        low = 2 if dp % 2 == 0 else 1
        core = 2 if fsdp % 2 == 0 else 1
        self.sizes = {"y": low, "x": dp // low, "z": fsdp // core, "c": core}
        self.count = dp * fsdp
        grid = np.arange(self.count).reshape(tuple(self.sizes.values()))
        self.grid = grid
        self.axis = {name: i for i, name in enumerate(self.sizes)}

    def exchange(self, block, axis, hop):
        size = self.sizes[axis]
        target = np.take(self.grid, np.arange(size) ^ hop, axis=self.axis[axis])
        perm = [(int(a), int(b)) for a, b in zip(self.grid.reshape(-1), target.reshape(-1))]
        return lax.ppermute(block, AXES, perm)

    def hops(self, axis):
        return range(1, self.sizes[axis])

    def powers(self, axis):
        return [1 << bit for bit in range(self.sizes[axis].bit_length() - 1)]

    def total(self, block, axes):
        for axis in axes:
            for hop in self.powers(axis):
                block = block + self.exchange(block, axis, hop)
        return block

    def position(self, me):
        return jnp.stack([(me // int(np.prod(self.grid.shape[i + 1 :]))) % n for i, n in enumerate(self.grid.shape)])


def block_at(at_ref, places, offset):
    number = 0
    for i, size in enumerate(places.grid.shape):
        number = number * size + (at_ref[i] ^ offset[i])
    return number


def copies_in(places, at_ref, parts, slots, whole_ref, sems):
    copies = []
    for part, listed in zip(parts, slots):
        count = part.shape[0] // len(listed)
        for i, slot in enumerate(listed):
            start = 0 if slot is None else block_at(at_ref, places, slot[0]) * (TILES // places.count) + slot[1]
            target = whole_ref.at[pl.ds(start, count)]
            copies.append(pltpu.make_async_copy(part.at[pl.ds(i * count, count)], target, sems.at[len(copies)]))
    return copies


def offset_of(**hops):
    return tuple(hops.get(axis, 0) for axis in ("y", "x", "z", "c"))


def join(blocks):
    return jnp.concatenate(blocks, axis=0) if len(blocks) > 1 else blocks[0]


ORDERS = (("x", "y"), ("y", "x"))


def group_of(shares, offsets):
    half = shares[0].shape[0] // 2
    return [(join([share[part * half : (part + 1) * half] for share in shares]), offsets) for part in range(2)]


def merge(*groups):
    return [(join([group[part][0] for group in groups]), sum((group[part][1] for group in groups), [])) for part in range(2)]


def fetch_column(places, share):
    return [places.exchange(share, "z", hop) for hop in places.hops("z")]


def column_offsets(places):
    return [offset_of(z=hop) for hop in range(places.sizes["z"])]


def fetch_plane(places, group, step):
    arrived = []
    for (block, offsets), order in zip(group, ORDERS):
        at = places.axis[order[step]]
        hops = range(1, places.sizes[order[step]])
        moved = [offset[:at] + (hop,) + offset[at + 1 :] for hop in hops for offset in offsets]
        arrived.append((join([places.exchange(block, order[step], hop) for hop in hops]), moved))
    return arrived


def fetch_plane_with(places, group, step, rows):
    (block, offsets), order = group[0], ORDERS[0]
    count, axis = block.shape[0], order[step]
    hops = range(1, places.sizes[axis])
    arrived = [places.exchange(jnp.concatenate([block, rows], axis=0), axis, hop) for hop in hops]
    moved = [tuple(hop if i == places.axis[axis] else part for i, part in enumerate(o)) for hop in hops for o in offsets]
    rows = sum([piece[count:] for piece in arrived], rows)
    other = fetch_plane(places, group, step)[1]
    return [(join([piece[:count] for piece in arrived]), moved), other], rows


def list_core(places, groups):
    parts = []
    for group in groups:
        half = TILES // places.count // 2
        parts += [(block, [(offset, part * half) for offset in offsets]) for part, (block, offsets) in enumerate(group)]
    return parts


def gather_core(places, groups):
    parts = list_core(places, groups)
    return [(join([block for block, _ in parts]), sum((slots for _, slots in parts), []))]


def fetch_core(places, parts):
    arrived = []
    for hop in range(1, places.sizes["c"]):
        for block, slots in parts:
            moved = [(offset[:3] + (hop,), first) for offset, first in slots]
            arrived.append((places.exchange(block, "c", hop), moved))
    return parts + arrived


def add_low(*blocks):
    total = blocks[0].astype(jnp.float32)
    for block in blocks[1:]:
        total = total + block.astype(jnp.float32)
    return total


def send_core(places, parts):
    cores = places.sizes["c"]
    halves = [parts[:cores], parts[cores:]]
    return [[mine] + [places.exchange(other, "c", hop) for hop, other in enumerate(others, 1)] for mine, *others in halves]


def plane_totals(places, blocks, axis):
    share = blocks[0].shape[0] // places.sizes[axis]
    cuts = [slice(i * share, (i + 1) * share) for i in range(places.sizes[axis])]
    return [add_low(*[block[cut] for block in blocks]).astype(jnp.bfloat16) for cut in cuts]


def send_totals(places, totals, axis):
    return totals[:1] + [places.exchange(total, axis, hop) for hop, total in enumerate(totals[1:], 1)]


def send_plane(places, sums, step):
    axes = [order[step] for order in ORDERS]
    return [send_totals(places, plane_totals(places, blocks, axis), axis) for blocks, axis in zip(sums, axes)]


def send_plane_tied(places, sums, step, later):
    (first, second), axes = sums, [order[step] for order in ORDERS]
    first, later = tie(first, later)
    first = plane_totals(places, first, axes[0])
    second, first, later = tie(second, first, later)
    result = [send_totals(places, first, axes[0])]
    second, later = tie(plane_totals(places, second, axes[1]), later)
    return result + [send_totals(places, second, axes[1])], later


def column_totals(places, sums):
    count = places.sizes["z"]
    share = sums[0][0].shape[0] // count
    cuts = [slice(hop * share, (hop + 1) * share) for hop in range(count)]
    return [join([add_low(*[block[cut] for block in blocks]).astype(jnp.bfloat16) for blocks in sums]) for cut in cuts]


def send_column(places, totals):
    return [totals[0]] + [places.exchange(total, "z", hop) for hop, total in enumerate(totals[1:], 1)]


class Layer:
    def __init__(self, places, position, counts, vectors):
        self.places, self.position, self.counts, self.vectors = places, position, counts, vectors

    def project(self, hidden, parts):
        normed, qkv, tiles = project(self.places, self.position, parts, hidden, self.vectors)
        self.saved = dict(hidden=hidden, normed=normed, qkv=qkv, tiles=tiles)

    def attend(self):
        saved = self.saved
        saved["attended"], saved["weights"] = attention(self.counts, saved["qkv"], self.bias)

    def finish(self):
        saved = self.saved
        names = ("branch", "middle", "normed2", "activ", "slope", "mlp_out")
        result, *kept = mlp(saved["attended"], saved["hidden"], self.vectors, saved["tiles"])
        saved.update(zip(names, kept))
        return result

    def back_mlp(self, grad):
        return mlp_back(grad, self.saved, self.vectors, self.saved["tiles"])

    def back_attention(self, passed):
        return attention_back(self.saved["qkv"], passed[1], self.saved["weights"])

    def back_weights(self, passed, grad_project, stepwise):
        _, _, grad_mlp, grad_pre, grad_branch, _ = passed
        saved = self.saved
        ins = [saved["normed"], grad_project, saved["attended"], grad_branch, saved["normed2"], grad_pre]
        return weight_back(self.places, self.position, stepwise, ins + [saved["activ"], grad_mlp])

    def back_input(self, passed, grad_project):
        return input_back(grad_project, passed[0], self.saved["hidden"], self.vectors, self.saved["tiles"])


def scatter_whole(parts):
    whole = parts[0].reshape(-1, LANES)
    return lax.psum_scatter(whole, AXES, scatter_dimension=0, tiled=True).astype(jnp.float32)


def local(dp, fsdp, tokens, counts, params_first, params_second, cotangent):
    devices = dp * fsdp
    places = Places(dp, fsdp)
    stepwise = TILES % (4 * devices) == 0 and all(size & (size - 1) == 0 for size in places.sizes.values())
    share_rows = TILES * TILE // devices
    me = lax.axis_index(AXES)
    position = places.position(me)
    owned = Owned([params_first, params_second], me, devices)
    own = owned.share(0)
    small_rows = owned.small_rows(own)
    tokens, cotangent, small_rows = tie(tokens, cotangent, small_rows)
    hidden, grad_output = pad_rows(tokens), pad_rows(cotangent)

    if stepwise:
        own = own.reshape(-1, TILE, LANES)
        column = fetch_column(places, own)
        near, small_rows = tie(group_of([own], [offset_of()]), small_rows)
        small_rows = small_rows.reshape(-1, TILE, LANES)
        near_first, small_rows = fetch_plane_with(places, near, 0, small_rows)
        near_first, small_rows = tie(near_first, small_rows)
        near_second, small_rows = fetch_plane_with(places, merge(near, near_first), 1, small_rows)
        small_rows = places.total(small_rows, "c")
        next_own, near_first = tie(owned.share(1, own), near_first)
        far, near_second = tie(group_of(column, column_offsets(places)[1:]), near_second)
        far_first = fetch_plane(places, far, 0)
        next_own, small_rows, far, hidden, grad_output = tie(next_own, small_rows, far, hidden, grad_output)
        next_own = jnp.concatenate([next_own, small_rows.reshape(-1, LANES)], axis=0)
        next_shares = [next_own] + fetch_column(places, next_own)
        small_rows = sum([rows[share_rows:] for rows in next_shares[1:]], next_own[share_rows:])
        small_rows = small_rows.reshape(2, -1, LANES)
        vectors = small_rows.astype(jnp.float32)
        next_shares = [rows[:share_rows].reshape(-1, TILE, LANES) for rows in next_shares]
        group = group_of(next_shares, column_offsets(places))
        far_second = fetch_plane(places, merge(far, far_first), 1)
        early = gather_core(places, [near, near_first, near_second, far, far_first])
    else:
        small_rows = lax.psum(small_rows, AXES)
    if stepwise:
        far_second, early, group, small_rows, vectors = tie(far_second, early, group, small_rows, vectors)
        first = fetch_plane(places, group, 0)
        parts = fetch_core(places, early) + fetch_core(places, list_core(places, [far_second]))
        first_layer = Layer(places, position, counts, vectors[0])
        parts, group = tie(parts, group)
        second_early = fetch_plane(places, group, 1)
        first_layer.project(hidden, parts)
        entries, first_layer.saved = tie(table_entries(small_rows), first_layer.saved)
        first_layer.bias, second_bias = bias_of(entries[0]), bias_of(entries[1])
        first, second_early, first_layer.bias, second_bias = tie(first, second_early, first_layer.bias, second_bias)
        second = fetch_plane(places, first, 1)
        next_parts = fetch_core(places, list_core(places, [first, second_early]))
        first_layer.attend()
        result = first_layer.finish()
        next_parts, result = tie(next_parts, result)
        next_parts += fetch_core(places, gather_core(places, [group]))
        second, next_parts, result = tie(second, next_parts, result)
        next_parts += fetch_core(places, list_core(places, [second]))
    else:
        vectors = small_rows.astype(jnp.float32)
        entries = table_entries(small_rows)
        second_bias = bias_of(entries[1])
        parts, next_parts = [
            [(lax.all_gather(share, AXES, axis=0, tiled=True).reshape(TILES, TILE, LANES), [None])]
            for share in (own, owned.share(1))
        ]
        first_layer = Layer(places, position, counts, vectors[0])
        first_layer.project(hidden, parts)
        first_layer.bias = bias_of(entries[0])
        first_layer.attend()
        result = first_layer.finish()
    second_layer = Layer(places, position, counts, vectors[1])
    second_layer.bias = second_bias
    second_layer.project(result, next_parts)
    second_layer.attend()
    result = second_layer.finish()
    output = cut_rows(result)

    next_passed = second_layer.back_mlp(grad_output)
    next_project, next_bias = second_layer.back_attention(next_passed)
    parts = second_layer.back_weights(next_passed, next_project, stepwise)
    if stepwise:
        sums = send_core(places, parts)
    else:
        next_share = scatter_whole(parts)
    grad, next_sums = second_layer.back_input(next_passed, next_project)
    if stepwise:
        sums, grad = send_plane_tied(places, sums, 0, grad)
    passed = first_layer.back_mlp(grad)
    project_grad, bias = first_layer.back_attention(passed)
    parts = first_layer.back_weights(passed, project_grad, stepwise)
    if stepwise:
        sums, parts, passed, project_grad = tie(sums, parts, passed, project_grad)
        sums = send_plane(places, sums, 1)
        own_sums = send_core(places, parts)
    else:
        share = scatter_whole(parts)
    if stepwise:
        own_sums, later = send_plane_tied(places, own_sums, 0, (bias, passed, project_grad))
        sums, (bias, passed, project_grad) = tie(sums, later)
        sums = send_column(places, column_totals(places, sums))
    grad, own_row_sums = first_layer.back_input(passed, project_grad)
    small_grads = small_gradients(
        [own_row_sums, next_sums], [passed[5], next_passed[5]], tables_from_biases(bias, next_bias)
    )
    flat_share = FlatShare(me, devices, params_first.shape[0] * devices)
    if stepwise:
        own_sums, sums, small_grads = tie(own_sums, sums, small_grads)
        own_sums = send_plane(places, own_sums, 1)
        small_grads = places.total(small_grads, "zc")
        own_sums, small_grads = tie(own_sums, small_grads)
        own_sums = send_column(places, column_totals(places, own_sums))
        small_grads = places.total(small_grads, "xy")
        small_grads, sums = tie(small_grads, sums)
        grad_second = flat_share(add_low(*sums).reshape(-1, LANES), small_grads[1])
        own_sums, grad_second, output, grad_tokens = tie(own_sums, grad_second, output, cut_rows(grad))
        share = add_low(*own_sums).reshape(-1, LANES)
    else:
        small_grads = lax.psum(small_grads, AXES)
        grad_second = flat_share(next_share, small_grads[1])
        grad_tokens = cut_rows(grad)
    grad_first = flat_share(share, small_grads[0])
    return output, grad_tokens, grad_first, grad_second


def solution(mesh):
    return jax.shard_map(
        functools.partial(local, mesh.shape["dp"], mesh.shape["fsdp"]),
        mesh=mesh,
        in_specs=(P(AXES, None, None), P(AXES), P(AXES), P(AXES), P(AXES, None, None)),
        out_specs=(P(AXES, None, None), P(AXES, None, None), P(AXES), P(AXES)),
        check_vma=False,
    )
```

```python
import functools
import math

import jax
import jax.numpy as jnp
import numpy as np
from jax import lax
from jax.experimental import pallas as pl
from jax.experimental.pallas import tpu as pltpu
from jax.sharding import PartitionSpec as P

D = 768
HEADS = 12
HEAD = D // HEADS
FF = 3072
GRID = 14
SEQ = 197
RELS = 732
ROWS = 208
LANES = 128
TILE = 16
AXES = ("dp", "fsdp")
VMEM_LIMIT = 56 * 2**20

EPSILON = 1e-06
NEGATIVE = -1000000000.0

ENTRIES = [
    ("norm1_gain", (D,)),
    ("norm1_bias", (D,)),
    ("qkv_weight", (D, 3 * D)),
    ("query_bias", (D,)),
    ("value_bias", (D,)),
    ("relative_table", (RELS, HEADS)),
    ("proj_weight", (D, D)),
    ("proj_bias", (D,)),
    ("gamma_attn", (D,)),
    ("norm2_gain", (D,)),
    ("norm2_bias", (D,)),
    ("fc1_weight", (D, FF)),
    ("fc1_bias", (FF,)),
    ("fc2_weight", (FF, D)),
    ("fc2_bias", (D,)),
    ("gamma_mlp", (D,)),
]
WEIGHTS = {name: dims for name, dims in ENTRIES if name.endswith("weight")}
SIZES = dict(ENTRIES)
VECTORS = [
    "norm1_gain",
    "norm1_bias",
    "query_bias",
    "value_bias",
    "proj_bias",
    "gamma_attn",
    "norm2_gain",
    "norm2_bias",
    "fc2_bias",
    "gamma_mlp",
]
ROW = {name: i for i, name in enumerate(VECTORS)}


def count_rows(dims):
    return -(-math.prod(dims) // LANES)


def virtual_starts():
    starts, at = {}, 0
    for name, dims in ENTRIES:
        starts[name] = at
        at += count_rows(dims)
    return starts, at


STARTS, VIRTUAL = virtual_starts()
SHIFT = RELS * HEADS % LANES
TABLE_END = STARTS["proj_weight"]


def tile_order():
    parts = []
    for name, (depth, width) in WEIGHTS.items():
        across = width // LANES
        rows = STARTS[name] + np.arange(depth * across).reshape(depth // TILE, TILE, across)
        parts.append(rows.transpose(0, 2, 1).reshape(-1))
    return np.concatenate(parts)


def small_order():
    groups = [VECTORS, ["fc1_bias"], ["relative_table"]]
    rows = []
    for group in groups:
        for name in group:
            rows += [STARTS[name] + i for i in range(count_rows(SIZES[name]))]
        rows += [-1] * (-len(rows) % 8)
    return np.array(rows)


TILE_ROWS = tile_order()
SMALL_ROWS = small_order()
TILES = len(TILE_ROWS) // TILE


def tie(*trees):
    leaves, structure = jax.tree.flatten(trees)
    tied = iter(lax.optimization_barrier([leaf for leaf in leaves if isinstance(leaf, jax.Array)]))
    return structure.unflatten([next(tied) if isinstance(leaf, jax.Array) else leaf for leaf in leaves])


def halo(block, before, after, devices, join=True):
    rows = block.shape[-2]
    pieces = [block] if join else []
    for hop in range(1, -(-before // rows) + 1):
        take = min(rows, before - (hop - 1) * rows)
        perm = [(i, i + hop) for i in range(devices - hop)]
        pieces.insert(0, lax.ppermute(block[..., rows - take :, :], AXES, perm))
    for hop in range(1, -(-after // rows) + 1):
        take = min(rows, after - (hop - 1) * rows)
        perm = [(i + hop, i) for i in range(devices - hop)]
        pieces.append(lax.ppermute(block[..., :take, :], AXES, perm))
    return jnp.concatenate(pieces, axis=-2)


def pick_rows(index, source):
    chosen = index[:, None] == lax.broadcasted_iota(jnp.int32, (1, source.shape[0]), 1)
    return jnp.dot(chosen.astype(jnp.bfloat16), source.astype(jnp.bfloat16), preferred_element_type=jnp.float32)


def round_up(value, unit):
    return -(-value // unit) * unit


class Owned:
    def __init__(self, flats, me, devices):
        length = flats[0].shape[0] // LANES
        share = len(TILE_ROWS) // devices
        starts = np.arange(devices)[:, None] * length
        wanted = TILE_ROWS.reshape(devices, share) - starts
        before = round_up(max(0, -wanted.min()) + 1, TILE)
        after = round_up(max(0, wanted.max() + 1 - length), TILE)
        smalls = SMALL_ROWS[None] - starts
        smalls = np.where((smalls >= 0) & (smalls < length), smalls + before - 1, -1)
        self.wanted = self.mine(wanted + before - 1, me)
        self.smalls = self.mine(smalls, me)
        around = halo(jnp.stack([flat.reshape(length, LANES) for flat in flats]), before, after, devices)
        shifted = jnp.concatenate([around[:, :-1, SHIFT:], around[:, 1:, :SHIFT]], axis=2)
        at = me * length - before + 1 + lax.broadcasted_iota(jnp.int32, (1, shifted.shape[1], 1), 1)
        self.virtual = jnp.where(at < TABLE_END, around[:, 1:], shifted)

    @staticmethod
    def mine(table, me):
        return lax.dynamic_index_in_dim(jnp.asarray(table.astype(np.int32)), me, 0, keepdims=False)

    def small_rows(self, *after):
        virtual, *_ = tie(self.virtual, *after)
        return jnp.stack([pick_rows(self.smalls, rows).astype(jnp.bfloat16) for rows in virtual])

    def share(self, number, *after):
        rows = self.virtual[number]
        if after:
            rows, *_ = tie(rows, *after)
        return pick_rows(self.wanted, rows).astype(jnp.bfloat16)


class FlatShare:
    def __init__(self, me, devices, flat_length):
        length = flat_length // LANES // devices
        share = len(TILE_ROWS) // devices
        place = np.full(max(VIRTUAL, devices * length + 1), -1, np.int64)
        place[TILE_ROWS] = np.arange(len(TILE_ROWS))
        small_place = np.full(place.shape, -1, np.int64)
        small_place[SMALL_ROWS[SMALL_ROWS >= 0]] = np.flatnonzero(SMALL_ROWS >= 0)
        span = np.arange(devices)[:, None] * length + np.arange(length + 1)[None]
        relative = place[span] - np.arange(devices)[:, None] * share
        has = place[span] >= 0
        self.before = round_up(max(0, -relative[has].min()), TILE)
        self.after = round_up(max(0, relative[has].max() + 1 - share), TILE)
        smalls_at = self.before + share + self.after
        index = np.where(has, relative + self.before, -1)
        index = np.where(small_place[span] >= 0, small_place[span] + smalls_at, index)
        self.index = Owned.mine(index, me)
        self.at = me * length + lax.broadcasted_iota(jnp.int32, (length, 1), 0)
        self.devices = devices

    def __call__(self, owned, smalls):
        owned = owned.astype(jnp.bfloat16)
        share = owned.shape[0]
        around = halo(owned, self.before, self.after, self.devices, join=False)
        ends = self.before + share
        here = jnp.concatenate([owned, smalls.astype(jnp.bfloat16)], axis=0)
        index = self.index - self.before
        outside = (self.index < self.before) | ((self.index >= ends) & (self.index < ends + self.after))
        index = jnp.where(outside, -1, jnp.where(self.index >= ends, index - self.after, index))
        virtual = pick_rows(index, here)
        index = jnp.where(self.index < self.before, self.index, self.index - share)
        index = jnp.where(outside, index, -1)
        virtual = virtual + pick_rows(index, around)
        here, following = virtual[:-1], virtual[1:]
        lane = lax.broadcasted_iota(jnp.int32, (1, LANES), 1)
        shifted = jnp.concatenate([here[:, LANES - SHIFT :], following[:, : LANES - SHIFT]], axis=1)
        straight = (self.at < TABLE_END - 1) | ((self.at == TABLE_END - 1) & (lane < SHIFT))
        return jnp.where(straight, here, shifted).reshape(-1)


VECTOR_ROWS = D // LANES
FC1_AT = round_up(len(VECTORS) * VECTOR_ROWS, 8)
TABLE_AT = FC1_AT + FF // LANES
TABLE_ROWS = count_rows(SIZES["relative_table"])
LATER = 4


def table_entries(rows):
    tables = rows[:, TABLE_AT : TABLE_AT + TABLE_ROWS].reshape(2, -1)[:, : RELS * HEADS].reshape(2, RELS, HEADS)
    return jnp.pad(tables.transpose(0, 2, 1), ((0, 0), (0, 16 - HEADS), (0, ENTRY_LANES - RELS)))


def small_gradients(first, later, tables):
    tables = tables.reshape(2, RELS * HEADS)
    tables = jnp.pad(tables, ((0, 0), (0, round_up(TABLE_ROWS, 8) * LANES - RELS * HEADS))).reshape(2, -1, LANES)
    return jnp.concatenate([jnp.stack(first), jnp.stack(later), tables], axis=1)


SIDE = 2 * GRID - 1
WINDOW = round_up(SIDE * GRID, LANES) + LANES
WIDE = round_up(ROWS, LANES)


ENTRY_LANES = round_up(RELS, LANES)
HEAD_ROWS = 2 * 16


def entry_choice(column, transposed):
    shape = (1, WINDOW) if transposed else (WINDOW, 1)
    source = lax.broadcasted_iota(jnp.int32, shape, 1 if transposed else 0)
    group = source // GRID
    target = (SIDE - 1 - group) * SIDE - (source - group * GRID) + GRID - 1 + column
    target = jnp.where(source < SIDE * GRID, target, -1)
    entries = (ENTRY_LANES, 1) if transposed else (1, ENTRY_LANES)
    entry = lax.broadcasted_iota(jnp.int32, entries, 0 if transposed else 1)
    return (entry == target).astype(jnp.float32).astype(jnp.bfloat16)


def bias_kernel(entries_ref, bias_ref, windows_ref):
    for column in range(GRID):
        windows_ref[column] = product(entries_ref[...], entry_choice(column, True), NN)
    lane = lax.broadcasted_iota(jnp.int32, (1, WIDE), 1)
    inner = (lane >= 1) & (lane < SEQ)

    def head(i, _):
        ends = entries_ref[pl.ds(pl.multiple_of(i // 16 * 16, 16), 16), :].astype(jnp.float32)
        picked = lax.broadcasted_iota(jnp.int32, (16, 1), 0) == i % 16
        ends = jnp.sum(jnp.where(picked, ends, 0.0), axis=0, keepdims=True)
        top, left, corner = [ends[:, RELS - k : RELS - k + 1] for k in (3, 2, 1)]
        bias_ref[i] = jnp.zeros(bias_ref.shape[1:], jnp.float32)
        bias_ref[i, 0:1] = jnp.where(inner, top, jnp.where(lane == 0, corner, 0.0))[:, :ROWS]
        spread = jnp.concatenate([windows_ref[column, pl.ds(i, 1)] for column in range(GRID)], axis=0)
        for row in range(GRID):
            start = (GRID - 1 - row) * GRID
            window = pltpu.roll(spread, (1 - start) % WINDOW, 1)[:, :WIDE]
            window = jnp.where(inner, window, jnp.where(lane == 0, left, 0.0))
            bias_ref[i, 1 + row * GRID : 1 + (row + 1) * GRID] = window[:, :ROWS]
        return 0

    lax.fori_loop(0, HEADS, head, 0)


def bias_of(entries):
    return pl.pallas_call(
        bias_kernel,
        grid=(1,),
        in_specs=[pl.BlockSpec(entries.shape, lambda i: (0, 0))],
        out_specs=pl.BlockSpec((HEADS, ROWS, ROWS), lambda i: (0, 0, 0)),
        out_shape=jax.ShapeDtypeStruct((HEADS, ROWS, ROWS), jnp.float32),
        scratch_shapes=[pltpu.VMEM((GRID, 16, WINDOW), jnp.float32)],
        compiler_params=pltpu.CompilerParams(vmem_limit_bytes=VMEM_LIMIT),
        name="bias",
    )(entries)


def table_kernel(first_ref, second_ref, out_ref, windows_ref, ends_ref):
    lane = lax.broadcasted_iota(jnp.int32, (1, ROWS), 1)
    inner = (lane >= 1) & (lane < SEQ)
    entry = lax.broadcasted_iota(jnp.int32, (1, ENTRY_LANES), 1)
    windows_ref[...] = jnp.zeros_like(windows_ref)
    ends_ref[...] = jnp.zeros_like(ends_ref)
    for number, grad_ref in enumerate((first_ref, second_ref)):

        def head(i, _, number=number, grad_ref=grad_ref):
            total = jnp.zeros((GRID, WINDOW), jnp.float32)
            left = jnp.zeros((1, 1), jnp.float32)
            for row in range(GRID):
                start = (GRID - 1 - row) * GRID
                block = grad_ref[i, 1 + row * GRID : 1 + (row + 1) * GRID]
                left = left + jnp.sum(jnp.where(lane == 0, block, 0.0), keepdims=True)
                block = jnp.where(inner, block, 0.0)
                block = jnp.concatenate([block, jnp.zeros((GRID, WINDOW - ROWS), jnp.float32)], axis=1)
                total = total + pltpu.roll(block, (start - 1) % WINDOW, 1)
            at = pl.ds(number * 16 + i, 1)
            for column in range(GRID):
                windows_ref[column, at] = total[column : column + 1]
            first = grad_ref[i, 0:1]
            top = jnp.sum(jnp.where(inner, first, 0.0), keepdims=True)
            corner = jnp.sum(jnp.where(lane == 0, first, 0.0), keepdims=True)
            ends = jnp.where(entry == RELS - 3, top, jnp.where(entry == RELS - 2, left, 0.0))
            ends_ref[at] = jnp.where(entry == RELS - 1, corner, ends)
            return 0

        lax.fori_loop(0, HEADS, head, 0)
    out_ref[...] = ends_ref[...]
    for column in range(GRID):
        rows = windows_ref[column]
        high = rows.astype(jnp.bfloat16)
        low = (rows - high.astype(jnp.float32)).astype(jnp.bfloat16)
        chosen = entry_choice(column, False)
        out_ref[...] += product(high, chosen, NN) + product(low, chosen, NN)


def tables_from_biases(first, second):
    entries = pl.pallas_call(
        table_kernel,
        grid=(1,),
        in_specs=[pl.BlockSpec(first.shape, lambda i: (0, 0, 0))] * 2,
        out_specs=pl.BlockSpec((HEAD_ROWS, ENTRY_LANES), lambda i: (0, 0)),
        out_shape=jax.ShapeDtypeStruct((HEAD_ROWS, ENTRY_LANES), jnp.float32),
        scratch_shapes=[
            pltpu.VMEM((GRID, HEAD_ROWS, WINDOW), jnp.float32),
            pltpu.VMEM((HEAD_ROWS, ENTRY_LANES), jnp.float32),
        ],
        compiler_params=pltpu.CompilerParams(vmem_limit_bytes=VMEM_LIMIT),
        name="table_back",
    )(first, second)
    return entries.reshape(2, 16, ENTRY_LANES)[:, :HEADS, :RELS].transpose(0, 2, 1)


NT = (((1,), (1,)), ((), ()))
NN = (((1,), (0,)), ((), ()))
TN = (((0,), (0,)), ((), ()))


def product(left, right, dims):
    return lax.dot_general(left, right, dims, preferred_element_type=jnp.float32)


def own_lanes(head):
    lane = lax.broadcasted_iota(jnp.int32, (1, LANES), 1)
    return lane < HEAD if head == 0 else lane >= HEAD


def head_weights(query, key, bias, count, head):
    chosen = jnp.where(own_lanes(head), query, jnp.zeros_like(query))
    scores = product(chosen, key, NT) + bias
    column = lax.broadcasted_iota(jnp.int32, (1, ROWS), 1)
    scores = jnp.where(column < count, scores, NEGATIVE)
    grown = jnp.exp(scores - jnp.max(scores, axis=1, keepdims=True))
    return grown * (1.0 / jnp.sum(grown, axis=1, keepdims=True))


def attention_kernel(pairs, counts_ref, query_ref, key_ref, value_ref, bias_ref, out_ref, weights_ref):
    count = counts_ref[pl.program_id(1)]
    for pair in range(pairs):
        lanes = slice(pair * LANES, (pair + 1) * LANES)
        query, key, value = query_ref[:, lanes], key_ref[:, lanes], value_ref[:, lanes]
        parts = []
        for head in range(2):
            weights = head_weights(query, key, bias_ref[2 * pair + head], count, head).astype(jnp.bfloat16)
            weights_ref[0, 2 * pair + head] = weights
            parts.append(product(weights, value, NN))
        out_ref[:, lanes] = jnp.where(own_lanes(0), parts[0], parts[1]).astype(jnp.bfloat16)


def attention_back_kernel(pairs, query_ref, key_ref, value_ref, grad_ref, weights_ref, out_ref, db_ref):
    image = pl.program_id(1)

    @pl.when(image == 0)
    def _():
        db_ref[...] = jnp.zeros_like(db_ref)

    for pair in range(pairs):
        lanes = slice(pair * LANES, (pair + 1) * LANES)
        query, key, value, grad = query_ref[:, lanes], key_ref[:, lanes], value_ref[:, lanes], grad_ref[:, lanes]
        dq, dk, dv = [], [], []
        for head in range(2):
            low_weights = weights_ref[0, 2 * pair + head]
            weights = low_weights.astype(jnp.float32)
            chosen = jnp.where(own_lanes(head), grad, jnp.zeros_like(grad))
            weighted = weights * product(chosen, value, NT)
            dv.append(product(low_weights, grad, TN))
            grad_scores = weighted - weights * jnp.sum(weighted, axis=1, keepdims=True)
            low = grad_scores.astype(jnp.bfloat16)
            dq.append(product(low, key, NN))
            dk.append(product(low, query, TN))
            db_ref[2 * pair + head] += grad_scores
        first = own_lanes(0)
        out_ref[0, :, lanes] = (jnp.where(first, dq[0], dq[1]) * HEAD**-0.5).astype(jnp.bfloat16)
        out_ref[1, :, lanes] = jnp.where(first, dk[0], dk[1]).astype(jnp.bfloat16)
        out_ref[2, :, lanes] = jnp.where(first, dv[0], dv[1]).astype(jnp.bfloat16)


def attention_specs(pairs):
    steps = D // LANES // pairs
    lanes = [
        pl.BlockSpec((ROWS, pairs * LANES), lambda step, image, *_, part=part: (image, part * steps + step))
        for part in range(3)
    ]
    bias = pl.BlockSpec((2 * pairs, ROWS, ROWS), lambda step, image, *_: (step, 0, 0))
    weights = pl.BlockSpec((1, 2 * pairs, ROWS, ROWS), lambda step, image, *_: (image, step, 0, 0))
    return steps, lanes, bias, weights


def attention(counts, qkv, bias, pairs=6):
    images = qkv.shape[0] // ROWS
    steps, lanes, bias_spec, weights_spec = attention_specs(pairs)
    return pl.pallas_call(
        functools.partial(attention_kernel, pairs),
        grid_spec=pltpu.PrefetchScalarGridSpec(
            num_scalar_prefetch=1,
            grid=(steps, images),
            in_specs=lanes + [bias_spec],
            out_specs=[lanes[0], weights_spec],
        ),
        out_shape=[
            jax.ShapeDtypeStruct((qkv.shape[0], D), jnp.bfloat16),
            jax.ShapeDtypeStruct((images, HEADS, ROWS, ROWS), jnp.bfloat16),
        ],
        compiler_params=pltpu.CompilerParams(vmem_limit_bytes=VMEM_LIMIT),
        name="attention",
    )(counts, qkv, qkv, qkv, bias)


def attention_back(qkv, grad, weights, pairs=3):
    images = qkv.shape[0] // ROWS
    steps, lanes, bias_spec, weights_spec = attention_specs(pairs)
    return pl.pallas_call(
        functools.partial(attention_back_kernel, pairs),
        grid=(steps, images),
        in_specs=lanes + [lanes[0], weights_spec],
        out_specs=[
            pl.BlockSpec((3, ROWS, pairs * LANES), lambda step, image: (0, image, step)),
            bias_spec,
        ],
        out_shape=[
            jax.ShapeDtypeStruct((3, qkv.shape[0], D), jnp.bfloat16),
            jax.ShapeDtypeStruct((HEADS, ROWS, ROWS), jnp.float32),
        ],
        compiler_params=pltpu.CompilerParams(vmem_limit_bytes=VMEM_LIMIT),
        name="attention_back",
    )(qkv, qkv, qkv, grad, weights)


def tile_starts():
    starts, at = {}, 0
    for name, (depth, width) in WEIGHTS.items():
        starts[name] = at
        at += depth // TILE * (width // LANES)
    return starts


FIRST = tile_starts()
MLP_FIRST = FIRST["proj_weight"]
SPAN = 1536


def load_weight(ref, base, name, row, rows, column, columns):
    first, across = FIRST[name] - base, WEIGHTS[name][1] // LANES
    lines = []
    for i in range(rows):
        at = first + (row + i) * across + column
        lines.append(jnp.concatenate([ref[at + j] for j in range(columns)], axis=1))
    return jnp.concatenate(lines, axis=0)


def gelu_and_slope(values):
    size = jnp.abs(values)
    step = 1.0 / (1.0 + (0.3275911 / math.sqrt(2.0)) * size)
    bell = jnp.exp(-0.5 * values * values)
    series = 1.061405429
    for term in (-1.453152027, 1.421413741, -0.284496736, 0.254829592):
        series = series * step + term
    tail = 0.5 * series * step * bell
    area = jnp.where(values < 0, tail, 1.0 - tail)
    return values * area, area + values * bell * (1.0 / math.sqrt(2.0 * math.pi))


def norm_parts(values):
    centre = values - jnp.mean(values, axis=-1, keepdims=True)
    spread = jnp.mean(centre * centre, axis=-1, keepdims=True)
    inverse = lax.rsqrt(spread + EPSILON)
    return centre * inverse, inverse


def norm_back(grad, normal, inverse, gain):
    scaled = grad * gain
    first = jnp.mean(scaled, axis=-1, keepdims=True)
    second = jnp.mean(scaled * normal, axis=-1, keepdims=True)
    return (scaled - first - normal * second) * inverse


def wide_row(ref, first, count):
    return jnp.concatenate([ref[first + i : first + i + 1] for i in range(count)], axis=1)


def vector(ref, name):
    return wide_row(ref, ROW[name] * VECTOR_ROWS, VECTOR_ROWS)


def put_vector(ref, row, values):
    sums = jnp.sum(values, axis=0, keepdims=True)
    for i in range(sums.shape[1] // LANES):
        ref[row + i : row + i + 1] = sums[:, i * LANES : (i + 1) * LANES]


def later_row(name):
    return (ROW[name] - LATER) * VECTOR_ROWS


def whole_spec(shape):
    return pl.BlockSpec(shape, lambda *_: (0,) * len(shape))


ANYWHERE = pl.BlockSpec(memory_space=pl.ANY)
PARAMS = pltpu.CompilerParams(vmem_limit_bytes=VMEM_LIMIT)


def low_like(*shape):
    return jax.ShapeDtypeStruct(shape, jnp.bfloat16)


def full_like(*shape):
    return jax.ShapeDtypeStruct(shape, jnp.float32)


def project_kernel(places, slots, at_ref, *refs):
    parts, refs = refs[: len(slots)], refs[len(slots) :]
    hidden_ref, vectors_ref, normed_ref, qkv_ref, tiles_ref, whole_ref, sems, out_sem = refs
    copies = copies_in(places, at_ref, parts, slots, whole_ref, sems)
    for copy in copies:
        copy.start()
    normal, _ = norm_parts(hidden_ref[...])
    normed_ref[...] = (normal * vector(vectors_ref, "norm1_gain") + vector(vectors_ref, "norm1_bias")).astype(
        jnp.bfloat16
    )
    for copy in copies:
        copy.wait()
    leaving = pltpu.make_async_copy(whole_ref, tiles_ref, out_sem)
    leaving.start()
    across = D // LANES
    for part in range(3):
        weight = load_weight(whole_ref, 0, "qkv_weight", 0, D // TILE, part * across, across)
        rows = product(normed_ref[...], weight, NN)
        if part == 0:
            rows = (rows + vector(vectors_ref, "query_bias")) * HEAD**-0.5
        if part == 2:
            rows = rows + vector(vectors_ref, "value_bias")
        qkv_ref[:, part * D : (part + 1) * D] = rows.astype(jnp.bfloat16)
    leaving.wait()


def project(places, position, parts, hidden, vectors):
    arrays = [array for array, _ in parts]
    slots = [listed for _, listed in parts]
    rows = hidden.shape[0]
    return pl.pallas_call(
        functools.partial(project_kernel, places, slots),
        grid_spec=pltpu.PrefetchScalarGridSpec(
            num_scalar_prefetch=1,
            grid=(1,),
            in_specs=[ANYWHERE] * len(arrays) + [whole_spec((rows, D)), whole_spec(vectors.shape)],
            out_specs=[whole_spec((rows, D)), whole_spec((rows, 3 * D)), ANYWHERE],
            scratch_shapes=[
                pltpu.VMEM((TILES, TILE, LANES), jnp.bfloat16),
                pltpu.SemaphoreType.DMA((sum(len(listed) for listed in slots),)),
                pltpu.SemaphoreType.DMA(()),
            ],
        ),
        out_shape=[low_like(rows, D), low_like(rows, 3 * D), low_like(TILES, TILE, LANES)],
        compiler_params=PARAMS,
        name="project",
    )(position, *arrays, hidden, vectors)


def mlp_weights(tiles_ref, weight_ref, sems, order):
    copies = []
    for i, name in enumerate(order):
        depth, width = WEIGHTS[name]
        count = depth // TILE * (width // LANES)
        here = weight_ref.at[pl.ds(FIRST[name] - MLP_FIRST, count)]
        copies.append(pltpu.make_async_copy(tiles_ref.at[pl.ds(FIRST[name], count)], here, sems.at[i]))
        copies[-1].start()
    return copies


def span_of(step):
    return slice(step * SPAN, (step + 1) * SPAN)


class Leaving:
    def __init__(self, outs, buffers, sems):
        self.outs, self.buffers, self.sems, self.copies = outs, buffers, sems, []

    def start(self, number, columns=None):
        source, target = self.buffers[number], self.outs[number]
        if columns is not None:
            source, target = source.at[:, columns], target.at[:, columns]
        self.copies.append(pltpu.make_async_copy(source, target, self.sems.at[len(self.copies)]))
        self.copies[-1].start()

    def wait(self):
        for copy in self.copies:
            copy.wait()


def mlp_kernel(attended_ref, hidden_ref, vectors_ref, tiles_ref, *refs):
    outs, buffers, (total_ref, weight_ref, sems, out_sems, fc1_bias_ref) = refs[:7], refs[7:14], refs[14:]
    result_ref, branch_ref, middle_ref, normed_ref, activ_ref, slope_ref, mlp_ref = buffers
    leaving = Leaving(outs, buffers, out_sems)
    copies = mlp_weights(tiles_ref, weight_ref, sems, ("proj_weight", "fc1_weight", "fc2_weight"))
    fc1_bias_ref[...] = wide_row(vectors_ref, FC1_AT, FF // LANES)
    copies[0].wait()
    across = D // LANES
    weight = load_weight(weight_ref, MLP_FIRST, "proj_weight", 0, D // TILE, 0, across)
    branch = product(attended_ref[...], weight, NN) + vector(vectors_ref, "proj_bias")
    branch_ref[...] = branch.astype(jnp.bfloat16)
    leaving.start(1)
    middle_ref[...] = hidden_ref[...] + vector(vectors_ref, "gamma_attn") * branch
    leaving.start(2)
    normal, _ = norm_parts(middle_ref[...])
    normed_ref[...] = (normal * vector(vectors_ref, "norm2_gain") + vector(vectors_ref, "norm2_bias")).astype(
        jnp.bfloat16
    )
    leaving.start(3)
    total_ref[...] = jnp.broadcast_to(vector(vectors_ref, "fc2_bias"), total_ref.shape)
    copies[1].wait()

    def step(i, _):
        span = span_of(i)
        weight = load_weight(weight_ref, MLP_FIRST, "fc1_weight", 0, D // TILE, i * (SPAN // LANES), SPAN // LANES)
        activ, slope = gelu_and_slope(product(normed_ref[...], weight, NN) + fc1_bias_ref[:, span])
        activ = activ.astype(jnp.bfloat16)
        activ_ref[:, span] = activ
        slope_ref[:, span] = slope.astype(jnp.bfloat16)
        leaving.start(4, span)
        leaving.start(5, span)
        if i == 0:
            copies[2].wait()
        weight = load_weight(weight_ref, MLP_FIRST, "fc2_weight", i * (SPAN // TILE), SPAN // TILE, 0, across)
        total_ref[...] += product(activ, weight, NN)
        return 0

    for i in range(FF // SPAN):
        step(i, 0)
    result_ref[...] = middle_ref[...] + vector(vectors_ref, "gamma_mlp") * total_ref[...]
    leaving.start(0)
    mlp_ref[...] = total_ref[...].astype(jnp.bfloat16)
    leaving.start(6)
    leaving.wait()


def mlp_scratch(rows, outs):
    return [pltpu.VMEM(out.shape, out.dtype) for out in outs] + [
        pltpu.VMEM((rows, D), jnp.float32),
        pltpu.VMEM((TILES - MLP_FIRST, TILE, LANES), jnp.bfloat16),
        pltpu.SemaphoreType.DMA((3,)),
        pltpu.SemaphoreType.DMA((len(outs) + 2 * (FF // SPAN),)),
    ]


def mlp(attended, hidden, vectors, tiles):
    rows = hidden.shape[0]
    outs = [full_like(rows, D), low_like(rows, D), full_like(rows, D), low_like(rows, D)]
    outs += [low_like(rows, FF), low_like(rows, FF), low_like(rows, D)]
    ins = [attended, hidden, vectors]
    return pl.pallas_call(
        mlp_kernel,
        grid=(1,),
        in_specs=[whole_spec(array.shape) for array in ins] + [ANYWHERE],
        out_specs=[ANYWHERE] * len(outs),
        out_shape=outs,
        scratch_shapes=mlp_scratch(rows, outs) + [pltpu.VMEM((1, FF), jnp.float32)],
        compiler_params=PARAMS,
        name="mlp",
    )(*ins, tiles)


def mlp_back_kernel(grad_ref, branch_ref, middle_ref, slope_ref, mlp_ref, vectors_ref, tiles_ref, *refs):
    outs, buffers, (total_ref, weight_ref, sems, out_sems) = refs[:6], refs[6:12], refs[12:]
    grad_middle_ref, grad_attended_ref, grad_mlp_ref, grad_pre_ref, grad_branch_ref, sums_ref = buffers
    leaving = Leaving(outs, buffers, out_sems)
    copies = mlp_weights(tiles_ref, weight_ref, sems, ("fc2_weight", "fc1_weight", "proj_weight"))
    across = D // LANES
    grad = grad_ref[...]
    sums_ref[...] = jnp.zeros_like(sums_ref)
    put_vector(sums_ref, later_row("gamma_mlp"), grad * mlp_ref[...].astype(jnp.float32))
    grad_mlp = grad * vector(vectors_ref, "gamma_mlp")
    put_vector(sums_ref, later_row("fc2_bias"), grad_mlp)
    grad_mlp_ref[...] = grad_mlp.astype(jnp.bfloat16)
    leaving.start(2)
    total_ref[...] = jnp.zeros_like(total_ref)
    copies[0].wait()

    def step(i, _):
        span = span_of(i)
        weight = load_weight(weight_ref, MLP_FIRST, "fc2_weight", i * (SPAN // TILE), SPAN // TILE, 0, across)
        grad_pre = product(grad_mlp_ref[...], weight, NT) * slope_ref[:, span].astype(jnp.float32)
        sums = jnp.sum(grad_pre, axis=0, keepdims=True)
        sums = jnp.concatenate([sums[:, k * LANES : (k + 1) * LANES] for k in range(SPAN // LANES)], axis=0)
        first = FC1_AT - LATER * VECTOR_ROWS + i * (SPAN // LANES)
        sums_ref[first : first + SPAN // LANES] = sums
        grad_pre = grad_pre.astype(jnp.bfloat16)
        grad_pre_ref[:, span] = grad_pre
        leaving.start(3, span)
        if i == 0:
            copies[1].wait()
        weight = load_weight(weight_ref, MLP_FIRST, "fc1_weight", 0, D // TILE, i * (SPAN // LANES), SPAN // LANES)
        total_ref[...] += product(grad_pre, weight, NT)
        return 0

    for i in range(FF // SPAN):
        step(i, 0)
    normal, inverse = norm_parts(middle_ref[...])
    grad_normed = total_ref[...]
    put_vector(sums_ref, later_row("norm2_gain"), grad_normed * normal)
    put_vector(sums_ref, later_row("norm2_bias"), grad_normed)
    grad_middle = grad_ref[...] + norm_back(grad_normed, normal, inverse, vector(vectors_ref, "norm2_gain"))
    grad_middle_ref[...] = grad_middle
    leaving.start(0)
    put_vector(sums_ref, later_row("gamma_attn"), grad_middle * branch_ref[...].astype(jnp.float32))
    grad_branch = grad_middle * vector(vectors_ref, "gamma_attn")
    put_vector(sums_ref, later_row("proj_bias"), grad_branch)
    leaving.start(5)
    grad_branch_ref[...] = grad_branch.astype(jnp.bfloat16)
    leaving.start(4)
    copies[2].wait()
    weight = load_weight(weight_ref, MLP_FIRST, "proj_weight", 0, D // TILE, 0, across)
    grad_attended_ref[...] = product(grad_branch_ref[...], weight, NT).astype(jnp.bfloat16)
    leaving.start(1)
    leaving.wait()


def mlp_back(grad, saved, vectors, tiles):
    rows = grad.shape[0]
    outs = [full_like(rows, D), low_like(rows, D), low_like(rows, D), low_like(rows, FF), low_like(rows, D)]
    outs += [full_like(TABLE_AT - LATER * VECTOR_ROWS, LANES)]
    ins = [grad, saved["branch"], saved["middle"], saved["slope"], saved["mlp_out"], vectors]
    return pl.pallas_call(
        mlp_back_kernel,
        grid=(1,),
        in_specs=[whole_spec(array.shape) for array in ins] + [ANYWHERE],
        out_specs=[ANYWHERE] * len(outs),
        out_shape=outs,
        scratch_shapes=mlp_scratch(rows, outs),
        compiler_params=PARAMS,
        name="mlp_back",
    )(*ins, tiles)


def scatter_place(places, at_ref, device, part):
    position = np.unravel_index(device, places.grid.shape)
    apart = {name: at_ref[i] ^ int(position[i]) for name, i in places.axis.items()}
    first, second = ORDERS[part]
    slot = (apart[first] * places.sizes[second] + apart[second]) * places.sizes["z"] + apart["z"]
    return apart["c"], slot


def weight_back_kernel(places, stepwise, at_ref, *refs):
    sources, refs = refs[:8], refs[8:]
    outs = refs[: 2 * places.sizes["c"] if stepwise else 1]
    operands, (whole_ref, in_sems, sems) = refs[len(outs) : len(outs) + 8], refs[len(outs) + 8 :]
    coming = [
        pltpu.make_async_copy(source, operand, in_sems.at[i]) for i, (source, operand) in enumerate(zip(sources, operands))
    ]
    for copy in coming:
        copy.start()
    normed_ref, project_ref, attended_ref, branch_ref, normed2_ref, pre_ref, activ_ref, mlp_ref = operands
    across = D // LANES

    def put(name, row, column, left, grad):
        block = product(left, grad, TN).astype(jnp.bfloat16)
        wide = WEIGHTS[name][1] // LANES
        for i in range(D // TILE):
            for j in range(across):
                at = FIRST[name] + (row + i) * wide + column + j
                whole_ref[at] = block[i * TILE : (i + 1) * TILE, j * LANES : (j + 1) * LANES]

    half = TILES // places.count // 2
    sent = []

    def send(ready):
        while stepwise and (len(sent) + 1) * half <= ready:
            number = len(sent)
            core, slot = scatter_place(places, at_ref, number // 2, number % 2)
            source = whole_ref.at[pl.ds(number * half, half)]
            for k in range(places.sizes["c"]):
                target = outs[number % 2 * places.sizes["c"] + k].at[pl.ds(slot * half, half)]
                copy = pltpu.make_async_copy(source, target, sems.at[number])
                pl.when(core == k)(copy.start)
            sent.append(copy)

    coming[0].wait()
    coming[1].wait()
    for part in range(3):
        put("qkv_weight", 0, part * across, normed_ref[...], project_ref[part])
    send(FIRST["proj_weight"])
    coming[2].wait()
    coming[3].wait()
    put("proj_weight", 0, 0, attended_ref[...], branch_ref[...])
    send(FIRST["fc1_weight"])
    coming[4].wait()
    coming[5].wait()
    for part in range(FF // D):
        put("fc1_weight", 0, part * across, normed2_ref[...], pre_ref[:, part * D : (part + 1) * D])
    send(FIRST["fc2_weight"])
    coming[6].wait()
    coming[7].wait()
    for part in range(FF // D):
        put("fc2_weight", part * (D // TILE), 0, activ_ref[:, part * D : (part + 1) * D], mlp_ref[...])
        send(FIRST["fc2_weight"] + (part + 1) * (D // TILE) * across)
    if not stepwise:
        sent.append(pltpu.make_async_copy(whole_ref, outs[0], sems.at[0]))
        sent[0].start()
    for copy in sent:
        copy.wait()


def weight_back(places, position, stepwise, ins):
    cores = places.sizes["c"]
    counts = [TILES // (2 * cores)] * (2 * cores) if stepwise else [TILES]
    return pl.pallas_call(
        functools.partial(weight_back_kernel, places, stepwise),
        grid_spec=pltpu.PrefetchScalarGridSpec(
            num_scalar_prefetch=1,
            grid=(1,),
            in_specs=[ANYWHERE] * len(ins),
            out_specs=[ANYWHERE] * len(counts),
            scratch_shapes=[pltpu.VMEM(array.shape, array.dtype) for array in ins]
            + [
                pltpu.VMEM((TILES, TILE, LANES), jnp.bfloat16),
                pltpu.SemaphoreType.DMA((len(ins),)),
                pltpu.SemaphoreType.DMA((2 * places.count,)),
            ],
        ),
        out_shape=[low_like(count, TILE, LANES) for count in counts],
        compiler_params=PARAMS,
        name="weight_back",
    )(position, *ins)


def input_back_kernel(project_ref, grad_middle_ref, hidden_ref, vectors_ref, tiles_ref, out_ref, sums_ref, total_ref):
    across = D // LANES
    for part in range(3):
        weight = load_weight(tiles_ref, 0, "qkv_weight", 0, D // TILE, part * across, across)
        rows = product(project_ref[part], weight, NT)
        total_ref[...] = rows if part == 0 else total_ref[...] + rows
    normal, inverse = norm_parts(hidden_ref[...])
    grad_normed = total_ref[...]
    put_vector(sums_ref, 0, grad_normed * normal)
    put_vector(sums_ref, VECTOR_ROWS, grad_normed)
    put_vector(sums_ref, 2 * VECTOR_ROWS, project_ref[0].astype(jnp.float32))
    put_vector(sums_ref, 3 * VECTOR_ROWS, project_ref[2].astype(jnp.float32))
    out_ref[...] = grad_middle_ref[...] + norm_back(
        grad_normed, normal, inverse, vector(vectors_ref, "norm1_gain")
    )


def input_back(grad_project, grad_middle, hidden, vectors, tiles):
    rows = hidden.shape[0]
    ins = [grad_project, grad_middle, hidden, vectors]
    return pl.pallas_call(
        input_back_kernel,
        grid=(1,),
        in_specs=[whole_spec(array.shape) for array in ins] + [whole_spec((MLP_FIRST, TILE, LANES))],
        out_specs=[whole_spec((rows, D)), whole_spec((LATER * VECTOR_ROWS, LANES))],
        out_shape=[full_like(rows, D), full_like(LATER * VECTOR_ROWS, LANES)],
        scratch_shapes=[pltpu.VMEM((rows, D), jnp.float32)],
        compiler_params=PARAMS,
        name="input_back",
    )(*ins, tiles)


def pad_kernel(images_ref, rows_ref):
    rows_ref[:SEQ] = images_ref[0].astype(jnp.float32)
    rows_ref[SEQ:] = jnp.zeros((ROWS - SEQ, D), jnp.float32)


def pad_rows(images):
    count = images.shape[0]
    return pl.pallas_call(
        pad_kernel,
        grid=(count,),
        in_specs=[pl.BlockSpec((1, SEQ, D), lambda i: (i, 0, 0))],
        out_specs=pl.BlockSpec((ROWS, D), lambda i: (i, 0)),
        out_shape=jax.ShapeDtypeStruct((count * ROWS, D), jnp.float32),
        name="pad_rows",
    )(images)


def cut_rows(rows):
    return rows.reshape(-1, ROWS, D)[:, :SEQ].astype(jnp.bfloat16)


class Places:
    def __init__(self, dp, fsdp):
        low = 2 if dp % 2 == 0 else 1
        core = 2 if fsdp % 2 == 0 else 1
        self.sizes = {"y": low, "x": dp // low, "z": fsdp // core, "c": core}
        self.count = dp * fsdp
        grid = np.arange(self.count).reshape(tuple(self.sizes.values()))
        self.grid = grid
        self.axis = {name: i for i, name in enumerate(self.sizes)}

    def exchange(self, block, axis, hop):
        size = self.sizes[axis]
        target = np.take(self.grid, np.arange(size) ^ hop, axis=self.axis[axis])
        perm = [(int(a), int(b)) for a, b in zip(self.grid.reshape(-1), target.reshape(-1))]
        return lax.ppermute(block, AXES, perm)

    def hops(self, axis):
        return range(1, self.sizes[axis])

    def powers(self, axis):
        return [1 << bit for bit in range(self.sizes[axis].bit_length() - 1)]

    def total(self, block, axes):
        for axis in axes:
            for hop in self.powers(axis):
                block = block + self.exchange(block, axis, hop)
        return block

    def position(self, me):
        return jnp.stack([(me // int(np.prod(self.grid.shape[i + 1 :]))) % n for i, n in enumerate(self.grid.shape)])


def block_at(at_ref, places, offset):
    number = 0
    for i, size in enumerate(places.grid.shape):
        number = number * size + (at_ref[i] ^ offset[i])
    return number


def copies_in(places, at_ref, parts, slots, whole_ref, sems):
    copies = []
    for part, listed in zip(parts, slots):
        count = part.shape[0] // len(listed)
        for i, slot in enumerate(listed):
            start = 0 if slot is None else block_at(at_ref, places, slot[0]) * (TILES // places.count) + slot[1]
            target = whole_ref.at[pl.ds(start, count)]
            copies.append(pltpu.make_async_copy(part.at[pl.ds(i * count, count)], target, sems.at[len(copies)]))
    return copies


def offset_of(**hops):
    return tuple(hops.get(axis, 0) for axis in ("y", "x", "z", "c"))


def join(blocks):
    return jnp.concatenate(blocks, axis=0) if len(blocks) > 1 else blocks[0]


ORDERS = (("x", "y"), ("y", "x"))


def group_of(shares, offsets):
    half = shares[0].shape[0] // 2
    return [(join([share[part * half : (part + 1) * half] for share in shares]), offsets) for part in range(2)]


def merge(*groups):
    return [(join([group[part][0] for group in groups]), sum((group[part][1] for group in groups), [])) for part in range(2)]


def fetch_column(places, share):
    return [places.exchange(share, "z", hop) for hop in places.hops("z")]


def column_offsets(places):
    return [offset_of(z=hop) for hop in range(places.sizes["z"])]


def fetch_plane(places, group, step):
    arrived = []
    for (block, offsets), order in zip(group, ORDERS):
        at = places.axis[order[step]]
        hops = range(1, places.sizes[order[step]])
        moved = [offset[:at] + (hop,) + offset[at + 1 :] for hop in hops for offset in offsets]
        arrived.append((join([places.exchange(block, order[step], hop) for hop in hops]), moved))
    return arrived


def fetch_plane_with(places, group, step, rows):
    (block, offsets), order = group[0], ORDERS[0]
    count, axis = block.shape[0], order[step]
    hops = range(1, places.sizes[axis])
    arrived = [places.exchange(jnp.concatenate([block, rows], axis=0), axis, hop) for hop in hops]
    moved = [tuple(hop if i == places.axis[axis] else part for i, part in enumerate(o)) for hop in hops for o in offsets]
    rows = sum([piece[count:] for piece in arrived], rows)
    other = fetch_plane(places, group, step)[1]
    return [(join([piece[:count] for piece in arrived]), moved), other], rows


def list_core(places, groups):
    parts = []
    for group in groups:
        half = TILES // places.count // 2
        parts += [(block, [(offset, part * half) for offset in offsets]) for part, (block, offsets) in enumerate(group)]
    return parts


def gather_core(places, groups):
    parts = list_core(places, groups)
    return [(join([block for block, _ in parts]), sum((slots for _, slots in parts), []))]


def fetch_core(places, parts):
    arrived = []
    for hop in range(1, places.sizes["c"]):
        for block, slots in parts:
            moved = [(offset[:3] + (hop,), first) for offset, first in slots]
            arrived.append((places.exchange(block, "c", hop), moved))
    return parts + arrived


def add_low(*blocks):
    total = blocks[0].astype(jnp.float32)
    for block in blocks[1:]:
        total = total + block.astype(jnp.float32)
    return total


def send_core(places, parts):
    cores = places.sizes["c"]
    halves = [parts[:cores], parts[cores:]]
    return [[mine] + [places.exchange(other, "c", hop) for hop, other in enumerate(others, 1)] for mine, *others in halves]


def plane_totals(places, blocks, axis):
    share = blocks[0].shape[0] // places.sizes[axis]
    cuts = [slice(i * share, (i + 1) * share) for i in range(places.sizes[axis])]
    return [add_low(*[block[cut] for block in blocks]).astype(jnp.bfloat16) for cut in cuts]


def send_totals(places, totals, axis):
    return totals[:1] + [places.exchange(total, axis, hop) for hop, total in enumerate(totals[1:], 1)]


def send_plane(places, sums, step):
    axes = [order[step] for order in ORDERS]
    return [send_totals(places, plane_totals(places, blocks, axis), axis) for blocks, axis in zip(sums, axes)]


def send_plane_tied(places, sums, step, later):
    (first, second), axes = sums, [order[step] for order in ORDERS]
    first, later = tie(first, later)
    first = plane_totals(places, first, axes[0])
    second, first, later = tie(second, first, later)
    result = [send_totals(places, first, axes[0])]
    second, later = tie(plane_totals(places, second, axes[1]), later)
    return result + [send_totals(places, second, axes[1])], later


def column_totals(places, sums):
    count = places.sizes["z"]
    share = sums[0][0].shape[0] // count
    cuts = [slice(hop * share, (hop + 1) * share) for hop in range(count)]
    return [join([add_low(*[block[cut] for block in blocks]).astype(jnp.bfloat16) for blocks in sums]) for cut in cuts]


def send_column(places, totals):
    return [totals[0]] + [places.exchange(total, "z", hop) for hop, total in enumerate(totals[1:], 1)]


class Layer:
    def __init__(self, places, position, counts, vectors):
        self.places, self.position, self.counts, self.vectors = places, position, counts, vectors

    def project(self, hidden, parts):
        normed, qkv, tiles = project(self.places, self.position, parts, hidden, self.vectors)
        self.saved = dict(hidden=hidden, normed=normed, qkv=qkv, tiles=tiles)

    def attend(self):
        saved = self.saved
        saved["attended"], saved["weights"] = attention(self.counts, saved["qkv"], self.bias)

    def finish(self):
        saved = self.saved
        names = ("branch", "middle", "normed2", "activ", "slope", "mlp_out")
        result, *kept = mlp(saved["attended"], saved["hidden"], self.vectors, saved["tiles"])
        saved.update(zip(names, kept))
        return result

    def back_mlp(self, grad):
        return mlp_back(grad, self.saved, self.vectors, self.saved["tiles"])

    def back_attention(self, passed):
        return attention_back(self.saved["qkv"], passed[1], self.saved["weights"])

    def back_weights(self, passed, grad_project, stepwise):
        _, _, grad_mlp, grad_pre, grad_branch, _ = passed
        saved = self.saved
        ins = [saved["normed"], grad_project, saved["attended"], grad_branch, saved["normed2"], grad_pre]
        return weight_back(self.places, self.position, stepwise, ins + [saved["activ"], grad_mlp])

    def back_input(self, passed, grad_project):
        return input_back(grad_project, passed[0], self.saved["hidden"], self.vectors, self.saved["tiles"])


def scatter_whole(parts):
    whole = parts[0].reshape(-1, LANES)
    return lax.psum_scatter(whole, AXES, scatter_dimension=0, tiled=True).astype(jnp.float32)


def local(dp, fsdp, tokens, counts, params_first, params_second, cotangent):
    devices = dp * fsdp
    places = Places(dp, fsdp)
    stepwise = TILES % (4 * devices) == 0 and all(size & (size - 1) == 0 for size in places.sizes.values())
    share_rows = TILES * TILE // devices
    me = lax.axis_index(AXES)
    position = places.position(me)
    owned = Owned([params_first, params_second], me, devices)
    own = owned.share(0)
    small_rows = owned.small_rows(own)
    tokens, cotangent, small_rows = tie(tokens, cotangent, small_rows)
    hidden, grad_output = pad_rows(tokens), pad_rows(cotangent)

    if stepwise:
        own = own.reshape(-1, TILE, LANES)
        column = fetch_column(places, own)
        near, small_rows = tie(group_of([own], [offset_of()]), small_rows)
        small_rows = small_rows.reshape(-1, TILE, LANES)
        near_first, small_rows = fetch_plane_with(places, near, 0, small_rows)
        near_first, small_rows = tie(near_first, small_rows)
        near_second, small_rows = fetch_plane_with(places, merge(near, near_first), 1, small_rows)
        small_rows = places.total(small_rows, "c")
        next_own, near_first = tie(owned.share(1, own), near_first)
        far, near_second = tie(group_of(column, column_offsets(places)[1:]), near_second)
        far_first = fetch_plane(places, far, 0)
        next_own, small_rows, far, hidden, grad_output = tie(next_own, small_rows, far, hidden, grad_output)
        next_own = jnp.concatenate([next_own, small_rows.reshape(-1, LANES)], axis=0)
        next_shares = [next_own] + fetch_column(places, next_own)
        small_rows = sum([rows[share_rows:] for rows in next_shares[1:]], next_own[share_rows:])
        small_rows = small_rows.reshape(2, -1, LANES)
        vectors = small_rows.astype(jnp.float32)
        next_shares = [rows[:share_rows].reshape(-1, TILE, LANES) for rows in next_shares]
        group = group_of(next_shares, column_offsets(places))
        far_second = fetch_plane(places, merge(far, far_first), 1)
        early = gather_core(places, [near, near_first, near_second, far, far_first])
    else:
        small_rows = lax.psum(small_rows, AXES)
    if stepwise:
        far_second, early, group, small_rows, vectors = tie(far_second, early, group, small_rows, vectors)
        first = fetch_plane(places, group, 0)
        parts = fetch_core(places, early) + fetch_core(places, list_core(places, [far_second]))
        first_layer = Layer(places, position, counts, vectors[0])
        parts, group = tie(parts, group)
        second_early = fetch_plane(places, group, 1)
        first_layer.project(hidden, parts)
        entries, first_layer.saved = tie(table_entries(small_rows), first_layer.saved)
        first_layer.bias, second_bias = bias_of(entries[0]), bias_of(entries[1])
        first, second_early, first_layer.bias, second_bias = tie(first, second_early, first_layer.bias, second_bias)
        second = fetch_plane(places, first, 1)
        next_parts = fetch_core(places, list_core(places, [first, second_early]))
        first_layer.attend()
        result = first_layer.finish()
        next_parts, result = tie(next_parts, result)
        next_parts += fetch_core(places, gather_core(places, [group]))
        second, next_parts, result = tie(second, next_parts, result)
        next_parts += fetch_core(places, list_core(places, [second]))
    else:
        vectors = small_rows.astype(jnp.float32)
        entries = table_entries(small_rows)
        second_bias = bias_of(entries[1])
        parts, next_parts = [
            [(lax.all_gather(share, AXES, axis=0, tiled=True).reshape(TILES, TILE, LANES), [None])]
            for share in (own, owned.share(1))
        ]
        first_layer = Layer(places, position, counts, vectors[0])
        first_layer.project(hidden, parts)
        first_layer.bias = bias_of(entries[0])
        first_layer.attend()
        result = first_layer.finish()
    second_layer = Layer(places, position, counts, vectors[1])
    second_layer.bias = second_bias
    second_layer.project(result, next_parts)
    second_layer.attend()
    result = second_layer.finish()
    output = cut_rows(result)

    next_passed = second_layer.back_mlp(grad_output)
    next_project, next_bias = second_layer.back_attention(next_passed)
    parts = second_layer.back_weights(next_passed, next_project, stepwise)
    if stepwise:
        sums = send_core(places, parts)
    else:
        next_share = scatter_whole(parts)
    grad, next_sums = second_layer.back_input(next_passed, next_project)
    if stepwise:
        sums, grad = send_plane_tied(places, sums, 0, grad)
    passed = first_layer.back_mlp(grad)
    project_grad, bias = first_layer.back_attention(passed)
    parts = first_layer.back_weights(passed, project_grad, stepwise)
    if stepwise:
        sums, parts, passed, project_grad = tie(sums, parts, passed, project_grad)
        sums = send_plane(places, sums, 1)
        own_sums = send_core(places, parts)
    else:
        share = scatter_whole(parts)
    if stepwise:
        own_sums, later = send_plane_tied(places, own_sums, 0, (bias, passed, project_grad))
        sums, (bias, passed, project_grad) = tie(sums, later)
        sums = send_column(places, column_totals(places, sums))
    grad, own_row_sums = first_layer.back_input(passed, project_grad)
    small_grads = small_gradients(
        [own_row_sums, next_sums], [passed[5], next_passed[5]], tables_from_biases(bias, next_bias)
    )
    flat_share = FlatShare(me, devices, params_first.shape[0] * devices)
    if stepwise:
        own_sums, sums, small_grads = tie(own_sums, sums, small_grads)
        own_sums = send_plane(places, own_sums, 1)
        small_grads = places.total(small_grads, "zc")
        own_sums, small_grads = tie(own_sums, small_grads)
        own_sums = send_column(places, column_totals(places, own_sums))
        small_grads = places.total(small_grads, "xy")
        small_grads, sums = tie(small_grads, sums)
        grad_second = flat_share(add_low(*sums).reshape(-1, LANES), small_grads[1])
        own_sums, grad_second, output, grad_tokens = tie(own_sums, grad_second, output, cut_rows(grad))
        share = add_low(*own_sums).reshape(-1, LANES)
    else:
        small_grads = lax.psum(small_grads, AXES)
        grad_second = flat_share(next_share, small_grads[1])
        grad_tokens = cut_rows(grad)
    grad_first = flat_share(share, small_grads[0])
    return output, grad_tokens, grad_first, grad_second


def solution(mesh):
    return jax.shard_map(
        functools.partial(local, mesh.shape["dp"], mesh.shape["fsdp"]),
        mesh=mesh,
        in_specs=(P(AXES, None, None), P(AXES), P(AXES), P(AXES), P(AXES, None, None)),
        out_specs=(P(AXES, None, None), P(AXES, None, None), P(AXES), P(AXES)),
        check_vma=False,
    )
```
